256 devices in a mesh: dp: 64 (over z, y_lo, x), ctx: 4 (over y_hi, core).
Axes of the slice: x: 4, y: 4 (y_hi: 2, y_lo: 2; y = y_hi * 2 + y_lo), z: 8, core: 2. Of those that a mesh axis runs over, the one named last changes fastest.
Arguments:
- event_ids: int32 [192, 1024], P('dp', 'ctx'), may hold values from 0 to 2047
- lengths: int32 [192], P('dp'), may hold values from 128 to 1024, as said below
- event_side: bfloat16 [192, 1024, 512], P('dp', 'ctx'), may hold values from -4 to 4
- dense_input: bfloat16 [192, 1024], P('dp'), may hold values from -6 to 6
- labels: int32 [192, 2], P('dp'), may hold values 0 or 1
- event_table: bfloat16 [2048, 512], replicated, may hold values from -6 to 6
- seq_gain: float32 [512], replicated, may hold values from 0.1 to 1.9
- w_mix: bfloat16 [1024, 512], replicated, may hold values from -0.1875 to 0.1875
- w_query: bfloat16 [512, 512], replicated
- w_key: bfloat16 [512, 512], replicated
- w_value: bfloat16 [512, 512], replicated, may hold values from -0.25 to 0.25
- w_out: bfloat16 [512, 512], replicated, may hold values from -0.25 to 0.25
- w_pool: bfloat16 [512, 1024], replicated, may hold values from -0.25 to 0.25
- w_cross: bfloat16 [1024, 1024], replicated, may hold values from -0.1875 to 0.1875
- b_cross: float32 [1024], replicated, may hold values from -3 to 3
- w_heads: float32 [1024, 2], replicated, may hold values from -0.1875 to 0.1875
Outputs:
- grad_sequence: float32 [3072, 512], P(('dp', 'ctx'))
- grad_mix: float32 [1024, 512], P(('dp', 'ctx'))
- grad_cross: float32 [1024, 1024], P(('dp', 'ctx'))
- grad_gain: float32 [512], replicated
- grad_bias: float32 [1024], replicated
- grad_heads: float32 [1024, 2], replicated
The draws below stay inside these ranges and needn't reach their ends.
Inputs may be any that keep to these rules, and one draw needn't show every extreme that they name: Sample b's history holds lengths[b] events in its first slots; the rest of its 1024 slots are padding.
All inputs are finite; a program needn't handle non-finite values. No bound on the sum of `labels` on one device may be relied on, other than what follows from the above.
Results may differ from the reference program's by a relative error of at most 0.015.
The reference program's roundings to bfloat16 on the way (of `mixed_in`, `shares_half`, `attended`, `residual_half`, `grad_pre`, `grad_residual`, `grad_attended` and `grad_scores`) count: a program that leaves them out, or rounds other values in their place, can miss the bound.
Values may be sent and summed in bfloat16 or wider, within the bound.
No kernel may reach another device: no remote copies, remote signals or barrier semaphores. Data moves between devices by JAX's collectives and lax.ppermute only.
A program may use at most 192 MiB of HBM per device.

```python
import math
import jax
import jax.numpy as jnp
import numpy as np
from jax import lax

D = 512
HEADS = 8
DI = 1024
HD = 64
V = 2048
LEN = 1024
BATCH = 192


def query_matrix(key):
    return jax.random.truncated_normal(key, -3.0, 3.0, (D, D), jnp.float32) / math.sqrt(D)


def draw_w_query(key, part):
    shared = query_matrix(key)
    return shared.astype(jnp.bfloat16)


def draw_w_key(key, part):
    key = jax.random.fold_in(key, 5)
    jitter = jax.random.truncated_normal(jax.random.fold_in(key, 1), -3.0, 3.0, (D, D), jnp.float32) / math.sqrt(D)
    return jitter.astype(jnp.bfloat16)


def draw_lengths(key, part):
    key = jax.random.fold_in(key, 7)
    drawn = jax.random.randint(key, (BATCH,), LEN // 8, LEN + 1, dtype=jnp.int32)
    drawn = drawn.at[0].set(LEN)
    return drawn.at[1].set(LEN // 8)


def touch_ends(values, stream_key, smallest, largest):
    dims = values.shape
    place = [jax.random.randint(jax.random.fold_in(stream_key, axis), (), 0, dims[axis]) for axis in range(len(dims))]
    values = values.at[tuple(place)].set(smallest)
    longest = dims.index(max(dims))
    place[longest] = (place[longest] + 1) % dims[longest]
    return values.at[tuple(place)].set(largest)


def steps_of(key, shape, cuts, low, high):
    gain, own = 1.0, jax.random.fold_in(key, 6)
    for position, parts in cuts:
        draws = jnp.exp(jax.random.uniform(jax.random.fold_in(own, position), (parts,), jnp.float32, low / len(cuts), high / len(cuts)))
        gain = gain * jnp.repeat(draws, shape[position] // parts).reshape([-1 if axis == position else 1 for axis in range(len(shape))])
    return gain


def rank_table(amount, lean):
    weights = [(1 << 20) // math.isqrt(rank ** lean) + 1 for rank in range(1, amount + 1)]
    width = 1 + sum(weights) // (1 << 30)
    return np.cumsum(np.array([max(1, weight // width) for weight in weights]))


def skewed_ids(own_key, extent, number_of, lean):
    listing = rank_table(number_of, lean)
    lot = jax.random.randint(jax.random.fold_in(own_key, 1), extent, 0, int(listing[number_of - 1]))
    rank = jnp.searchsorted(jnp.asarray(listing, jnp.int32), lot, side="right")
    return jax.random.permutation(jax.random.fold_in(own_key, 2), number_of)[rank].astype(jnp.int32)


def bell_draw(key, extent, scale, limit, cuts=(), held_as=jnp.bfloat16):
    array = scale * jax.random.normal(key, extent, jnp.float32)
    if cuts:
        array = array * steps_of(key, extent, cuts, -0.22, 0.18)
    return jnp.clip(array, -limit, limit).astype(held_as)


def setup_inputs(seed: int = 0) -> dict:
    key_of = jax.random.split(jax.random.key(seed), 17)
    event_ids = touch_ends(skewed_ids(key_of[0], (BATCH, LEN), V, 2), jax.random.fold_in(key_of[0], 3), 0, V - 1).astype(jnp.int32)
    lengths = draw_lengths(jax.random.fold_in(key_of[16], 71), 0)
    event_side = bell_draw(key_of[2], (BATCH, LEN, D), 0.5, 4.0, ((0, 64), (1, 4)))
    dense_input = bell_draw(key_of[3], (BATCH, DI), 1.0, 6.0, ((0, 64),))
    labels = touch_ends((jax.random.randint(key_of[4], (BATCH, 2), 0, 2) < 1).astype(jnp.int32), jax.random.fold_in(key_of[4], 1), 0, 1)
    event_table = bell_draw(key_of[5], (V, D), 1.0, 6.0)
    seq_gain = jnp.clip(1.0 + 0.18 * jax.random.normal(key_of[6], (D,), jnp.float32), 0.1, 1.9)
    w_mix = bell_draw(key_of[7], (DI, D), DI ** -0.5, 0.1875)
    w_query = draw_w_query(jax.random.fold_in(key_of[16], 71), 0)
    w_key = draw_w_key(jax.random.fold_in(key_of[16], 71), 0)
    w_value = bell_draw(key_of[10], (D, D), D ** -0.5, 0.25)
    w_out = bell_draw(key_of[11], (D, D), D ** -0.5, 0.25)
    w_pool = bell_draw(key_of[12], (D, DI), D ** -0.5, 0.25)
    w_cross = bell_draw(key_of[13], (DI, DI), DI ** -0.5, 0.1875)
    b_cross = bell_draw(key_of[14], (DI,), 0.5, 3.0, (), jnp.float32)
    w_heads = bell_draw(key_of[15], (DI, 2), DI ** -0.5, 0.1875, (), jnp.float32)
    return dict(event_ids=event_ids, lengths=lengths, event_side=event_side, dense_input=dense_input, labels=labels, event_table=event_table, seq_gain=seq_gain, w_mix=w_mix, w_query=w_query, w_key=w_key, w_value=w_value, w_out=w_out, w_pool=w_pool, w_cross=w_cross, b_cross=b_cross, w_heads=w_heads)


MASKED = -1e+30
EPSILON = 1e-06
LOSS_SCALE = 32768.0
HIGHEST = lax.Precision.HIGHEST

def widen(half):
    return lax.optimization_barrier(half).astype(jnp.float32)

def silu_slope(pre_act):
    sigmoid = jax.nn.sigmoid(pre_act)
    return sigmoid * (1.0 + pre_act * (1.0 - sigmoid))

def objective(logits, labels):
    clicked = labels[:, 0].astype(jnp.float32)
    converted = (labels[:, 0] * labels[:, 1]).astype(jnp.float32)
    ctr_logit = logits[:, 0]
    cvr_logit = logits[:, 1]
    ctr_loss = jax.nn.softplus(ctr_logit) - clicked * ctr_logit
    log_hit = -jax.nn.softplus(-ctr_logit) - jax.nn.softplus(-cvr_logit)
    stacked = jnp.stack([jnp.zeros_like(ctr_logit), ctr_logit, cvr_logit], axis=1)
    log_miss = jax.nn.logsumexp(stacked, axis=1) - jax.nn.softplus(ctr_logit) - jax.nn.softplus(cvr_logit)
    return jnp.sum(ctr_loss - converted * log_hit - (1.0 - converted) * log_miss)

def split_heads(rows):
    return widen(rows).reshape(rows.shape[0], HEADS, -1)

def attention_shares(queries, key_rows, length):
    positions = jnp.arange(LEN, dtype=jnp.int32)
    scores = jnp.einsum('qhd,khd->hqk', split_heads(queries), split_heads(key_rows)) * HD ** (-0.5)
    allowed = (positions[None, :] <= positions[:, None]) & (positions[None, :] < length)
    scores = jnp.where(allowed[None], scores, MASKED)
    raised = jnp.exp(scores - lax.optimization_barrier(jnp.max(scores, axis=-1, keepdims=True)))
    return raised / lax.optimization_barrier(jnp.sum(raised, axis=-1, keepdims=True))

def sequence_forward(event_row, side_row, length, mix_row, event_table, seq_gain, w_query, w_key, w_value, w_out, w_pool):
    tokens = jnp.take(event_table, event_row, axis=0).astype(jnp.float32) + side_row.astype(jnp.float32)
    normed = tokens * lax.rsqrt(lax.optimization_barrier(jnp.mean(tokens * tokens, axis=-1, keepdims=True)) + EPSILON)
    mixed_in = (normed * seq_gain + mix_row).astype(jnp.bfloat16)
    queries = jnp.dot(mixed_in, w_query, preferred_element_type=jnp.float32).astype(jnp.bfloat16)
    key_rows = jnp.dot(mixed_in, w_key, preferred_element_type=jnp.float32).astype(jnp.bfloat16)
    value_rows = jnp.dot(mixed_in, w_value, preferred_element_type=jnp.float32).astype(jnp.bfloat16)
    shares = attention_shares(queries, key_rows, length)
    shares_half = widen(shares.astype(jnp.bfloat16))
    attended = jnp.einsum('hqk,khd->qhd', shares_half, split_heads(value_rows)).reshape(LEN, D).astype(jnp.bfloat16)
    residual = tokens + jnp.dot(attended, w_out, preferred_element_type=jnp.float32)
    residual_half = residual.astype(jnp.bfloat16)
    pre_act = jnp.dot(residual_half, w_pool, preferred_element_type=jnp.float32)
    is_valid = jnp.arange(LEN, dtype=jnp.int32) < length
    summary = lax.optimization_barrier(jnp.sum(jnp.where(is_valid[:, None], jax.nn.silu(pre_act), 0.0), axis=0)) / length.astype(jnp.float32)
    return (normed, mixed_in, queries, key_rows, value_rows, shares, shares_half, attended, residual_half, pre_act, is_valid, summary)

def sequence_backward(event_row, side_row, length, mix_row, gate_row, event_table, seq_gain, w_query, w_key, w_value, w_out, w_pool):
    forward = sequence_forward(event_row, side_row, length, mix_row, event_table, seq_gain, w_query, w_key, w_value, w_out, w_pool)
    normed, mixed_in, queries, key_rows, value_rows, shares, shares_half, attended, residual_half, pre_act, is_valid, summary = forward
    scaled_row = gate_row / length.astype(jnp.float32)
    grad_pre = jnp.where(is_valid[:, None], silu_slope(pre_act) * scaled_row[None, :], 0.0).astype(jnp.bfloat16)
    pool_term = jnp.dot(grad_pre.T, residual_half, preferred_element_type=jnp.float32)
    grad_residual = jnp.dot(grad_pre, w_pool.T, preferred_element_type=jnp.float32).astype(jnp.bfloat16)
    out_term = jnp.dot(attended.T, grad_residual, preferred_element_type=jnp.float32)
    grad_attended = jnp.dot(grad_residual, w_out.T, preferred_element_type=jnp.float32).astype(jnp.bfloat16)
    grad_shares = jnp.einsum('qhd,khd->hqk', split_heads(grad_attended), split_heads(value_rows))
    row_delta = lax.optimization_barrier(jnp.sum(grad_shares * shares, axis=-1, keepdims=True))
    grad_scores = widen((shares * (grad_shares - row_delta) * HD ** (-0.5)).astype(jnp.bfloat16))
    grad_queries = jnp.einsum('hqk,khd->qhd', grad_scores, split_heads(key_rows)).reshape(LEN, D).astype(jnp.bfloat16)
    grad_keys = jnp.einsum('hqk,qhd->khd', grad_scores, split_heads(queries)).reshape(LEN, D).astype(jnp.bfloat16)
    grad_values = jnp.einsum('hqk,qhd->khd', shares_half, split_heads(grad_attended)).reshape(LEN, D).astype(jnp.bfloat16)
    query_term = jnp.dot(mixed_in.T, grad_queries, preferred_element_type=jnp.float32)
    key_term = jnp.dot(mixed_in.T, grad_keys, preferred_element_type=jnp.float32)
    value_term = jnp.dot(mixed_in.T, grad_values, preferred_element_type=jnp.float32)
    grad_mixed = jnp.dot(grad_queries, w_query.T, preferred_element_type=jnp.float32)
    grad_mixed = grad_mixed + jnp.dot(grad_keys, w_key.T, preferred_element_type=jnp.float32)
    grad_mixed = grad_mixed + jnp.dot(grad_values, w_value.T, preferred_element_type=jnp.float32)
    gain_term = lax.optimization_barrier(jnp.sum(grad_mixed * normed, axis=0))
    mix_term = lax.optimization_barrier(jnp.sum(grad_mixed, axis=0))
    flat_term = jnp.concatenate([query_term, key_term, value_term, out_term, pool_term], axis=0)
    return (flat_term, gain_term, mix_term)

def reference(event_ids, lengths, event_side, dense_input, labels, event_table, seq_gain, w_mix, w_query, w_key, w_value, w_out, w_pool, w_cross, b_cross, w_heads):
    mix_rows = jnp.dot(dense_input, w_mix, preferred_element_type=jnp.float32)

    def sample_summary(sample):
        event_row, side_row, length, mix_row = sample
        forward = sequence_forward(event_row, side_row, length, mix_row, event_table, seq_gain, w_query, w_key, w_value, w_out, w_pool)
        return forward[-1]
    summary = lax.map(sample_summary, (event_ids, event_side, lengths, mix_rows))
    inputs = dense_input.astype(jnp.float32)
    cross_gate = jnp.dot(dense_input, w_cross, preferred_element_type=jnp.float32) + b_cross + summary
    crossed = inputs + inputs * cross_gate
    logits = jnp.dot(crossed, w_heads, precision=HIGHEST)
    factor = LOSS_SCALE / BATCH
    grad_logits = jax.grad(objective)(logits, labels) * factor
    grad_crossed = jnp.dot(grad_logits, w_heads.T, precision=HIGHEST)
    grad_gate = grad_crossed * inputs
    grad_heads = jnp.dot(crossed.T, grad_logits, precision=HIGHEST)
    grad_bias = lax.optimization_barrier(jnp.sum(grad_gate, axis=0))
    grad_cross = jnp.dot(inputs.T, grad_gate, precision=HIGHEST)

    def accumulate(running, sample):
        event_row, side_row, length, mix_row, gate_row = sample
        flat_term, gain_term, mix_term = sequence_backward(event_row, side_row, length, mix_row, gate_row, event_table, seq_gain, w_query, w_key, w_value, w_out, w_pool)
        return ((running[0] + flat_term, running[1] + gain_term), mix_term)
    starting = (jnp.zeros((4 * D + DI, D), jnp.float32), jnp.zeros((D,), jnp.float32))
    totals, mix_sums = lax.scan(accumulate, starting, (event_ids, event_side, lengths, mix_rows, grad_gate))
    grad_sequence, grad_gain = totals
    grad_mix = jnp.dot(inputs.T, mix_sums, precision=HIGHEST)
    return (grad_sequence, grad_mix, grad_cross, grad_gain, grad_bias, grad_heads)
```

```python
import functools

import jax
import jax.numpy as jnp
from jax import lax
from jax.experimental import pallas as pl
from jax.experimental.pallas import tpu as pltpu
from jax.sharding import Mesh, PartitionSpec as P

HEADS = 8
BATCH = 192
SAMPLES = 3
BLOCK = 256
BLOCKS = 4
LEN = 1024
D = 512
DI = 1024
MASKED = -1e30
EPSILON = 1e-06
LOSS_SCALE = 32768.0
F32 = jnp.float32
BF16 = jnp.bfloat16
CTX = ("yhi", "core")
PLANE = ("ylo", "x", "yhi")


def dot(a, b):
    return lax.dot_general(a, b, (((1,), (0,)), ((), ())), preferred_element_type=F32)


def dot_nt(a, b):
    return lax.dot_general(a, b, (((1,), (1,)), ((), ())), preferred_element_type=F32)


def dot_tn(a, b):
    return lax.dot_general(a, b, (((0,), (0,)), ((), ())), preferred_element_type=F32)


def both_heads(rows):
    low = lax.broadcasted_iota(jnp.int32, rows.shape, 1) < 64
    zero = jnp.zeros_like(rows)
    return jnp.concatenate([jnp.where(low, rows, zero), jnp.where(low, zero, rows)], axis=0)


def causal(tile):
    key = lax.broadcasted_iota(jnp.int32, tile.shape, 0)
    query = lax.broadcasted_iota(jnp.int32, tile.shape, 1) & (BLOCK - 1)
    return key <= query


def forward_kernel(
    meta, rows_ref, side_ref, mix_ref, gain_ref, wq_ref, wk_ref, wv_ref, wo_ref, wp_ref,
    wot_ref, wpt_ref, base_ref, dense_ref, heads_ref,
    q_ref, k_ref, v_ref, do_ref, mixed_ref, normed_ref, lse_ref, delta_ref, pool_ref, out_ref,
    crossed_ref, logit_ref,
    vt_ref, att_ref, o_ref, res_ref, pre_ref, sum_ref, scaled_ref, pool_acc, out_acc,
):
    step = pl.program_id(0)
    length = meta[1]

    @pl.when(step == 0)
    def _():
        sum_ref[...] = jnp.zeros_like(sum_ref)
        pool_acc[...] = jnp.zeros_like(pool_acc)
        out_acc[...] = jnp.zeros_like(out_acc)

    def ahead(c):
        here = slice(c * BLOCK, (c + 1) * BLOCK)
        tokens = rows_ref[0].astype(F32) + side_ref[0].astype(F32)
        mean = jnp.mean(tokens * tokens, axis=1, keepdims=True)
        normed = tokens * lax.rsqrt(mean + EPSILON)
        normed_ref[here, :] = normed
        mixed = (normed * gain_ref[...] + mix_ref[...]).astype(BF16)
        mixed_ref[here, :] = mixed
        queries = (dot(mixed, wq_ref[...]).astype(BF16).astype(F32) * 0.125).astype(BF16)
        q_ref[here, :] = queries
        k_ref[here, :] = dot(mixed, wk_ref[...]).astype(BF16)
        values = dot(mixed, wv_ref[...]).astype(BF16)
        v_ref[here, :] = values
        vt_ref[:, here] = values.T
        for p in range(4):
            lanes = slice(p * 128, (p + 1) * 128)
            chosen = both_heads(q_ref[here, lanes])
            tiles = []
            for j in range(c + 1):
                tile = dot_nt(k_ref[j * BLOCK : (j + 1) * BLOCK, lanes], chosen)
                if j == c:
                    tile = jnp.where(causal(tile), tile, MASKED)
                tiles.append(tile)
            top = functools.reduce(jnp.maximum, [jnp.max(t, axis=0, keepdims=True) for t in tiles])
            raised = [jnp.exp(t - top) for t in tiles]
            total = functools.reduce(jnp.add, [jnp.sum(t, axis=0, keepdims=True) for t in raised])
            inverse = 1.0 / total
            shares = [(t * inverse).astype(BF16) for t in raised]
            lse = top + jnp.log(total)
            lse_ref[2 * p : 2 * p + 1, here] = lse[:, :BLOCK]
            lse_ref[2 * p + 1 : 2 * p + 2, here] = lse[:, BLOCK:]
            first = jnp.zeros((64, BLOCK), F32)
            second = jnp.zeros((64, BLOCK), F32)
            for j in range(c + 1):
                keys = slice(j * BLOCK, (j + 1) * BLOCK)
                first += dot(vt_ref[p * 128 : p * 128 + 64, keys], shares[j][:, :BLOCK])
                second += dot(vt_ref[p * 128 + 64 : p * 128 + 128, keys], shares[j][:, BLOCK:])
            joined = jnp.concatenate([first, second], axis=0).T
            o_ref[here, lanes] = joined
            att_ref[here, lanes] = joined.astype(BF16)
        residual = tokens + dot(att_ref[here, :], wo_ref[...])
        half = residual.astype(BF16)
        res_ref[here, :] = half
        pre = dot(half, wp_ref[...])
        pre_ref[here, :] = pre
        valid = (c * BLOCK + lax.broadcasted_iota(jnp.int32, pre.shape, 0)) < length
        silu = jnp.where(valid, pre * jax.nn.sigmoid(pre), 0.0)
        sum_ref[...] += jnp.sum(silu, axis=0, keepdims=True)

    def blank(c):
        here = slice(c * BLOCK, (c + 1) * BLOCK)
        for ref in (q_ref, k_ref, v_ref, mixed_ref, normed_ref, do_ref):
            ref[here, :] = jnp.zeros((BLOCK, D), ref.dtype)
        lse_ref[:, here] = jnp.zeros((HEADS, BLOCK), F32)
        delta_ref[:, here] = jnp.zeros((HEADS, BLOCK), F32)

    for c in range(BLOCKS):
        pl.when((step == c) & (length > c * BLOCK))(functools.partial(ahead, c))
        pl.when((step == c) & (length <= c * BLOCK))(functools.partial(blank, c))

    @pl.when(step == BLOCKS)
    def _():
        span = jnp.maximum(length, 1).astype(F32)
        dense = dense_ref[...]
        gate = base_ref[...] + sum_ref[...] / span
        crossed = dense + dense * gate
        crossed_ref[...] = crossed
        a = jnp.sum(crossed * heads_ref[0:1, :], axis=1, keepdims=True)
        c = jnp.sum(crossed * heads_ref[1:2, :], axis=1, keepdims=True)
        clicked = meta[2].astype(F32)
        converted = (meta[2] * meta[3]).astype(F32)
        top = jnp.maximum(jnp.maximum(a, c), 0.0)
        ea, ec = jnp.exp(a - top), jnp.exp(c - top)
        below = jnp.exp(-top) + ea + ec
        grad_a = jax.nn.sigmoid(a) - clicked - converted * jax.nn.sigmoid(-a)
        grad_a = grad_a - (1.0 - converted) * (ea / below - jax.nn.sigmoid(a))
        grad_c = -converted * jax.nn.sigmoid(-c)
        grad_c = grad_c - (1.0 - converted) * (ec / below - jax.nn.sigmoid(c))
        factor = jnp.where(length > 0, LOSS_SCALE / BATCH, 0.0)
        grad_a = grad_a * factor
        grad_c = grad_c * factor
        lane = lax.broadcasted_iota(jnp.int32, (1, 128), 1)
        logit_ref[...] = jnp.where(lane == 0, grad_a, jnp.where(lane == 1, grad_c, 0.0))
        grad_gate = (grad_a * heads_ref[0:1, :] + grad_c * heads_ref[1:2, :]) * dense
        scaled_ref[...] = grad_gate / span

    def back(c):
        here = slice(c * BLOCK, (c + 1) * BLOCK)
        pre = pre_ref[here, :]
        sig = jax.nn.sigmoid(pre)
        valid = (c * BLOCK + lax.broadcasted_iota(jnp.int32, pre.shape, 0)) < length
        slope = sig * (1.0 + pre * (1.0 - sig)) * scaled_ref[...]
        grad_pre = jnp.where(valid, slope, 0.0).astype(BF16)
        pool_acc[...] += dot_tn(grad_pre, res_ref[here, :])
        grad_res = dot(grad_pre, wpt_ref[...]).astype(BF16)
        out_acc[...] += dot_tn(att_ref[here, :], grad_res)
        grad_att = dot(grad_res, wot_ref[...]).astype(BF16)
        do_ref[here, :] = grad_att
        product = grad_att.astype(F32) * o_ref[here, :]
        head = lax.broadcasted_iota(jnp.int32, (HEADS, D), 0)
        column = lax.broadcasted_iota(jnp.int32, (HEADS, D), 1) // 64
        picks = jnp.where(head == column, 1.0, 0.0)
        delta_ref[:, here] = lax.dot_general(
            picks, product, (((1,), (1,)), ((), ())),
            precision=lax.Precision.HIGHEST, preferred_element_type=F32,
        )

    for c in range(BLOCKS):
        pl.when((step == BLOCKS + c) & (length > c * BLOCK))(functools.partial(back, c))

    @pl.when(step == 2 * BLOCKS - 1)
    def _():
        pool_ref[...] = pool_acc[...].astype(BF16)
        out_ref[...] = out_acc[...].astype(BF16)


def backward_kernel(
    meta, q_ref, k_ref, v_ref, do_ref, lse_ref, delta_ref, mixed_ref, normed_ref,
    wqt_ref, wkt_ref, wvt_ref,
    term_ref, small_ref,
    dq_ref, dk_ref, dv_ref, dk_acc, dv_acc, kt_ref,
):
    step = pl.program_id(0)
    length = meta[1]

    @pl.when(step < 4)
    def _():
        dk_acc[...] = jnp.zeros_like(dk_acc)
        dv_acc[...] = jnp.zeros_like(dv_acc)
        kt_ref[...] = k_ref[...].T

        def block(c):
            here = slice(c * BLOCK, (c + 1) * BLOCK)
            chosen = both_heads(q_ref[here, :])
            grads = both_heads(do_ref[here, :])
            lse = jnp.concatenate([lse_ref[0, 0:1, here], lse_ref[0, 1:2, here]], axis=1)
            delta = jnp.concatenate([delta_ref[0, 0:1, here], delta_ref[0, 1:2, here]], axis=1)
            first = jnp.zeros((64, BLOCK), F32)
            second = jnp.zeros((64, BLOCK), F32)
            for j in range(c + 1):
                keys = slice(j * BLOCK, (j + 1) * BLOCK)
                shares = jnp.exp(dot_nt(k_ref[keys, :], chosen) - lse)
                if j == c:
                    shares = jnp.where(causal(shares), shares, 0.0)
                grad_shares = dot_nt(v_ref[keys, :], grads)
                grad_scores = (shares * (grad_shares - delta)).astype(BF16)
                dv_acc[keys, :] += dot(shares.astype(BF16), grads)
                dk_acc[keys, :] += dot(grad_scores, chosen)
                first += dot(kt_ref[0:64, keys], grad_scores[:, :BLOCK])
                second += dot(kt_ref[64:128, keys], grad_scores[:, BLOCK:])
            joined = jnp.concatenate([first, second], axis=0) * 0.125
            dq_ref[step, here, :] = joined.T.astype(BF16)

        def blank(c):
            here = slice(c * BLOCK, (c + 1) * BLOCK)
            dq_ref[step, here, :] = jnp.zeros((BLOCK, 128), BF16)

        for c in range(BLOCKS):
            pl.when(length > c * BLOCK)(functools.partial(block, c))
            pl.when(length <= c * BLOCK)(functools.partial(blank, c))
        dk_ref[step] = dk_acc[...].astype(BF16)
        dv_ref[step] = dv_acc[...].astype(BF16)

    @pl.when(step == 4)
    def _():
        mixed_t = mixed_ref[...].T
        grad_mixed = None
        for n, (ref, weight) in enumerate(((dq_ref, wqt_ref), (dk_ref, wkt_ref), (dv_ref, wvt_ref))):
            rows = jnp.concatenate([ref[p] for p in range(4)], axis=1)
            term_ref[n * D : (n + 1) * D, :] = dot(mixed_t, rows).astype(BF16)
            part = dot(rows, weight[...])
            grad_mixed = part if grad_mixed is None else grad_mixed + part
        small_ref[0:1, :] = jnp.sum(grad_mixed, axis=0, keepdims=True)
        small_ref[1:2, :] = jnp.sum(grad_mixed * normed_ref[...], axis=0, keepdims=True)


def whole(shape):
    return pl.BlockSpec(shape, lambda i, m: (0,) * len(shape))


def forward(meta, rows, side, *rest):
    block = pl.BlockSpec(
        (1, BLOCK, D),
        lambda i, m: (lax.rem(m[0] - jnp.minimum(i, BLOCKS - 1) + BLOCKS, BLOCKS), 0, 0),
    )
    outs = [((LEN, D), BF16)] * 5 + [
        ((LEN, D), F32), ((HEADS, LEN), F32), ((HEADS, LEN), F32), ((DI, D), BF16), ((D, D), BF16),
        ((1, DI), F32), ((1, 128), F32),
    ]
    return pl.pallas_call(
        forward_kernel,
        grid_spec=pltpu.PrefetchScalarGridSpec(
            num_scalar_prefetch=1,
            grid=(2 * BLOCKS,),
            in_specs=[block, block] + [whole(a.shape) for a in rest],
            out_specs=[whole(s) for s, _ in outs],
            scratch_shapes=[
                pltpu.VMEM((D, LEN), BF16),
                pltpu.VMEM((LEN, D), BF16),
                pltpu.VMEM((LEN, D), F32),
                pltpu.VMEM((LEN, D), BF16),
                pltpu.VMEM((LEN, DI), F32),
                pltpu.VMEM((1, DI), F32),
                pltpu.VMEM((1, DI), F32),
                pltpu.VMEM((DI, D), F32),
                pltpu.VMEM((D, D), F32),
            ],
        ),
        out_shape=[jax.ShapeDtypeStruct(s, t) for s, t in outs],
        compiler_params=pltpu.CompilerParams(
            dimension_semantics=("arbitrary",), vmem_limit_bytes=56 * 2**20
        ),
        cost_estimate=pl.CostEstimate(flops=10**10, bytes_accessed=2 * 10**7, transcendentals=10**7),
    )(meta, rows, side, *rest)


def backward(meta, queries, keys, values, grads, lse, delta, mixed, normed, *weights):
    lanes = pl.BlockSpec((LEN, 128), lambda i, m: (0, jnp.minimum(i, 3)))
    pair = pl.BlockSpec((1, 2, LEN), lambda i, m: (jnp.minimum(i, 3), 0, 0))
    outs = [((3 * D, D), BF16), ((2, D), F32)]
    return pl.pallas_call(
        backward_kernel,
        grid_spec=pltpu.PrefetchScalarGridSpec(
            num_scalar_prefetch=1,
            grid=(5,),
            in_specs=[lanes] * 4 + [pair] * 2 + [whole(a.shape) for a in (mixed, normed, *weights)],
            out_specs=[whole(s) for s, _ in outs],
            scratch_shapes=[
                pltpu.VMEM((4, LEN, 128), BF16),
                pltpu.VMEM((4, LEN, 128), BF16),
                pltpu.VMEM((4, LEN, 128), BF16),
                pltpu.VMEM((LEN, 128), F32),
                pltpu.VMEM((LEN, 128), F32),
                pltpu.VMEM((128, LEN), BF16),
            ],
        ),
        out_shape=[jax.ShapeDtypeStruct(s, t) for s, t in outs],
        compiler_params=pltpu.CompilerParams(
            dimension_semantics=("arbitrary",), vmem_limit_bytes=56 * 2**20
        ),
        cost_estimate=pl.CostEstimate(flops=10**10, bytes_accessed=10**7, transcendentals=10**7),
    )(
        meta, queries, keys, values, grads, lse.reshape(4, 2, LEN), delta.reshape(4, 2, LEN),
        mixed, normed, *weights,
    )


def to_samples(parts, me):
    got = [lax.dynamic_index_in_dim(parts, jnp.minimum(me, SAMPLES - 1), 0, keepdims=False)]
    for k in (1, 2, 3):
        sent = lax.dynamic_index_in_dim(
            parts, jnp.minimum((me + k) % 4, SAMPLES - 1), 0, keepdims=False
        )
        pairs = [(i, (i + k) % 4) for i in range(4) if (i + k) % 4 < SAMPLES]
        got.append(lax.ppermute(sent, CTX, pairs))
    return jnp.stack(got)


def swap_cores(value):
    return lax.ppermute(value, "core", [(0, 1), (1, 0)])


def scatter_half(terms, packet, upper):
    core = lax.axis_index("core")
    count = packet.shape[0]
    mine = lax.dynamic_slice_in_dim(terms, core * 256, 256, 1)
    other = lax.dynamic_slice_in_dim(terms, (1 - core) * 256, 256, 1)
    mine = mine.astype(F32) + swap_cores(other).astype(F32)
    pieces = mine.astype(BF16).reshape(4, 8, 48, 2, 128).transpose(1, 3, 0, 2, 4).reshape(16, 192, 128)
    pieces = jnp.concatenate([pieces, jnp.broadcast_to(packet[None], (16, count, 128))], axis=1)
    got = lax.all_to_all(pieces, PLANE, 0, 0)
    rows = jnp.sum(got[:, :192].astype(F32), axis=0).astype(BF16).reshape(4, 48, 128)
    packets = got[:, 192:].reshape(16 * count, 128)
    zeros = jnp.zeros_like(rows)
    rows = jnp.concatenate([zeros, rows] if upper else [rows, zeros], axis=0)
    pieces = jnp.concatenate([rows, jnp.broadcast_to(packets[None], (8, 16 * count, 128))], axis=1)
    got = lax.all_to_all(pieces, "z", 0, 0)
    rows = jnp.sum(got[:, :48].astype(F32), axis=0)
    return rows, got[:, 48:].reshape(128, count, 128)


def per_device(
    event_ids, lengths, event_side, dense_input, labels, event_table, seq_gain, w_mix, w_query,
    w_key, w_value, w_out, w_pool, w_cross, b_cross, w_heads,
):
    me = lax.axis_index(CTX)
    core = lax.axis_index("core")
    own = jnp.minimum(me, SAMPLES - 1)
    ids = to_samples(event_ids, me)
    side = to_samples(event_side, me)
    rows = jnp.take(event_table, ids, axis=0)
    length = jnp.where(me < SAMPLES, lengths[own], 0)
    meta = jnp.stack([me, length, labels[own, 0], labels[own, 1]]).astype(jnp.int32)
    dense = lax.dynamic_slice_in_dim(dense_input, own, 1, 0)
    dense_float = dense.astype(F32)
    mix_row = dot(dense, w_mix)
    base = dot(dense, w_cross) + b_cross[None]
    (queries, keys, values, grads, mixed, normed, lse, delta, pool_term, out_term, crossed, logit) = forward(
        meta, rows, side, mix_row, seq_gain[None], w_query, w_key, w_value, w_out, w_pool,
        w_out.T, w_pool.T, base, dense_float, w_heads.T,
    )
    packet = jnp.concatenate([dense.reshape(8, 128), crossed.astype(BF16).reshape(8, 128)])
    upper_rows, upper_packets = scatter_half(jnp.concatenate([out_term, pool_term]), packet, True)
    terms, small = backward(
        meta, queries, keys, values, grads, lse, delta, mixed, normed, w_query.T, w_key.T, w_value.T
    )
    logit_high = logit.astype(BF16)
    logit_low = (logit - logit_high.astype(F32)).astype(BF16)
    packet = jnp.concatenate(
        [small.astype(BF16).reshape(8, 128), logit_high, logit_low, jnp.zeros((6, 128), BF16)]
    )
    lower_rows, lower_packets = scatter_half(terms, packet, False)

    all_dense = upper_packets[:, :8].reshape(128, DI)
    all_crossed = upper_packets[:, 8:].reshape(128, DI).astype(F32)
    all_mix = lower_packets[:, :4].reshape(128, D)
    all_gain = lower_packets[:, 4:8].reshape(128, D).astype(F32)
    all_logit = (lower_packets[:, 8, :2].astype(F32) + lower_packets[:, 9, :2].astype(F32))
    high = lax.Precision.HIGHEST
    dense_rows = all_dense.astype(F32)
    all_gate = jnp.dot(all_logit, w_heads.T, precision=high) * dense_rows
    chip = lax.axis_index(("z", "ylo", "x", "yhi"))
    columns = lax.dynamic_slice_in_dim(dense_rows, chip * 8, 8, 1)
    cross = lax.dot_general(columns, all_gate, (((0,), (0,)), ((), ())), precision=high)
    mix = lax.dot_general(columns, all_mix.astype(F32), (((0,), (0,)), ((), ())), precision=high)
    gain = jnp.sum(all_gain, axis=0)
    bias = jnp.sum(all_gate, axis=0)
    heads = lax.dot_general(all_crossed, all_logit, (((0,), (0,)), ((), ())), precision=high)
    both = jnp.concatenate([cross, mix], axis=1)
    theirs = swap_cores(lax.dynamic_slice_in_dim(both, (1 - core) * 4, 4, 0))
    both = lax.dynamic_slice_in_dim(both, core * 4, 4, 0) + theirs
    flat = jnp.concatenate([gain, bias, heads.T.reshape(2 * DI)]).reshape(28, 128)
    flat = (flat + swap_cores(flat)).reshape(28 * 128)
    grad_heads = flat[D + DI :].reshape(2, DI).T

    z = lax.axis_index("z")
    block = jnp.where(z < 4, lower_rows, upper_rows).reshape(4, 12, 128)
    mine = lax.dynamic_index_in_dim(block, me, 0, keepdims=False)
    got = [mine]
    for k in (1, 2, 3):
        sent = lax.dynamic_index_in_dim(block, (me + k) % 4, 0, keepdims=False)
        got.append(lax.ppermute(sent, CTX, [(i, (i + k) % 4) for i in range(4)]))
    got = jnp.stack(got)
    ordered = [
        lax.dynamic_index_in_dim(got, (me - s) % 4, 0, keepdims=False) for s in (0, 2, 1, 3)
    ]
    grad_sequence = jnp.concatenate(ordered, axis=1)
    return (grad_sequence, both[:, DI:], both[:, :DI], flat[:D], flat[D : D + DI], grad_heads)


def solution(mesh):
    fine = Mesh(mesh.devices.reshape(8, 2, 4, 2, 2), ("z", "ylo", "x", "yhi", "core"))
    dp = ("z", "ylo", "x")
    every = dp + CTX
    in_specs = (P(dp, CTX), P(dp), P(dp, CTX, None), P(dp, None), P(dp, None)) + (P(),) * 11
    out_specs = (P(every, None), P(every, None), P(every, None), P(), P(), P())
    return jax.shard_map(
        per_device, mesh=fine, in_specs=in_specs, out_specs=out_specs, check_vma=False
    )
```

```python
import functools

import jax
import jax.numpy as jnp
from jax import lax
from jax.experimental import pallas as pl
from jax.experimental.pallas import tpu as pltpu
from jax.sharding import Mesh, PartitionSpec as P

HEADS = 8
BATCH = 192
SAMPLES = 3
BLOCK = 256
BLOCKS = 4
LEN = 1024
D = 512
DI = 1024
VOCAB = 2048
MASKED = -1e30
EPSILON = 1e-06
LOSS_SCALE = 32768.0
F32 = jnp.float32
BF16 = jnp.bfloat16
CTX = ("yhi", "core")
PLANE = ("ylo", "x", "yhi")


def dot(a, b):
    return lax.dot_general(a, b, (((1,), (0,)), ((), ())), preferred_element_type=F32)


def dot_nt(a, b):
    return lax.dot_general(a, b, (((1,), (1,)), ((), ())), preferred_element_type=F32)


def dot_tn(a, b):
    return lax.dot_general(a, b, (((0,), (0,)), ((), ())), preferred_element_type=F32)


def both_heads(rows):
    low = lax.broadcasted_iota(jnp.int32, rows.shape, 1) < 64
    zero = jnp.zeros_like(rows)
    return jnp.concatenate([jnp.where(low, rows, zero), jnp.where(low, zero, rows)], axis=0)


def causal(tile):
    key = lax.broadcasted_iota(jnp.int32, tile.shape, 0)
    query = lax.broadcasted_iota(jnp.int32, tile.shape, 1) & (BLOCK - 1)
    return key <= query


def forward_kernel(
    meta, part0, part1, part2, part3, table_ref, mix_ref, gain_ref, wq_ref, wk_ref, wv_ref, wo_ref,
    wp_ref, base_ref, dense_ref, heads_ref,
    q_ref, k_ref, v_ref, do_ref, mixed_ref, normed_ref, lse_ref, delta_ref, pool_ref, out_ref,
    packet_ref, logit_ref,
    part_ref, q_all, k_all, vt_ref, att_ref, o_ref, res_ref, pre_ref, sum_ref, scaled_ref,
    pool_acc, out_acc,
):
    step = pl.program_id(0)
    length = meta[1]

    @pl.when(step == 0)
    def _():
        sum_ref[...] = jnp.zeros_like(sum_ref)
        pool_acc[...] = jnp.zeros_like(pool_acc)
        out_acc[...] = jnp.zeros_like(out_acc)

    source = lax.rem(meta[0] - jnp.minimum(step, BLOCKS - 1) + BLOCKS, BLOCKS)
    for n, ref in enumerate((part0, part1, part2, part3)):

        @pl.when((step < BLOCKS) & (source == n))
        def _():
            part_ref[...] = ref[...]

    def ahead(c):
        here = slice(c * BLOCK, (c + 1) * BLOCK)
        codes = part_ref[BLOCK:, :].astype(F32)
        ids = (codes[:, :BLOCK] * 256.0 + codes[:, BLOCK:]).T[:, 0:1].astype(jnp.int32)
        slots = lax.broadcasted_iota(jnp.int32, (BLOCK, VOCAB), 1)
        picked = jnp.where(slots == ids, 1.0, 0.0).astype(BF16)
        tokens = dot(picked, table_ref[...]) + part_ref[:BLOCK, :].astype(F32)
        mean = jnp.mean(tokens * tokens, axis=1, keepdims=True)
        normed = tokens * lax.rsqrt(mean + EPSILON)
        normed_ref[...] = normed.astype(BF16)
        mixed = (normed * gain_ref[...] + mix_ref[...]).astype(BF16)
        mixed_ref[...] = mixed
        queries = (dot(mixed, wq_ref[...]).astype(BF16).astype(F32) * 0.125).astype(BF16)
        q_ref[...] = queries
        q_all[...] = queries
        keys_now = dot(mixed, wk_ref[...]).astype(BF16)
        k_ref[...] = keys_now
        k_all[here, :] = keys_now
        values = dot(mixed, wv_ref[...]).astype(BF16)
        v_ref[...] = values
        vt_ref[:, here] = values.T
        for p in range(4):
            lanes = slice(p * 128, (p + 1) * 128)
            chosen = both_heads(q_all[:, lanes])
            tiles = []
            for j in range(c + 1):
                tile = dot_nt(k_all[j * BLOCK : (j + 1) * BLOCK, lanes], chosen)
                if j == c:
                    tile = jnp.where(causal(tile), tile, MASKED)
                tiles.append(tile)
            top = functools.reduce(jnp.maximum, [jnp.max(t, axis=0, keepdims=True) for t in tiles])
            raised = [jnp.exp(t - top) for t in tiles]
            total = functools.reduce(jnp.add, [jnp.sum(t, axis=0, keepdims=True) for t in raised])
            inverse = 1.0 / total
            shares = [(t * inverse).astype(BF16) for t in raised]
            lse = top + jnp.log(total)
            lse_ref[p, 0:1, here] = lse[:, :BLOCK]
            lse_ref[p, 1:2, here] = lse[:, BLOCK:]
            first = jnp.zeros((64, BLOCK), F32)
            second = jnp.zeros((64, BLOCK), F32)
            for j in range(c + 1):
                keys = slice(j * BLOCK, (j + 1) * BLOCK)
                first += dot(vt_ref[p * 128 : p * 128 + 64, keys], shares[j][:, :BLOCK])
                second += dot(vt_ref[p * 128 + 64 : p * 128 + 128, keys], shares[j][:, BLOCK:])
            joined = jnp.concatenate([first, second], axis=0).T
            o_ref[here, lanes] = joined
            att_ref[here, lanes] = joined.astype(BF16)
        residual = tokens + dot(att_ref[here, :], wo_ref[...])
        half = residual.astype(BF16)
        res_ref[here, :] = half
        pre = dot(half, wp_ref[...])
        pre_ref[here, :] = pre
        valid = (c * BLOCK + lax.broadcasted_iota(jnp.int32, pre.shape, 0)) < length
        silu = jnp.where(valid, pre * jax.nn.sigmoid(pre), 0.0)
        sum_ref[...] += jnp.sum(silu, axis=0, keepdims=True)

    def blank(c):
        here = slice(c * BLOCK, (c + 1) * BLOCK)
        for ref in (q_ref, k_ref, v_ref, mixed_ref, normed_ref):
            ref[...] = jnp.zeros((BLOCK, D), ref.dtype)
        lse_ref[:, :, here] = jnp.zeros((4, 2, BLOCK), F32)
        delta_ref[:, :, here] = jnp.zeros((4, 2, BLOCK), F32)

    for c in range(BLOCKS):
        pl.when((step == c) & (length > c * BLOCK))(functools.partial(ahead, c))
        pl.when((step == c) & (length <= c * BLOCK))(functools.partial(blank, c))

    @pl.when(step == BLOCKS)
    def _():
        span = jnp.maximum(length, 1).astype(F32)
        dense = dense_ref[...]
        gate = base_ref[...] + sum_ref[...] / span
        crossed = dense + dense * gate
        rows = [dense[:, n * 128 : (n + 1) * 128] for n in range(8)]
        rows += [crossed[:, n * 128 : (n + 1) * 128] for n in range(8)]
        packet_ref[...] = jnp.concatenate(rows, axis=0).astype(BF16)
        a = jnp.sum(crossed * heads_ref[0:1, :], axis=1, keepdims=True)
        c = jnp.sum(crossed * heads_ref[1:2, :], axis=1, keepdims=True)
        clicked = meta[2].astype(F32)
        converted = (meta[2] * meta[3]).astype(F32)
        top = jnp.maximum(jnp.maximum(a, c), 0.0)
        ea, ec = jnp.exp(a - top), jnp.exp(c - top)
        below = jnp.exp(-top) + ea + ec
        grad_a = jax.nn.sigmoid(a) - clicked - converted * jax.nn.sigmoid(-a)
        grad_a = grad_a - (1.0 - converted) * (ea / below - jax.nn.sigmoid(a))
        grad_c = -converted * jax.nn.sigmoid(-c)
        grad_c = grad_c - (1.0 - converted) * (ec / below - jax.nn.sigmoid(c))
        factor = jnp.where(length > 0, LOSS_SCALE / BATCH, 0.0)
        grad_a = grad_a * factor
        grad_c = grad_c * factor
        lane = lax.broadcasted_iota(jnp.int32, (1, 128), 1)
        logit_ref[...] = jnp.where(lane == 0, grad_a, jnp.where(lane == 1, grad_c, 0.0))
        grad_gate = (grad_a * heads_ref[0:1, :] + grad_c * heads_ref[1:2, :]) * dense
        scaled_ref[...] = grad_gate / span

    def back(c):
        here = slice(c * BLOCK, (c + 1) * BLOCK)
        pre = pre_ref[here, :]
        sig = jax.nn.sigmoid(pre)
        valid = (c * BLOCK + lax.broadcasted_iota(jnp.int32, pre.shape, 0)) < length
        slope = sig * (1.0 + pre * (1.0 - sig)) * scaled_ref[...]
        grad_pre = jnp.where(valid, slope, 0.0).astype(BF16)
        pool_acc[...] += dot_tn(grad_pre, res_ref[here, :])
        grad_res = dot_nt(grad_pre, wp_ref[...]).astype(BF16)
        out_acc[...] += dot_tn(att_ref[here, :], grad_res)
        grad_att = dot_nt(grad_res, wo_ref[...]).astype(BF16)
        do_ref[...] = grad_att
        product = grad_att.astype(F32) * o_ref[here, :]
        head = lax.broadcasted_iota(jnp.int32, (HEADS, D), 0)
        column = lax.broadcasted_iota(jnp.int32, (HEADS, D), 1) // 64
        picks = jnp.where(head == column, 1.0, 0.0).astype(BF16)
        high = product.astype(BF16)
        low = (product - high.astype(F32)).astype(BF16)
        delta = dot_nt(picks, high) + dot_nt(picks, low)
        for p in range(4):
            delta_ref[p, :, here] = delta[2 * p : 2 * p + 2, :]

    def quiet():
        do_ref[...] = jnp.zeros((BLOCK, D), BF16)

    for c in range(BLOCKS):
        pl.when((step == BLOCKS + c) & (length > c * BLOCK))(functools.partial(back, c))
        pl.when((step == BLOCKS + c) & (length <= c * BLOCK))(quiet)

    @pl.when(step == 2 * BLOCKS - 1)
    def _():
        pool_ref[...] = pool_acc[...].astype(BF16)
        out_ref[...] = out_acc[...].astype(BF16)


def pair_kernel(
    meta, q_ref, k_ref, v_ref, do_ref, lse_ref, delta_ref, grad_ref, dk_acc, dv_acc, kt_ref
):
    length = meta[1]
    dk_acc[...] = jnp.zeros_like(dk_acc)
    dv_acc[...] = jnp.zeros_like(dv_acc)
    kt_ref[...] = k_ref[...].T

    def block(c):
        here = slice(c * BLOCK, (c + 1) * BLOCK)
        chosen = both_heads(q_ref[here, :])
        grads = both_heads(do_ref[here, :])
        lse = jnp.concatenate([lse_ref[0, 0:1, here], lse_ref[0, 1:2, here]], axis=1)
        delta = jnp.concatenate([delta_ref[0, 0:1, here], delta_ref[0, 1:2, here]], axis=1)
        first = jnp.zeros((64, BLOCK), F32)
        second = jnp.zeros((64, BLOCK), F32)
        for j in range(c + 1):
            keys = slice(j * BLOCK, (j + 1) * BLOCK)
            shares = jnp.exp(dot_nt(k_ref[keys, :], chosen) - lse)
            if j == c:
                shares = jnp.where(causal(shares), shares, 0.0)
            grad_shares = dot_nt(v_ref[keys, :], grads)
            grad_scores = (shares * (grad_shares - delta)).astype(BF16)
            dv_acc[keys, :] += dot(shares.astype(BF16), grads)
            dk_acc[keys, :] += dot(grad_scores, chosen)
            first += dot(kt_ref[0:64, keys], grad_scores[:, :BLOCK])
            second += dot(kt_ref[64:128, keys], grad_scores[:, BLOCK:])
        joined = jnp.concatenate([first, second], axis=0) * 0.125
        grad_ref[0, 0, here, :] = joined.T.astype(BF16)

    def blank(c):
        here = slice(c * BLOCK, (c + 1) * BLOCK)
        grad_ref[0, 0, here, :] = jnp.zeros((BLOCK, 128), BF16)

    for c in range(BLOCKS):
        pl.when(length > c * BLOCK)(functools.partial(block, c))
        pl.when(length <= c * BLOCK)(functools.partial(blank, c))
    grad_ref[1, 0] = dk_acc[...].astype(BF16)
    grad_ref[2, 0] = dv_acc[...].astype(BF16)


def term_kernel(
    one_ref, three_ref, mixed_ref, normed_ref, wq_ref, wk_ref, wv_ref, logit_ref,
    term_ref, packet_ref,
    turned_ref, total_ref,
):
    step = pl.program_id(0)

    @pl.when(step == 0)
    def _():
        turned_ref[...] = mixed_ref[...].T

    rows = jnp.concatenate([one_ref[0, 0]] + [three_ref[0, p] for p in range(3)], axis=1)
    term_ref[...] = dot(turned_ref[...], rows).astype(BF16)

    @pl.when(step == 0)
    def _():
        total_ref[...] = dot_nt(rows, wq_ref[...])

    @pl.when(step == 1)
    def _():
        total_ref[...] += dot_nt(rows, wk_ref[...])

    @pl.when(step == 2)
    def _():
        total = total_ref[...] + dot_nt(rows, wv_ref[...])
        mix = jnp.sum(total, axis=0, keepdims=True)
        gain = jnp.sum(total * normed_ref[...].astype(F32), axis=0, keepdims=True)
        logit = logit_ref[...]
        high = logit.astype(BF16).astype(F32)
        lines = [mix[:, n * 128 : (n + 1) * 128] for n in range(4)]
        lines += [gain[:, n * 128 : (n + 1) * 128] for n in range(4)]
        lines += [high, logit - high, jnp.zeros((6, 128), F32)]
        packet_ref[...] = jnp.concatenate(lines, axis=0).astype(BF16)


def piece_kernel(meta, term_ref, got_ref, packet_ref, piece_ref):
    for g in range(16):
        lanes = slice((g % 2) * 128, (g % 2) * 128 + 128)
        for n in range(4):
            total = term_ref[n, g // 2, :, lanes].astype(F32) + got_ref[n, g // 2, :, lanes].astype(F32)
            piece_ref[g, n * 48 : (n + 1) * 48, :] = total.astype(BF16)
        piece_ref[g, 192:, :] = packet_ref[...]


def sum_kernel(upper, got_ref, piece_ref):
    total = functools.reduce(jnp.add, [got_ref[g, :192, :].astype(F32) for g in range(16)])
    total = total.astype(BF16)
    packets = [got_ref[g, 192:, :] for g in range(16)]
    for z in range(8):
        n = z - 4 if upper else z
        inside = 0 <= n < 4
        piece_ref[z, :48, :] = total[n * 48 : (n + 1) * 48] if inside else jnp.zeros((48, 128), BF16)
        for g in range(16):
            piece_ref[z, 48 + g * 16 : 64 + g * 16, :] = packets[g]


def final_kernel(
    meta, upper_ref, lower_ref, upper_packets, lower_packets, heads_ref, row_ref, both_ref, flat_ref
):
    upper = functools.reduce(jnp.add, [upper_ref[z].astype(F32) for z in range(8)])
    lower = functools.reduce(jnp.add, [lower_ref[z].astype(F32) for z in range(8)])
    row_ref[...] = jnp.where(meta[5] < 4, lower, upper)
    logits = lower_packets[8].astype(F32) + lower_packets[9].astype(F32)
    grad_a, grad_c = logits[:, 0:1], logits[:, 1:2]
    chip = meta[4]
    first = lax.rem(chip, 16) * 8
    lane = lax.broadcasted_iota(jnp.int32, (8, 128), 1)
    line = lax.broadcasted_iota(jnp.int32, (8, 128), 0)
    picks = jnp.where(lane == first + line, 1.0, 0.0).astype(BF16)
    columns = dot_nt(picks, upper_packets[chip // 16])
    for r in range(8):
        lanes = slice(r * 128, (r + 1) * 128)
        dense = upper_packets[r].astype(F32)
        crossed = upper_packets[8 + r].astype(F32)
        gate = (grad_a * heads_ref[0:1, lanes] + grad_c * heads_ref[1:2, lanes]) * dense
        both_ref[:, lanes] = lax.dot_general(
            columns, gate, (((1,), (0,)), ((), ())),
            precision=lax.Precision.HIGHEST, preferred_element_type=F32,
        )
        flat_ref[4 + r : 5 + r, :] = jnp.sum(gate, axis=0, keepdims=True)
        flat_ref[12 + r : 13 + r, :] = jnp.sum(crossed * grad_a, axis=0, keepdims=True)
        flat_ref[20 + r : 21 + r, :] = jnp.sum(crossed * grad_c, axis=0, keepdims=True)
    for r in range(4):
        both_ref[:, DI + r * 128 : DI + (r + 1) * 128] = dot(columns.astype(BF16), lower_packets[r])
        flat_ref[r : r + 1, :] = jnp.sum(lower_packets[4 + r].astype(F32), axis=0, keepdims=True)


def whole(shape):
    return pl.BlockSpec(shape, lambda i, m: (0,) * len(shape))


def params(megabytes):
    return pltpu.CompilerParams(
        dimension_semantics=("arbitrary",), vmem_limit_bytes=megabytes * 2**20
    )


def cost(flops, moved, exps=0):
    return pl.CostEstimate(flops=flops, bytes_accessed=moved, transcendentals=exps)


def forward(meta, *rest):
    early = pl.BlockSpec((BLOCK, D), lambda i, m: (jnp.minimum(i, BLOCKS - 1), 0))
    late = pl.BlockSpec((BLOCK, D), lambda i, m: (jnp.maximum(i - BLOCKS, 0), 0))
    outs = [((LEN, D), BF16)] * 6 + [
        ((4, 2, LEN), F32), ((4, 2, LEN), F32), ((DI, D), BF16), ((D, D), BF16),
        ((16, 128), BF16), ((1, 128), F32),
    ]
    return pl.pallas_call(
        forward_kernel,
        grid_spec=pltpu.PrefetchScalarGridSpec(
            num_scalar_prefetch=1,
            grid=(2 * BLOCKS,),
            in_specs=[whole(a.shape) for a in rest],
            out_specs=[early] * 3 + [late] + [early] * 2 + [whole(s) for s, _ in outs[6:]],
            scratch_shapes=[
                pltpu.VMEM((BLOCK + 16, D), BF16),
                pltpu.VMEM((BLOCK, D), BF16),
                pltpu.VMEM((LEN, D), BF16),
                pltpu.VMEM((D, LEN), BF16),
                pltpu.VMEM((LEN, D), BF16),
                pltpu.VMEM((LEN, D), F32),
                pltpu.VMEM((LEN, D), BF16),
                pltpu.VMEM((LEN, DI), F32),
                pltpu.VMEM((1, DI), F32),
                pltpu.VMEM((1, DI), F32),
                pltpu.VMEM((DI, D), F32),
                pltpu.VMEM((D, D), F32),
            ],
        ),
        out_shape=[jax.ShapeDtypeStruct(s, t) for s, t in outs],
        compiler_params=params(56),
        cost_estimate=cost(10**10, 2 * 10**7, 10**7),
    )(meta, *rest)


def pairs_back(meta, first, count, queries, keys, values, grads, lse, delta):
    lanes = pl.BlockSpec((LEN, 128), lambda i, m: (0, first + i))
    pair = pl.BlockSpec((1, 2, LEN), lambda i, m: (first + i, 0, 0))
    return pl.pallas_call(
        pair_kernel,
        grid_spec=pltpu.PrefetchScalarGridSpec(
            num_scalar_prefetch=1,
            grid=(count,),
            in_specs=[lanes] * 4 + [pair] * 2,
            out_specs=pl.BlockSpec((3, 1, LEN, 128), lambda i, m: (0, i, 0, 0)),
            scratch_shapes=[
                pltpu.VMEM((LEN, 128), F32),
                pltpu.VMEM((LEN, 128), F32),
                pltpu.VMEM((128, LEN), BF16),
            ],
        ),
        out_shape=jax.ShapeDtypeStruct((3, count, LEN, 128), BF16),
        compiler_params=params(48),
        cost_estimate=cost(4 * 10**9 * count, 2 * 10**6 * count, 2 * 10**6 * count),
    )(meta, queries, keys, values, grads, lse, delta)


def terms_back(one, three, mixed, normed, w_query, w_key, w_value, logit):
    def full(array):
        return pl.BlockSpec(array.shape, lambda i: (0,) * array.ndim)

    rest = (mixed, normed, w_query, w_key, w_value, logit)
    return pl.pallas_call(
        term_kernel,
        grid=(3,),
        in_specs=[
            pl.BlockSpec((1, 1, LEN, 128), lambda i: (i, 0, 0, 0)),
            pl.BlockSpec((1, 3, LEN, 128), lambda i: (i, 0, 0, 0)),
        ] + [full(a) for a in rest],
        out_specs=[
            pl.BlockSpec((D, D), lambda i: (i, 0)),
            pl.BlockSpec((16, 128), lambda i: (0, 0)),
        ],
        out_shape=[
            jax.ShapeDtypeStruct((3 * D, D), BF16), jax.ShapeDtypeStruct((16, 128), BF16)
        ],
        scratch_shapes=[pltpu.VMEM((D, LEN), BF16), pltpu.VMEM((LEN, D), F32)],
        compiler_params=params(48),
        cost_estimate=cost(4 * 10**9, 8 * 10**6),
    )(one, three, *rest)


def cut_pieces(meta, terms, got, packet):
    half = pl.BlockSpec((4, 8, 48, 256), lambda i, m: (0, 0, 0, m[6]))
    return pl.pallas_call(
        piece_kernel,
        grid_spec=pltpu.PrefetchScalarGridSpec(
            num_scalar_prefetch=1,
            grid=(1,),
            in_specs=[half, whole((4, 8, 48, 256)), whole((16, 128))],
            out_specs=whole((16, 208, 128)),
        ),
        out_shape=jax.ShapeDtypeStruct((16, 208, 128), BF16),
        compiler_params=params(32),
        cost_estimate=cost(10**6, 3 * 10**6),
    )(meta, terms.reshape(4, 8, 48, D), got.reshape(4, 8, 48, 256), packet)


def sum_pieces(got, upper):
    return pl.pallas_call(
        functools.partial(sum_kernel, upper),
        out_shape=jax.ShapeDtypeStruct((8, 304, 128), BF16),
        compiler_params=pltpu.CompilerParams(vmem_limit_bytes=32 * 2**20),
        cost_estimate=cost(10**6, 2 * 10**6),
    )(got)


def finish(meta, upper, lower, w_heads):
    def packets(got):
        return got[:, 48:].reshape(128, 16, 128).transpose(1, 0, 2)

    rest = (upper[:, :48], lower[:, :48], packets(upper), packets(lower), w_heads.T)
    outs = ((48, 128), (8, DI + D), (28, 128))
    return pl.pallas_call(
        final_kernel,
        grid_spec=pltpu.PrefetchScalarGridSpec(
            num_scalar_prefetch=1,
            grid=(1,),
            in_specs=[whole(a.shape) for a in rest],
            out_specs=[whole(s) for s in outs],
        ),
        out_shape=[jax.ShapeDtypeStruct(s, F32) for s in outs],
        compiler_params=params(32),
        cost_estimate=cost(10**7, 10**6),
    )(meta, *rest)


def to_samples(event_ids, event_side, me):
    codes = jnp.concatenate([event_ids // 256, event_ids % 256], axis=1).astype(BF16)
    codes = jnp.concatenate([codes[:, None], jnp.zeros((SAMPLES, 15, D), BF16)], axis=1)

    def part(sample):
        sample = jnp.minimum(sample, SAMPLES - 1)
        side = lax.dynamic_index_in_dim(event_side, sample, 0, keepdims=False)
        code = lax.dynamic_index_in_dim(codes, sample, 0, keepdims=False)
        return jnp.concatenate([side, code])

    got = [part(me)]
    for k in (1, 2, 3):
        pairs = [(i, (i + k) % 4) for i in range(4) if (i + k) % 4 < SAMPLES]
        got.append(lax.ppermute(part((me + k) % 4), CTX, pairs))
    return got


def swap_cores(value):
    return lax.ppermute(value, "core", [(0, 1), (1, 0)])


def per_device(
    event_ids, lengths, event_side, dense_input, labels, event_table, seq_gain, w_mix, w_query,
    w_key, w_value, w_out, w_pool, w_cross, b_cross, w_heads,
):
    me = lax.axis_index(CTX)
    core = lax.axis_index("core")
    chip = lax.axis_index(("z", "ylo", "x", "yhi"))
    own = jnp.minimum(me, SAMPLES - 1)
    parts = to_samples(event_ids, event_side, me)
    length = jnp.where(me < SAMPLES, lengths[own], 0)
    meta = [me, length, labels[own, 0], labels[own, 1], chip, lax.axis_index("z"), core]
    meta = jnp.stack(meta).astype(jnp.int32)
    dense = lax.dynamic_slice_in_dim(dense_input, own, 1, 0)
    mix_row = dot(dense, w_mix)
    base = dot(dense, w_cross) + b_cross[None]

    def other_half(terms):
        return swap_cores(lax.dynamic_slice_in_dim(terms, (1 - core) * 256, 256, 1))

    (queries, keys, values, grads, mixed, normed, lse, delta, pool_term, out_term, packet, logit) = forward(
        meta, *parts, event_table, mix_row, seq_gain[None], w_query, w_key, w_value, w_out, w_pool,
        base, dense.astype(F32), w_heads.T,
    )
    upper = jnp.concatenate([out_term, pool_term])
    upper_got = other_half(upper)
    attention = (queries, keys, values, grads, lse, delta)
    one = pairs_back(meta, 0, 1, *attention)
    upper_got, one = lax.optimization_barrier((upper_got, one))
    pieces = cut_pieces(meta, upper, upper_got, packet)
    pieces, attention = lax.optimization_barrier((pieces, attention))
    upper_plane = lax.all_to_all(pieces, PLANE, 0, 0)
    three = pairs_back(meta, 1, 3, *attention)
    upper_plane, three = lax.optimization_barrier((upper_plane, three))
    pieces = sum_pieces(upper_plane, True)
    pieces, three = lax.optimization_barrier((pieces, three))
    upper_all = lax.all_to_all(pieces, "z", 0, 0)
    lower, packet = terms_back(one, three, mixed, normed, w_query, w_key, w_value, logit)
    lower_got = other_half(lower)
    pieces = cut_pieces(meta, lower, lower_got, packet)
    lower_plane = lax.all_to_all(pieces, PLANE, 0, 0)
    pieces = sum_pieces(lower_plane, False)
    lower_all = lax.all_to_all(pieces, "z", 0, 0)
    rows, both, flat = finish(meta, upper_all, lower_all, w_heads)
    theirs = swap_cores(lax.dynamic_slice_in_dim(both, (1 - core) * 4, 4, 0))
    both = lax.dynamic_slice_in_dim(both, core * 4, 4, 0) + theirs
    flat = (flat + swap_cores(flat)).reshape(28 * 128)
    grad_heads = flat[D + DI :].reshape(2, DI).T
    block = rows.reshape(4, 12, 128)
    mine = lax.dynamic_index_in_dim(block, me, 0, keepdims=False)
    got = [mine]
    for k in (1, 2, 3):
        sent = lax.dynamic_index_in_dim(block, (me + k) % 4, 0, keepdims=False)
        got.append(lax.ppermute(sent, CTX, [(i, (i + k) % 4) for i in range(4)]))
    got = jnp.stack(got)
    ordered = [
        lax.dynamic_index_in_dim(got, (me - s) % 4, 0, keepdims=False) for s in (0, 2, 1, 3)
    ]
    grad_sequence = jnp.concatenate(ordered, axis=1)
    return (grad_sequence, both[:, DI:], both[:, :DI], flat[:D], flat[D : D + DI], grad_heads)


def solution(mesh):
    fine = Mesh(mesh.devices.reshape(8, 2, 4, 2, 2), ("z", "ylo", "x", "yhi", "core"))
    dp = ("z", "ylo", "x")
    every = dp + CTX
    in_specs = (P(dp, CTX), P(dp), P(dp, CTX, None), P(dp, None), P(dp, None)) + (P(),) * 11
    out_specs = (P(every, None), P(every, None), P(every, None), P(), P(), P())
    return jax.shard_map(
        per_device, mesh=fine, in_specs=in_specs, out_specs=out_specs, check_vma=False
    )
```

```python
import functools

import jax
import jax.numpy as jnp
from jax import lax
from jax.experimental import pallas as pl
from jax.experimental.pallas import tpu as pltpu
from jax.sharding import Mesh, PartitionSpec as P

HEADS = 8
BATCH = 192
SAMPLES = 3
BLOCK = 256
BLOCKS = 4
LEN = 1024
D = 512
DI = 1024
VOCAB = 2048
MASKED = -1e30
EPSILON = 1e-06
LOSS_SCALE = 32768.0
F32 = jnp.float32
BF16 = jnp.bfloat16
CTX = ("yhi", "core")
PLANE = ("ylo", "x", "yhi")


def dot(a, b):
    return lax.dot_general(a, b, (((1,), (0,)), ((), ())), preferred_element_type=F32)


def dot_nt(a, b):
    return lax.dot_general(a, b, (((1,), (1,)), ((), ())), preferred_element_type=F32)


def dot_tn(a, b):
    return lax.dot_general(a, b, (((0,), (0,)), ((), ())), preferred_element_type=F32)


def both_heads(rows):
    low = lax.broadcasted_iota(jnp.int32, rows.shape, 1) < 64
    zero = jnp.zeros_like(rows)
    return jnp.concatenate([jnp.where(low, rows, zero), jnp.where(low, zero, rows)], axis=0)


def causal(tile):
    key = lax.broadcasted_iota(jnp.int32, tile.shape, 0)
    query = lax.broadcasted_iota(jnp.int32, tile.shape, 1) & (BLOCK - 1)
    return key <= query


def forward_kernel(
    meta, part0, part1, part2, part3, mix_ref, gain_ref, base_ref, dense_ref, heads_ref,
    table_far, wq_far, wk_far, wv_far, wo_far, wp_far,
    q_ref, k_ref, v_ref, do_ref, mixed_ref, normed_ref, lse_ref, delta_ref, upper_ref,
    packet_ref, logit_ref,
    part_ref, q_all, k_all, vt_ref, att_ref, o_ref, res_ref, pre_ref, sum_ref, scaled_ref,
    pool_acc, out_acc, table_ref, wq_ref, wk_ref, wv_ref, wo_ref, wp_ref, sems,
):
    far = (table_far, wq_far, wk_far, wv_far, wo_far, wp_far)
    near = (table_ref, wq_ref, wk_ref, wv_ref, wo_ref, wp_ref)
    copies = [pltpu.make_async_copy(f, n, sems.at[i]) for i, (f, n) in enumerate(zip(far, near))]
    step = pl.program_id(0)
    length = meta[1]

    @pl.when(step == 0)
    def _():
        for copy in copies:
            copy.start()
        sum_ref[...] = jnp.zeros_like(sum_ref)
        pool_acc[...] = jnp.zeros_like(pool_acc)
        out_acc[...] = jnp.zeros_like(out_acc)

    source = lax.rem(meta[0] - jnp.minimum(step, BLOCKS - 1) + BLOCKS, BLOCKS)
    for n, ref in enumerate((part0, part1, part2, part3)):

        @pl.when((step < BLOCKS) & (source == n))
        def _():
            part_ref[...] = ref[...]

    def ahead(c):
        here = slice(c * BLOCK, (c + 1) * BLOCK)
        if c == 0:
            for copy in copies[:4]:
                copy.wait()
        codes = part_ref[BLOCK:, :].astype(F32)
        ids = (codes[:, :BLOCK] * 256.0 + codes[:, BLOCK:]).T[:, 0:1].astype(jnp.int32)
        slots = lax.broadcasted_iota(jnp.int32, (BLOCK, VOCAB), 1)
        picked = jnp.where(slots == ids, 1.0, 0.0).astype(BF16)
        tokens = dot(picked, table_ref[...]) + part_ref[:BLOCK, :].astype(F32)
        mean = jnp.mean(tokens * tokens, axis=1, keepdims=True)
        normed = tokens * lax.rsqrt(mean + EPSILON)
        normed_ref[...] = normed.astype(BF16)
        mixed = (normed * gain_ref[...] + mix_ref[...]).astype(BF16)
        mixed_ref[...] = mixed
        queries = (dot(mixed, wq_ref[...]).astype(BF16).astype(F32) * 0.125).astype(BF16)
        q_ref[...] = queries
        q_all[...] = queries
        keys_now = dot(mixed, wk_ref[...]).astype(BF16)
        k_ref[...] = keys_now
        k_all[here, :] = keys_now
        values = dot(mixed, wv_ref[...]).astype(BF16)
        v_ref[...] = values
        vt_ref[:, here] = values.T
        for p in range(4):
            lanes = slice(p * 128, (p + 1) * 128)
            chosen = both_heads(q_all[:, lanes])
            tiles = []
            for j in range(c + 1):
                tile = dot_nt(k_all[j * BLOCK : (j + 1) * BLOCK, lanes], chosen)
                if j == c:
                    tile = jnp.where(causal(tile), tile, MASKED)
                tiles.append(tile)
            top = functools.reduce(jnp.maximum, [jnp.max(t, axis=0, keepdims=True) for t in tiles])
            raised = [jnp.exp(t - top) for t in tiles]
            total = functools.reduce(jnp.add, [jnp.sum(t, axis=0, keepdims=True) for t in raised])
            inverse = 1.0 / total
            shares = [(t * inverse).astype(BF16) for t in raised]
            lse = top + jnp.log(total)
            lse_ref[p, 0:1, here] = lse[:, :BLOCK]
            lse_ref[p, 1:2, here] = lse[:, BLOCK:]
            first = jnp.zeros((64, BLOCK), F32)
            second = jnp.zeros((64, BLOCK), F32)
            for j in range(c + 1):
                keys = slice(j * BLOCK, (j + 1) * BLOCK)
                first += dot(vt_ref[p * 128 : p * 128 + 64, keys], shares[j][:, :BLOCK])
                second += dot(vt_ref[p * 128 + 64 : p * 128 + 128, keys], shares[j][:, BLOCK:])
            joined = jnp.concatenate([first, second], axis=0).T
            o_ref[here, lanes] = joined
            att_ref[here, lanes] = joined.astype(BF16)
        if c == 0:
            for copy in copies[4:]:
                copy.wait()
        residual = tokens + dot(att_ref[here, :], wo_ref[...])
        half = residual.astype(BF16)
        res_ref[here, :] = half
        pre = dot(half, wp_ref[...])
        pre_ref[here, :] = pre
        valid = (c * BLOCK + lax.broadcasted_iota(jnp.int32, pre.shape, 0)) < length
        silu = jnp.where(valid, pre * jax.nn.sigmoid(pre), 0.0)
        sum_ref[...] += jnp.sum(silu, axis=0, keepdims=True)

    def blank(c):
        if c == 0:
            for copy in copies:
                copy.wait()
        here = slice(c * BLOCK, (c + 1) * BLOCK)
        for ref in (q_ref, k_ref, v_ref, mixed_ref, normed_ref):
            ref[...] = jnp.zeros((BLOCK, D), ref.dtype)
        lse_ref[:, :, here] = jnp.zeros((4, 2, BLOCK), F32)
        delta_ref[:, :, here] = jnp.zeros((4, 2, BLOCK), F32)

    for c in range(BLOCKS):
        pl.when((step == c) & (length > c * BLOCK))(functools.partial(ahead, c))
        pl.when((step == c) & (length <= c * BLOCK))(functools.partial(blank, c))

    @pl.when(step == BLOCKS)
    def _():
        span = jnp.maximum(length, 1).astype(F32)
        dense = dense_ref[...]
        gate = base_ref[...] + sum_ref[...] / span
        crossed = dense + dense * gate
        rows = [dense[:, n * 128 : (n + 1) * 128] for n in range(8)]
        rows += [crossed[:, n * 128 : (n + 1) * 128] for n in range(8)]
        packet_ref[...] = jnp.concatenate(rows, axis=0).astype(BF16)
        a = jnp.sum(crossed * heads_ref[0:1, :], axis=1, keepdims=True)
        c = jnp.sum(crossed * heads_ref[1:2, :], axis=1, keepdims=True)
        clicked = meta[2].astype(F32)
        converted = (meta[2] * meta[3]).astype(F32)
        top = jnp.maximum(jnp.maximum(a, c), 0.0)
        ea, ec = jnp.exp(a - top), jnp.exp(c - top)
        below = jnp.exp(-top) + ea + ec
        grad_a = jax.nn.sigmoid(a) - clicked - converted * jax.nn.sigmoid(-a)
        grad_a = grad_a - (1.0 - converted) * (ea / below - jax.nn.sigmoid(a))
        grad_c = -converted * jax.nn.sigmoid(-c)
        grad_c = grad_c - (1.0 - converted) * (ec / below - jax.nn.sigmoid(c))
        factor = jnp.where(length > 0, LOSS_SCALE / BATCH, 0.0)
        grad_a = grad_a * factor
        grad_c = grad_c * factor
        lane = lax.broadcasted_iota(jnp.int32, (1, 128), 1)
        logit_ref[...] = jnp.where(lane == 0, grad_a, jnp.where(lane == 1, grad_c, 0.0))
        grad_gate = (grad_a * heads_ref[0:1, :] + grad_c * heads_ref[1:2, :]) * dense
        scaled_ref[...] = grad_gate / span

    def back(c):
        here = slice(c * BLOCK, (c + 1) * BLOCK)
        pre = pre_ref[here, :]
        sig = jax.nn.sigmoid(pre)
        valid = (c * BLOCK + lax.broadcasted_iota(jnp.int32, pre.shape, 0)) < length
        slope = sig * (1.0 + pre * (1.0 - sig)) * scaled_ref[...]
        grad_pre = jnp.where(valid, slope, 0.0).astype(BF16)
        pool_acc[...] += dot_tn(grad_pre, res_ref[here, :])
        grad_res = dot_nt(grad_pre, wp_ref[...]).astype(BF16)
        out_acc[...] += dot_tn(att_ref[here, :], grad_res)
        grad_att = dot_nt(grad_res, wo_ref[...]).astype(BF16)
        do_ref[...] = grad_att
        product = grad_att.astype(F32) * o_ref[here, :]
        head = lax.broadcasted_iota(jnp.int32, (HEADS, D), 0)
        column = lax.broadcasted_iota(jnp.int32, (HEADS, D), 1) // 64
        picks = jnp.where(head == column, 1.0, 0.0).astype(BF16)
        high = product.astype(BF16)
        low = (product - high.astype(F32)).astype(BF16)
        delta = dot_nt(picks, high) + dot_nt(picks, low)
        for p in range(4):
            delta_ref[p, :, here] = delta[2 * p : 2 * p + 2, :]

    def quiet():
        do_ref[...] = jnp.zeros((BLOCK, D), BF16)

    for c in range(BLOCKS):
        pl.when((step == BLOCKS + c) & (length > c * BLOCK))(functools.partial(back, c))
        pl.when((step == BLOCKS + c) & (length <= c * BLOCK))(quiet)

    @pl.when(step == 2 * BLOCKS - 1)
    def _():
        upper_ref[:D, :] = out_acc[...].astype(BF16)
        upper_ref[D:, :] = pool_acc[...].astype(BF16)


def pair_body(
    length, q_ref, k_ref, v_ref, do_ref, lse_ref, delta_ref, dq_ref, dk_ref, dv_ref, dk_acc, dv_acc, kt_ref
):
    dk_acc[...] = jnp.zeros_like(dk_acc)
    dv_acc[...] = jnp.zeros_like(dv_acc)
    kt_ref[...] = k_ref[...].T

    def block(c):
        here = slice(c * BLOCK, (c + 1) * BLOCK)
        chosen = both_heads(q_ref[here, :])
        grads = both_heads(do_ref[here, :])
        lse = jnp.concatenate([lse_ref[0, 0:1, here], lse_ref[0, 1:2, here]], axis=1)
        delta = jnp.concatenate([delta_ref[0, 0:1, here], delta_ref[0, 1:2, here]], axis=1)
        first = jnp.zeros((64, BLOCK), F32)
        second = jnp.zeros((64, BLOCK), F32)
        for j in range(c + 1):
            keys = slice(j * BLOCK, (j + 1) * BLOCK)
            shares = jnp.exp(dot_nt(k_ref[keys, :], chosen) - lse)
            if j == c:
                shares = jnp.where(causal(shares), shares, 0.0)
            grad_shares = dot_nt(v_ref[keys, :], grads)
            grad_scores = (shares * (grad_shares - delta)).astype(BF16)
            dv_acc[keys, :] += dot(shares.astype(BF16), grads)
            dk_acc[keys, :] += dot(grad_scores, chosen)
            first += dot(kt_ref[0:64, keys], grad_scores[:, :BLOCK])
            second += dot(kt_ref[64:128, keys], grad_scores[:, BLOCK:])
        joined = jnp.concatenate([first, second], axis=0) * 0.125
        dq_ref[here, :] = joined.T.astype(BF16)

    def blank(c):
        here = slice(c * BLOCK, (c + 1) * BLOCK)
        dq_ref[here, :] = jnp.zeros((BLOCK, 128), BF16)

    for c in range(BLOCKS):
        pl.when(length > c * BLOCK)(functools.partial(block, c))
        pl.when(length <= c * BLOCK)(functools.partial(blank, c))
    dk_ref[...] = dk_acc[...].astype(BF16)
    dv_ref[...] = dv_acc[...].astype(BF16)


def pair_kernel(
    meta, q_ref, k_ref, v_ref, do_ref, lse_ref, delta_ref, grad_ref, dk_acc, dv_acc, kt_ref
):
    pair_body(
        meta[1], q_ref, k_ref, v_ref, do_ref, lse_ref, delta_ref,
        grad_ref.at[0], grad_ref.at[1], grad_ref.at[2], dk_acc, dv_acc, kt_ref,
    )


def rest_kernel(
    meta, q_ref, k_ref, v_ref, do_ref, lse_ref, delta_ref, logit_ref,
    one_far, mixed_far, normed_far, wq_far, wk_far, wv_far,
    term_ref, packet_ref,
    dk_acc, dv_acc, kt_ref, grad_ref, one_ref, mixed_ref, normed_ref, wq_ref, wk_ref, wv_ref, sems,
):
    step = pl.program_id(0)
    far = (one_far, mixed_far, normed_far, wq_far, wk_far, wv_far)
    near = (one_ref, mixed_ref, normed_ref, wq_ref, wk_ref, wv_ref)
    copies = [pltpu.make_async_copy(f, n, sems.at[i]) for i, (f, n) in enumerate(zip(far, near))]

    @pl.when(step == 0)
    def _():
        for copy in copies:
            copy.start()

    pair_body(
        meta[1], q_ref, k_ref, v_ref, do_ref, lse_ref, delta_ref,
        grad_ref.at[0, step], grad_ref.at[1, step], grad_ref.at[2, step], dk_acc, dv_acc, kt_ref,
    )

    @pl.when(step == 2)
    def _():
        for copy in copies:
            copy.wait()
        turned = mixed_ref[...].T
        total = None
        for n, weight in enumerate((wq_ref, wk_ref, wv_ref)):
            rows = jnp.concatenate([one_ref[n]] + [grad_ref[n, p] for p in range(3)], axis=1)
            term_ref[n * D : (n + 1) * D, :] = dot(turned, rows).astype(BF16)
            part = dot_nt(rows, weight[...])
            total = part if total is None else total + part
        mix = jnp.sum(total, axis=0, keepdims=True)
        gain = jnp.sum(total * normed_ref[...].astype(F32), axis=0, keepdims=True)
        logit = logit_ref[...]
        high = logit.astype(BF16).astype(F32)
        lines = [mix[:, n * 128 : (n + 1) * 128] for n in range(4)]
        lines += [gain[:, n * 128 : (n + 1) * 128] for n in range(4)]
        lines += [high, logit - high, jnp.zeros((6, 128), F32)]
        packet_ref[...] = jnp.concatenate(lines, axis=0).astype(BF16)


def piece_kernel(meta, term_ref, got_ref, packet_ref, piece_ref):
    for g in range(16):
        lanes = slice((g % 2) * 128, (g % 2) * 128 + 128)
        for n in range(4):
            total = term_ref[n, g // 2, :, lanes].astype(F32) + got_ref[n, g // 2, :, lanes].astype(F32)
            piece_ref[g, n * 48 : (n + 1) * 48, :] = total.astype(BF16)
        piece_ref[g, 192:, :] = packet_ref[...]


def exact_dot(a, b):
    return lax.dot_general(
        a, b, (((1,), (0,)), ((), ())),
        precision=lax.Precision.HIGHEST, preferred_element_type=F32,
    )


def sum_kernel(meta, upper_ref, lower_ref, heads_ref, piece_ref):
    upper_packets = [upper_ref[g, 192:, :].astype(F32) for g in range(16)]
    lower_packets = [lower_ref[g, 192:, :].astype(F32) for g in range(16)]

    def pick(packets, row):
        return jnp.concatenate([p[row : row + 1, :] for p in packets], axis=0)

    upper = functools.reduce(jnp.add, [upper_ref[g, :192, :].astype(F32) for g in range(16)])
    lower = functools.reduce(jnp.add, [lower_ref[g, :192, :].astype(F32) for g in range(16)])
    for n in range(4):
        piece_ref[n, :48, :] = lower[n * 48 : (n + 1) * 48].astype(BF16)
        piece_ref[4 + n, :48, :] = upper[n * 48 : (n + 1) * 48].astype(BF16)
    logits = pick(lower_packets, 8) + pick(lower_packets, 9)
    grad_a, grad_c = logits[:, 0:1], logits[:, 1:2]
    lane = lax.broadcasted_iota(jnp.int32, (8, 128), 1)
    line = lax.broadcasted_iota(jnp.int32, (8, 128), 0)
    picks = jnp.where(lane == meta[7] * 8 + line, 1.0, 0.0).astype(BF16)
    dense = [pick(upper_packets, r) for r in range(8)]
    columns = jnp.concatenate([dot_nt(picks, d.astype(BF16)) for d in dense], axis=0)
    flat = [jnp.sum(pick(lower_packets, 4 + r), axis=0, keepdims=True) for r in range(4)]
    gates = []
    for r in range(8):
        lanes = slice(r * 128, (r + 1) * 128)
        gate = (grad_a * heads_ref[0:1, lanes] + grad_c * heads_ref[1:2, lanes]) * dense[r]
        gates.append(gate)
        flat.append(jnp.sum(gate, axis=0, keepdims=True))
    crossed = [pick(upper_packets, 8 + r) for r in range(8)]
    flat += [jnp.sum(d * grad_a, axis=0, keepdims=True) for d in crossed]
    flat += [jnp.sum(d * grad_c, axis=0, keepdims=True) for d in crossed]
    flat = jnp.concatenate(flat + [jnp.zeros((4, 128), F32)], axis=0).astype(BF16)
    products = [exact_dot(columns, gate) for gate in gates]
    products += [exact_dot(columns, pick(lower_packets, r)) for r in range(4)]
    for z in range(8):
        rows = jnp.concatenate([p[z * 8 : (z + 1) * 8, :] for p in products], axis=0)
        piece_ref[z, 48:144, :] = rows.astype(BF16)
        piece_ref[z, 144:176, :] = flat


def final_kernel(got_ref, row_ref, share_ref):
    total = functools.reduce(jnp.add, [got_ref[z].astype(F32) for z in range(8)])
    for n in range(4):
        row_ref[n] = total[n * 12 : (n + 1) * 12, :]
    share_ref[...] = total[48:176, :]


def join_kernel(meta, row0, row1, row2, row3, share_ref, swapped_ref, sequence_ref, mix_ref, cross_ref, gain_ref, bias_ref, heads_ref):
    for source, place in ((0, 0), (2, 1), (1, 2), (3, 3)):
        entry = lax.rem(meta[0] - source + 4, 4)
        for n, ref in enumerate((row0, row1, row2, row3)):

            @pl.when(entry == n)
            def _():
                sequence_ref[:, place * 128 : (place + 1) * 128] = ref[...]

    total = share_ref[...] + swapped_ref[...]
    upper = meta[6] == 1
    for r in range(12):
        mine = jnp.where(upper, total[r * 8 + 4 : r * 8 + 8, :], total[r * 8 : r * 8 + 4, :])
        if r < 8:
            cross_ref[:, r * 128 : (r + 1) * 128] = mine
        else:
            mix_ref[:, (r - 8) * 128 : (r - 7) * 128] = mine
    for r in range(4):
        gain_ref[:, r * 128 : (r + 1) * 128] = total[96 + r : 97 + r, :]
    for r in range(8):
        lanes = slice(r * 128, (r + 1) * 128)
        bias_ref[:, lanes] = total[100 + r : 101 + r, :]
        heads_ref[0:1, lanes] = total[108 + r : 109 + r, :]
        heads_ref[1:2, lanes] = total[116 + r : 117 + r, :]


def whole(shape):
    return pl.BlockSpec(shape, lambda i, m: (0,) * len(shape))


def params(megabytes):
    return pltpu.CompilerParams(
        dimension_semantics=("arbitrary",), vmem_limit_bytes=megabytes * 2**20
    )


def cost(flops, moved, exps=0):
    return pl.CostEstimate(flops=flops, bytes_accessed=moved, transcendentals=exps)


def forward(meta, small, large):
    early = pl.BlockSpec((BLOCK, D), lambda i, m: (jnp.minimum(i, BLOCKS - 1), 0))
    late = pl.BlockSpec((BLOCK, D), lambda i, m: (jnp.maximum(i - BLOCKS, 0), 0))
    outs = [((LEN, D), BF16)] * 6 + [
        ((4, 2, LEN), F32), ((4, 2, LEN), F32), ((3 * D, D), BF16), ((16, 128), BF16),
        ((1, 128), F32),
    ]
    return pl.pallas_call(
        forward_kernel,
        grid_spec=pltpu.PrefetchScalarGridSpec(
            num_scalar_prefetch=1,
            grid=(2 * BLOCKS,),
            in_specs=[whole(a.shape) for a in small] + [pl.BlockSpec(memory_space=pl.ANY)] * 6,
            out_specs=[early] * 3 + [late] + [early] * 2 + [whole(s) for s, _ in outs[6:]],
            scratch_shapes=[
                pltpu.VMEM((BLOCK + 16, D), BF16),
                pltpu.VMEM((BLOCK, D), BF16),
                pltpu.VMEM((LEN, D), BF16),
                pltpu.VMEM((D, LEN), BF16),
                pltpu.VMEM((LEN, D), BF16),
                pltpu.VMEM((LEN, D), F32),
                pltpu.VMEM((LEN, D), BF16),
                pltpu.VMEM((LEN, DI), F32),
                pltpu.VMEM((1, DI), F32),
                pltpu.VMEM((1, DI), F32),
                pltpu.VMEM((DI, D), F32),
                pltpu.VMEM((D, D), F32),
            ] + [pltpu.VMEM(a.shape, BF16) for a in large] + [pltpu.SemaphoreType.DMA((6,))],
        ),
        out_shape=[jax.ShapeDtypeStruct(s, t) for s, t in outs],
        compiler_params=params(58),
        cost_estimate=cost(10**10, 2 * 10**7, 10**7),
    )(meta, *small, *large)


def first_pair_back(meta, queries, keys, values, grads, lse, delta):
    lanes = pl.BlockSpec((LEN, 128), lambda i, m: (0, i))
    pair = pl.BlockSpec((1, 2, LEN), lambda i, m: (i, 0, 0))
    return pl.pallas_call(
        pair_kernel,
        grid_spec=pltpu.PrefetchScalarGridSpec(
            num_scalar_prefetch=1,
            grid=(1,),
            in_specs=[lanes] * 4 + [pair] * 2,
            out_specs=whole((3, LEN, 128)),
            scratch_shapes=[
                pltpu.VMEM((LEN, 128), F32),
                pltpu.VMEM((LEN, 128), F32),
                pltpu.VMEM((128, LEN), BF16),
            ],
        ),
        out_shape=jax.ShapeDtypeStruct((3, LEN, 128), BF16),
        compiler_params=params(60),
        cost_estimate=cost(4 * 10**9, 2 * 10**6, 2 * 10**6),
    )(meta, queries, keys, values, grads, lse, delta)


def rest_back(meta, queries, keys, values, grads, lse, delta, logit, *far):
    lanes = pl.BlockSpec((LEN, 128), lambda i, m: (0, 1 + i))
    pair = pl.BlockSpec((1, 2, LEN), lambda i, m: (1 + i, 0, 0))
    outs = ((3 * D, D), (16, 128))
    return pl.pallas_call(
        rest_kernel,
        grid_spec=pltpu.PrefetchScalarGridSpec(
            num_scalar_prefetch=1,
            grid=(3,),
            in_specs=[lanes] * 4 + [pair] * 2 + [whole(logit.shape)]
            + [pl.BlockSpec(memory_space=pl.ANY)] * 6,
            out_specs=[whole(s) for s in outs],
            scratch_shapes=[
                pltpu.VMEM((LEN, 128), F32),
                pltpu.VMEM((LEN, 128), F32),
                pltpu.VMEM((128, LEN), BF16),
                pltpu.VMEM((3, 3, LEN, 128), BF16),
            ] + [pltpu.VMEM(a.shape, BF16) for a in far] + [pltpu.SemaphoreType.DMA((6,))],
        ),
        out_shape=[jax.ShapeDtypeStruct(s, BF16) for s in outs],
        compiler_params=params(60),
        cost_estimate=cost(16 * 10**9, 10**7, 6 * 10**6),
    )(meta, queries, keys, values, grads, lse, delta, logit, *far)


def cut_pieces(meta, terms, got, packet):
    half = pl.BlockSpec((4, 8, 48, 256), lambda i, m: (0, 0, 0, m[6]))
    return pl.pallas_call(
        piece_kernel,
        grid_spec=pltpu.PrefetchScalarGridSpec(
            num_scalar_prefetch=1,
            grid=(1,),
            in_specs=[half, whole((4, 8, 48, 256)), whole((16, 128))],
            out_specs=whole((16, 208, 128)),
        ),
        out_shape=jax.ShapeDtypeStruct((16, 208, 128), BF16),
        compiler_params=params(60),
        cost_estimate=cost(10**6, 3 * 10**6),
    )(meta, terms.reshape(4, 8, 48, D), got.reshape(4, 8, 48, 256), packet)


def sum_pieces(meta, upper, lower, heads):
    return pl.pallas_call(
        sum_kernel,
        grid_spec=pltpu.PrefetchScalarGridSpec(
            num_scalar_prefetch=1,
            grid=(1,),
            in_specs=[whole(a.shape) for a in (upper, lower, heads)],
            out_specs=whole((8, 176, 128)),
        ),
        out_shape=jax.ShapeDtypeStruct((8, 176, 128), BF16),
        compiler_params=params(60),
        cost_estimate=cost(10**7, 2 * 10**6),
    )(meta, upper, lower, heads)


def total_rows(got):
    outs = ((4, 12, 128), (128, 128))
    return pl.pallas_call(
        final_kernel,
        out_shape=[jax.ShapeDtypeStruct(s, F32) for s in outs],
        compiler_params=pltpu.CompilerParams(vmem_limit_bytes=60 * 2**20),
        cost_estimate=cost(10**6, 10**6),
    )(got)


def join(meta, rows, share, swapped):
    outs = ((12, D), (4, D), (4, DI), (1, D), (1, DI), (2, DI))
    args = (*rows, share, swapped)
    return pl.pallas_call(
        join_kernel,
        grid_spec=pltpu.PrefetchScalarGridSpec(
            num_scalar_prefetch=1,
            grid=(1,),
            in_specs=[whole(a.shape) for a in args],
            out_specs=[whole(s) for s in outs],
        ),
        out_shape=[jax.ShapeDtypeStruct(s, F32) for s in outs],
        compiler_params=params(60),
        cost_estimate=cost(10**5, 10**5),
    )(meta, *args)


def to_samples(event_ids, event_side, me):
    codes = jnp.concatenate([event_ids // 256, event_ids % 256], axis=1).astype(BF16)
    codes = jnp.concatenate([codes[:, None], jnp.zeros((SAMPLES, 15, D), BF16)], axis=1)

    def part(sample):
        sample = jnp.minimum(sample, SAMPLES - 1)
        side = lax.dynamic_index_in_dim(event_side, sample, 0, keepdims=False)
        code = lax.dynamic_index_in_dim(codes, sample, 0, keepdims=False)
        return jnp.concatenate([side, code])

    got = [part(me)]
    for k in (1, 2, 3):
        pairs = [(i, (i + k) % 4) for i in range(4) if (i + k) % 4 < SAMPLES]
        got.append(lax.ppermute(part((me + k) % 4), CTX, pairs))
    return got


def swap_cores(value):
    return lax.ppermute(value, "core", [(0, 1), (1, 0)])


def per_device(
    event_ids, lengths, event_side, dense_input, labels, event_table, seq_gain, w_mix, w_query,
    w_key, w_value, w_out, w_pool, w_cross, b_cross, w_heads,
):
    me = lax.axis_index(CTX)
    core = lax.axis_index("core")
    chip = lax.axis_index(("z", "ylo", "x", "yhi"))
    own = jnp.minimum(me, SAMPLES - 1)
    parts = to_samples(event_ids, event_side, me)
    length = jnp.where(me < SAMPLES, lengths[own], 0)
    plane = lax.axis_index(PLANE)
    meta = [me, length, labels[own, 0], labels[own, 1], chip, lax.axis_index("z"), core, plane]
    meta = jnp.stack(meta).astype(jnp.int32)
    dense = lax.dynamic_slice_in_dim(dense_input, own, 1, 0)
    mix_row = dot(dense, w_mix)
    base = dot(dense, w_cross) + b_cross[None]

    def other_half(terms):
        return swap_cores(lax.dynamic_slice_in_dim(terms, (1 - core) * 256, 256, 1))

    heads = w_heads.T
    (queries, keys, values, grads, mixed, normed, lse, delta, upper, packet, logit) = forward(
        meta,
        (*parts, mix_row, seq_gain[None], base, dense.astype(F32), heads),
        (event_table, w_query, w_key, w_value, w_out, w_pool),
    )
    upper_got = other_half(upper)
    attention = (queries, keys, values, grads, lse, delta)
    one = first_pair_back(meta, *attention)
    upper_got, one = lax.optimization_barrier((upper_got, one))
    pieces = cut_pieces(meta, upper, upper_got, packet)
    pieces, attention = lax.optimization_barrier((pieces, attention))
    upper_plane = lax.all_to_all(pieces, PLANE, 0, 0)
    lower, packet = rest_back(
        meta, *attention, logit, one, mixed, normed, w_query, w_key, w_value
    )
    upper_plane, lower = lax.optimization_barrier((upper_plane, lower))
    lower_got = other_half(lower)
    pieces = cut_pieces(meta, lower, lower_got, packet)
    lower_plane = lax.all_to_all(pieces, PLANE, 0, 0)
    got = lax.all_to_all(sum_pieces(meta, upper_plane, lower_plane, heads), "z", 0, 0)
    rows, share = total_rows(got)
    swapped = swap_cores(share)
    entries = [lax.dynamic_index_in_dim(rows, me, 0, keepdims=False)]
    for k in (1, 2, 3):
        sent = lax.dynamic_index_in_dim(rows, (me + k) % 4, 0, keepdims=False)
        entries.append(lax.ppermute(sent, CTX, [(i, (i + k) % 4) for i in range(4)]))
    sequence, mix, cross, gain, bias, grad_heads = join(meta, entries, share, swapped)
    return (sequence, mix, cross, gain.reshape(D), bias.reshape(DI), grad_heads.T)


def solution(mesh):
    fine = Mesh(mesh.devices.reshape(8, 2, 4, 2, 2), ("z", "ylo", "x", "yhi", "core"))
    dp = ("z", "ylo", "x")
    every = dp + CTX
    in_specs = (P(dp, CTX), P(dp), P(dp, CTX, None), P(dp, None), P(dp, None)) + (P(),) * 11
    out_specs = (P(every, None), P(every, None), P(every, None), P(), P(), P())
    return jax.shard_map(
        per_device, mesh=fine, in_specs=in_specs, out_specs=out_specs, check_vma=False
    )
```

```python
import functools

import jax
import jax.numpy as jnp
from jax import lax
from jax.experimental import pallas as pl
from jax.experimental.pallas import tpu as pltpu
from jax.sharding import Mesh, PartitionSpec as P

HEADS = 8
BATCH = 192
SAMPLES = 3
BLOCK = 256
BLOCKS = 4
LEN = 1024
D = 512
DI = 1024
VOCAB = 2048
MASKED = -1e30
EPSILON = 1e-06
LOSS_SCALE = 32768.0
F32 = jnp.float32
BF16 = jnp.bfloat16
CTX = ("yhi", "core")
PLANE = ("ylo", "x", "yhi")


def dot(a, b):
    return lax.dot_general(a, b, (((1,), (0,)), ((), ())), preferred_element_type=F32)


def dot_nt(a, b):
    return lax.dot_general(a, b, (((1,), (1,)), ((), ())), preferred_element_type=F32)


def dot_tn(a, b):
    return lax.dot_general(a, b, (((0,), (0,)), ((), ())), preferred_element_type=F32)


def both_heads(rows):
    low = lax.broadcasted_iota(jnp.int32, rows.shape, 1) < 64
    zero = jnp.zeros_like(rows)
    return jnp.concatenate([jnp.where(low, rows, zero), jnp.where(low, zero, rows)], axis=0)


def causal(tile):
    key = lax.broadcasted_iota(jnp.int32, tile.shape, 0)
    query = lax.broadcasted_iota(jnp.int32, tile.shape, 1) & (BLOCK - 1)
    return key <= query


def spread(core, block_of, own_ref, other_ref):
    for mine in (0, 1):

        @pl.when(core == mine)
        def _():
            for quarter in range(4):
                target = own_ref if quarter // 2 == mine else other_ref
                lanes = slice(quarter * 128, (quarter + 1) * 128)
                for n in range(4):
                    for a in range(8):
                        start = n * 384 + a * 48
                        target[2 * a + quarter % 2, n * 48 : (n + 1) * 48, :] = block_of(start, lanes)


def forward_kernel(
    meta, part0, part1, part2, part3, mix_ref, gain_ref, base_ref, dense_ref, heads_ref,
    table_far, wq_far, wk_far, wv_far, wo_far, wp_far,
    q_ref, k_ref, v_ref, do_ref, mixed_ref, normed_ref, lse_ref, delta_ref, own_ref, other_ref,
    packet_ref, logit_ref,
    part_ref, q_all, k_all, vt_ref, att_ref, o_ref, res_ref, pre_ref, sum_ref, scaled_ref,
    term_acc, table_ref, wq_ref, wk_ref, wv_ref, wo_ref, wp_ref, sems,
):
    far = (table_far, wq_far, wk_far, wv_far, wo_far, wp_far)
    near = (table_ref, wq_ref, wk_ref, wv_ref, wo_ref, wp_ref)
    copies = [pltpu.make_async_copy(f, n, sems.at[i]) for i, (f, n) in enumerate(zip(far, near))]
    step = pl.program_id(0)
    length = meta[1]

    @pl.when(step == 0)
    def _():
        for copy in copies:
            copy.start()
        sum_ref[...] = jnp.zeros_like(sum_ref)
        term_acc[...] = jnp.zeros_like(term_acc)

    source = lax.rem(meta[0] - jnp.minimum(step, BLOCKS - 1) + BLOCKS, BLOCKS)
    for n, ref in enumerate((part0, part1, part2, part3)):

        @pl.when((step < BLOCKS) & (source == n))
        def _():
            part_ref[...] = ref[...]

    def ahead(c):
        here = slice(c * BLOCK, (c + 1) * BLOCK)
        if c == 0:
            for copy in copies[:4]:
                copy.wait()
        codes = part_ref[BLOCK:, :].astype(F32)
        ids = (codes[:, :BLOCK] * 256.0 + codes[:, BLOCK:]).T[:, 0:1].astype(jnp.int32)
        slots = lax.broadcasted_iota(jnp.int32, (BLOCK, VOCAB), 1)
        picked = jnp.where(slots == ids, 1.0, 0.0).astype(BF16)
        tokens = dot(picked, table_ref[...]) + part_ref[:BLOCK, :].astype(F32)
        mean = jnp.mean(tokens * tokens, axis=1, keepdims=True)
        normed = tokens * lax.rsqrt(mean + EPSILON)
        normed_ref[...] = normed.astype(BF16)
        mixed = (normed * gain_ref[...] + mix_ref[...]).astype(BF16)
        mixed_ref[...] = mixed
        queries = (dot(mixed, wq_ref[...]).astype(BF16).astype(F32) * 0.125).astype(BF16)
        q_ref[...] = queries
        q_all[...] = queries
        keys_now = dot(mixed, wk_ref[...]).astype(BF16)
        k_ref[...] = keys_now
        k_all[here, :] = keys_now
        values = dot(mixed, wv_ref[...]).astype(BF16)
        v_ref[...] = values
        vt_ref[:, here] = values.T
        for p in range(4):
            lanes = slice(p * 128, (p + 1) * 128)
            chosen = both_heads(q_all[:, lanes])
            tiles = []
            for j in range(c + 1):
                tile = dot_nt(k_all[j * BLOCK : (j + 1) * BLOCK, lanes], chosen)
                if j == c:
                    tile = jnp.where(causal(tile), tile, MASKED)
                tiles.append(tile)
            top = functools.reduce(jnp.maximum, [jnp.max(t, axis=0, keepdims=True) for t in tiles])
            raised = [jnp.exp(t - top) for t in tiles]
            total = functools.reduce(jnp.add, [jnp.sum(t, axis=0, keepdims=True) for t in raised])
            inverse = 1.0 / total
            shares = [(t * inverse).astype(BF16) for t in raised]
            lse = top + jnp.log(total)
            lse_ref[p, 0:1, here] = lse[:, :BLOCK]
            lse_ref[p, 1:2, here] = lse[:, BLOCK:]
            first = jnp.zeros((64, BLOCK), F32)
            second = jnp.zeros((64, BLOCK), F32)
            for j in range(c + 1):
                keys = slice(j * BLOCK, (j + 1) * BLOCK)
                first += dot(vt_ref[p * 128 : p * 128 + 64, keys], shares[j][:, :BLOCK])
                second += dot(vt_ref[p * 128 + 64 : p * 128 + 128, keys], shares[j][:, BLOCK:])
            joined = jnp.concatenate([first, second], axis=0).T
            o_ref[here, lanes] = joined
            att_ref[here, lanes] = joined.astype(BF16)
        if c == 0:
            for copy in copies[4:]:
                copy.wait()
        residual = tokens + dot(att_ref[here, :], wo_ref[...])
        half = residual.astype(BF16)
        res_ref[here, :] = half
        pre = dot(half, wp_ref[...])
        pre_ref[here, :] = pre
        valid = (c * BLOCK + lax.broadcasted_iota(jnp.int32, pre.shape, 0)) < length
        silu = jnp.where(valid, pre * jax.nn.sigmoid(pre), 0.0)
        sum_ref[...] += jnp.sum(silu, axis=0, keepdims=True)

    def blank(c):
        if c == 0:
            for copy in copies:
                copy.wait()
        here = slice(c * BLOCK, (c + 1) * BLOCK)
        for ref in (q_ref, k_ref, v_ref, mixed_ref, normed_ref):
            ref[...] = jnp.zeros((BLOCK, D), ref.dtype)
        lse_ref[:, :, here] = jnp.zeros((4, 2, BLOCK), F32)
        delta_ref[:, :, here] = jnp.zeros((4, 2, BLOCK), F32)

    for c in range(BLOCKS):
        pl.when((step == c) & (length > c * BLOCK))(functools.partial(ahead, c))
        pl.when((step == c) & (length <= c * BLOCK))(functools.partial(blank, c))

    @pl.when(step == BLOCKS)
    def _():
        span = jnp.maximum(length, 1).astype(F32)
        dense = dense_ref[...]
        gate = base_ref[...] + sum_ref[...] / span
        crossed = dense + dense * gate
        rows = [dense[:, n * 128 : (n + 1) * 128] for n in range(8)]
        rows += [crossed[:, n * 128 : (n + 1) * 128] for n in range(8)]
        packet_ref[...] = jnp.concatenate(rows, axis=0).astype(BF16)
        a = jnp.sum(crossed * heads_ref[0:1, :], axis=1, keepdims=True)
        c = jnp.sum(crossed * heads_ref[1:2, :], axis=1, keepdims=True)
        clicked = meta[2].astype(F32)
        converted = (meta[2] * meta[3]).astype(F32)
        top = jnp.maximum(jnp.maximum(a, c), 0.0)
        ea, ec = jnp.exp(a - top), jnp.exp(c - top)
        below = jnp.exp(-top) + ea + ec
        grad_a = jax.nn.sigmoid(a) - clicked - converted * jax.nn.sigmoid(-a)
        grad_a = grad_a - (1.0 - converted) * (ea / below - jax.nn.sigmoid(a))
        grad_c = -converted * jax.nn.sigmoid(-c)
        grad_c = grad_c - (1.0 - converted) * (ec / below - jax.nn.sigmoid(c))
        factor = jnp.where(length > 0, LOSS_SCALE / BATCH, 0.0)
        grad_a = grad_a * factor
        grad_c = grad_c * factor
        lane = lax.broadcasted_iota(jnp.int32, (1, 128), 1)
        logit_ref[...] = jnp.where(lane == 0, grad_a, jnp.where(lane == 1, grad_c, 0.0))
        grad_gate = (grad_a * heads_ref[0:1, :] + grad_c * heads_ref[1:2, :]) * dense
        scaled_ref[...] = grad_gate / span

    def back(c):
        here = slice(c * BLOCK, (c + 1) * BLOCK)
        pre = pre_ref[here, :]
        sig = jax.nn.sigmoid(pre)
        valid = (c * BLOCK + lax.broadcasted_iota(jnp.int32, pre.shape, 0)) < length
        slope = sig * (1.0 + pre * (1.0 - sig)) * scaled_ref[...]
        grad_pre = jnp.where(valid, slope, 0.0).astype(BF16)
        term_acc[D:, :] += dot_tn(grad_pre, res_ref[here, :])
        grad_res = dot_nt(grad_pre, wp_ref[...]).astype(BF16)
        term_acc[:D, :] += dot_tn(att_ref[here, :], grad_res)
        grad_att = dot_nt(grad_res, wo_ref[...]).astype(BF16)
        do_ref[...] = grad_att
        product = grad_att.astype(F32) * o_ref[here, :]
        head = lax.broadcasted_iota(jnp.int32, (HEADS, D), 0)
        column = lax.broadcasted_iota(jnp.int32, (HEADS, D), 1) // 64
        picks = jnp.where(head == column, 1.0, 0.0).astype(BF16)
        high = product.astype(BF16)
        low = (product - high.astype(F32)).astype(BF16)
        delta = dot_nt(picks, high) + dot_nt(picks, low)
        for p in range(4):
            delta_ref[p, :, here] = delta[2 * p : 2 * p + 2, :]

    def quiet():
        do_ref[...] = jnp.zeros((BLOCK, D), BF16)

    for c in range(BLOCKS):
        pl.when((step == BLOCKS + c) & (length > c * BLOCK))(functools.partial(back, c))
        pl.when((step == BLOCKS + c) & (length <= c * BLOCK))(quiet)

    @pl.when(step == 2 * BLOCKS - 1)
    def _():
        spread(
            meta[6], lambda row, lanes: term_acc[row : row + 48, lanes].astype(BF16), own_ref, other_ref
        )


def pair_body(
    length, q_ref, k_ref, v_ref, do_ref, lse_ref, delta_ref, dq_ref, dk_ref, dv_ref, dk_acc, dv_acc, kt_ref
):
    dk_acc[...] = jnp.zeros_like(dk_acc)
    dv_acc[...] = jnp.zeros_like(dv_acc)
    kt_ref[...] = k_ref[...].T

    def block(c):
        here = slice(c * BLOCK, (c + 1) * BLOCK)
        chosen = both_heads(q_ref[here, :])
        grads = both_heads(do_ref[here, :])
        lse = jnp.concatenate([lse_ref[0, 0:1, here], lse_ref[0, 1:2, here]], axis=1)
        delta = jnp.concatenate([delta_ref[0, 0:1, here], delta_ref[0, 1:2, here]], axis=1)
        first = jnp.zeros((64, BLOCK), F32)
        second = jnp.zeros((64, BLOCK), F32)
        for j in range(c + 1):
            keys = slice(j * BLOCK, (j + 1) * BLOCK)
            shares = jnp.exp(dot_nt(k_ref[keys, :], chosen) - lse)
            if j == c:
                shares = jnp.where(causal(shares), shares, 0.0)
            grad_shares = dot_nt(v_ref[keys, :], grads)
            grad_scores = (shares * (grad_shares - delta)).astype(BF16)
            dv_acc[keys, :] += dot(shares.astype(BF16), grads)
            dk_acc[keys, :] += dot(grad_scores, chosen)
            first += dot(kt_ref[0:64, keys], grad_scores[:, :BLOCK])
            second += dot(kt_ref[64:128, keys], grad_scores[:, BLOCK:])
        joined = jnp.concatenate([first, second], axis=0) * 0.125
        dq_ref[here, :] = joined.T.astype(BF16)

    def blank(c):
        here = slice(c * BLOCK, (c + 1) * BLOCK)
        dq_ref[here, :] = jnp.zeros((BLOCK, 128), BF16)

    for c in range(BLOCKS):
        pl.when(length > c * BLOCK)(functools.partial(block, c))
        pl.when(length <= c * BLOCK)(functools.partial(blank, c))
    dk_ref[...] = dk_acc[...].astype(BF16)
    dv_ref[...] = dv_acc[...].astype(BF16)


def pair_kernel(
    meta, q_ref, k_ref, v_ref, do_ref, lse_ref, delta_ref, grad_ref, dk_acc, dv_acc, kt_ref
):
    pair_body(
        meta[1], q_ref, k_ref, v_ref, do_ref, lse_ref, delta_ref,
        grad_ref.at[0], grad_ref.at[1], grad_ref.at[2], dk_acc, dv_acc, kt_ref,
    )


def rest_kernel(
    meta, q_ref, k_ref, v_ref, do_ref, lse_ref, delta_ref, logit_ref,
    one_far, mixed_far, normed_far, wq_far, wk_far, wv_far,
    own_ref, other_ref, packet_ref,
    dk_acc, dv_acc, kt_ref, term_ref, grad_ref, one_ref, mixed_ref, normed_ref, wq_ref, wk_ref, wv_ref, sems,
):
    step = pl.program_id(0)
    far = (one_far, mixed_far, normed_far, wq_far, wk_far, wv_far)
    near = (one_ref, mixed_ref, normed_ref, wq_ref, wk_ref, wv_ref)
    copies = [pltpu.make_async_copy(f, n, sems.at[i]) for i, (f, n) in enumerate(zip(far, near))]

    @pl.when(step == 0)
    def _():
        for copy in copies:
            copy.start()

    pair_body(
        meta[1], q_ref, k_ref, v_ref, do_ref, lse_ref, delta_ref,
        grad_ref.at[0, step], grad_ref.at[1, step], grad_ref.at[2, step], dk_acc, dv_acc, kt_ref,
    )

    @pl.when(step == 2)
    def _():
        for copy in copies:
            copy.wait()
        turned = mixed_ref[...].T
        total = None
        for n, weight in enumerate((wq_ref, wk_ref, wv_ref)):
            rows = jnp.concatenate([one_ref[n]] + [grad_ref[n, p] for p in range(3)], axis=1)
            term_ref[n * D : (n + 1) * D, :] = dot(turned, rows).astype(BF16)
            part = dot_nt(rows, weight[...])
            total = part if total is None else total + part
        spread(meta[6], lambda row, lanes: term_ref[row : row + 48, lanes], own_ref, other_ref)
        mix = jnp.sum(total, axis=0, keepdims=True)
        gain = jnp.sum(total * normed_ref[...].astype(F32), axis=0, keepdims=True)
        logit = logit_ref[...]
        high = logit.astype(BF16).astype(F32)
        lines = [mix[:, n * 128 : (n + 1) * 128] for n in range(4)]
        lines += [gain[:, n * 128 : (n + 1) * 128] for n in range(4)]
        lines += [high, logit - high, jnp.zeros((6, 128), F32)]
        packet_ref[...] = jnp.concatenate(lines, axis=0).astype(BF16)


def piece_kernel(own_ref, got_ref, packet_ref, piece_ref):
    for g in range(16):
        total = own_ref[g].astype(F32) + got_ref[g].astype(F32)
        piece_ref[g, :192, :] = total.astype(BF16)
        piece_ref[g, 192:, :] = packet_ref[...]


def exact_dot(a, b):
    return lax.dot_general(
        a, b, (((1,), (0,)), ((), ())),
        precision=lax.Precision.HIGHEST, preferred_element_type=F32,
    )


def sum_kernel(meta, upper_ref, lower_ref, heads_ref, piece_ref):
    upper_packets = [upper_ref[g, 192:, :].astype(F32) for g in range(16)]
    lower_packets = [lower_ref[g, 192:, :].astype(F32) for g in range(16)]

    def pick(packets, row):
        return jnp.concatenate([p[row : row + 1, :] for p in packets], axis=0)

    upper = functools.reduce(jnp.add, [upper_ref[g, :192, :].astype(F32) for g in range(16)])
    lower = functools.reduce(jnp.add, [lower_ref[g, :192, :].astype(F32) for g in range(16)])
    for n in range(4):
        piece_ref[n, :48, :] = lower[n * 48 : (n + 1) * 48].astype(BF16)
        piece_ref[4 + n, :48, :] = upper[n * 48 : (n + 1) * 48].astype(BF16)
    logits = pick(lower_packets, 8) + pick(lower_packets, 9)
    grad_a, grad_c = logits[:, 0:1], logits[:, 1:2]
    lane = lax.broadcasted_iota(jnp.int32, (8, 128), 1)
    line = lax.broadcasted_iota(jnp.int32, (8, 128), 0)
    picks = jnp.where(lane == meta[7] * 8 + line, 1.0, 0.0).astype(BF16)
    dense = [pick(upper_packets, r) for r in range(8)]
    columns = jnp.concatenate([dot_nt(picks, d.astype(BF16)) for d in dense], axis=0)
    flat = [jnp.sum(pick(lower_packets, 4 + r), axis=0, keepdims=True) for r in range(4)]
    gates = []
    for r in range(8):
        lanes = slice(r * 128, (r + 1) * 128)
        gate = (grad_a * heads_ref[0:1, lanes] + grad_c * heads_ref[1:2, lanes]) * dense[r]
        gates.append(gate)
        flat.append(jnp.sum(gate, axis=0, keepdims=True))
    crossed = [pick(upper_packets, 8 + r) for r in range(8)]
    flat += [jnp.sum(d * grad_a, axis=0, keepdims=True) for d in crossed]
    flat += [jnp.sum(d * grad_c, axis=0, keepdims=True) for d in crossed]
    flat = jnp.concatenate(flat + [jnp.zeros((4, 128), F32)], axis=0).astype(BF16)
    products = [exact_dot(columns, gate) for gate in gates]
    products += [exact_dot(columns, pick(lower_packets, r)) for r in range(4)]
    for z in range(8):
        rows = jnp.concatenate([p[z * 8 : (z + 1) * 8, :] for p in products], axis=0)
        piece_ref[z, 48:144, :] = rows.astype(BF16)
        piece_ref[z, 144:176, :] = flat


def final_kernel(meta, got_ref, row0, row1, row2, row3, share_ref):
    total = functools.reduce(jnp.add, [got_ref[z].astype(F32) for z in range(8)])
    for n in range(4):
        for k, ref in enumerate((row0, row1, row2, row3)):

            @pl.when(lax.rem(meta[0] + k, 4) == n)
            def _():
                ref[...] = total[n * 12 : (n + 1) * 12, :]

    share_ref[...] = total[48:176, :]


def join_kernel(meta, row0, row1, row2, row3, share_ref, swapped_ref, sequence_ref, mix_ref, cross_ref, gain_ref, bias_ref, heads_ref):
    for source, place in ((0, 0), (2, 1), (1, 2), (3, 3)):
        entry = lax.rem(meta[0] - source + 4, 4)
        for n, ref in enumerate((row0, row1, row2, row3)):

            @pl.when(entry == n)
            def _():
                sequence_ref[:, place * 128 : (place + 1) * 128] = ref[...]

    total = share_ref[...] + swapped_ref[...]
    upper = meta[6] == 1
    for r in range(12):
        mine = jnp.where(upper, total[r * 8 + 4 : r * 8 + 8, :], total[r * 8 : r * 8 + 4, :])
        if r < 8:
            cross_ref[:, r * 128 : (r + 1) * 128] = mine
        else:
            mix_ref[:, (r - 8) * 128 : (r - 7) * 128] = mine
    for r in range(4):
        gain_ref[:, r * 128 : (r + 1) * 128] = total[96 + r : 97 + r, :]
    for r in range(8):
        lanes = slice(r * 128, (r + 1) * 128)
        bias_ref[:, lanes] = total[100 + r : 101 + r, :]
        heads_ref[0:1, lanes] = total[108 + r : 109 + r, :]
        heads_ref[1:2, lanes] = total[116 + r : 117 + r, :]


def whole(shape):
    return pl.BlockSpec(shape, lambda i, m: (0,) * len(shape))


def params(megabytes):
    return pltpu.CompilerParams(
        dimension_semantics=("arbitrary",), vmem_limit_bytes=megabytes * 2**20
    )


def cost(flops, moved, exps=0):
    return pl.CostEstimate(flops=flops, bytes_accessed=moved, transcendentals=exps)


def forward(meta, small, large):
    early = pl.BlockSpec((BLOCK, D), lambda i, m: (jnp.minimum(i, BLOCKS - 1), 0))
    late = pl.BlockSpec((BLOCK, D), lambda i, m: (jnp.maximum(i - BLOCKS, 0), 0))
    outs = [((LEN, D), BF16)] * 6 + [
        ((4, 2, LEN), F32), ((4, 2, LEN), F32), ((16, 192, 128), BF16), ((16, 192, 128), BF16),
        ((16, 128), BF16),
        ((1, 128), F32),
    ]
    return pl.pallas_call(
        forward_kernel,
        grid_spec=pltpu.PrefetchScalarGridSpec(
            num_scalar_prefetch=1,
            grid=(2 * BLOCKS,),
            in_specs=[whole(a.shape) for a in small] + [pl.BlockSpec(memory_space=pl.ANY)] * 6,
            out_specs=[early] * 3 + [late] + [early] * 2 + [whole(s) for s, _ in outs[6:]],
            scratch_shapes=[
                pltpu.VMEM((BLOCK + 16, D), BF16),
                pltpu.VMEM((BLOCK, D), BF16),
                pltpu.VMEM((LEN, D), BF16),
                pltpu.VMEM((D, LEN), BF16),
                pltpu.VMEM((LEN, D), BF16),
                pltpu.VMEM((LEN, D), F32),
                pltpu.VMEM((LEN, D), BF16),
                pltpu.VMEM((LEN, DI), F32),
                pltpu.VMEM((1, DI), F32),
                pltpu.VMEM((1, DI), F32),
                pltpu.VMEM((3 * D, D), F32),
            ] + [pltpu.VMEM(a.shape, BF16) for a in large] + [pltpu.SemaphoreType.DMA((6,))],
        ),
        out_shape=[jax.ShapeDtypeStruct(s, t) for s, t in outs],
        compiler_params=params(58),
        cost_estimate=cost(10**10, 2 * 10**7, 10**7),
    )(meta, *small, *large)


def first_pair_back(meta, queries, keys, values, grads, lse, delta):
    lanes = pl.BlockSpec((LEN, 128), lambda i, m: (0, i))
    pair = pl.BlockSpec((1, 2, LEN), lambda i, m: (i, 0, 0))
    return pl.pallas_call(
        pair_kernel,
        grid_spec=pltpu.PrefetchScalarGridSpec(
            num_scalar_prefetch=1,
            grid=(1,),
            in_specs=[lanes] * 4 + [pair] * 2,
            out_specs=whole((3, LEN, 128)),
            scratch_shapes=[
                pltpu.VMEM((LEN, 128), F32),
                pltpu.VMEM((LEN, 128), F32),
                pltpu.VMEM((128, LEN), BF16),
            ],
        ),
        out_shape=jax.ShapeDtypeStruct((3, LEN, 128), BF16),
        compiler_params=params(60),
        cost_estimate=cost(4 * 10**9, 2 * 10**6, 2 * 10**6),
    )(meta, queries, keys, values, grads, lse, delta)


def rest_back(meta, queries, keys, values, grads, lse, delta, logit, *far):
    lanes = pl.BlockSpec((LEN, 128), lambda i, m: (0, 1 + i))
    pair = pl.BlockSpec((1, 2, LEN), lambda i, m: (1 + i, 0, 0))
    outs = ((16, 192, 128), (16, 192, 128), (16, 128))
    return pl.pallas_call(
        rest_kernel,
        grid_spec=pltpu.PrefetchScalarGridSpec(
            num_scalar_prefetch=1,
            grid=(3,),
            in_specs=[lanes] * 4 + [pair] * 2 + [whole(logit.shape)]
            + [pl.BlockSpec(memory_space=pl.ANY)] * 6,
            out_specs=[whole(s) for s in outs],
            scratch_shapes=[
                pltpu.VMEM((LEN, 128), F32),
                pltpu.VMEM((LEN, 128), F32),
                pltpu.VMEM((128, LEN), BF16),
                pltpu.VMEM((3 * D, D), BF16),
                pltpu.VMEM((3, 3, LEN, 128), BF16),
            ] + [pltpu.VMEM(a.shape, BF16) for a in far] + [pltpu.SemaphoreType.DMA((6,))],
        ),
        out_shape=[jax.ShapeDtypeStruct(s, BF16) for s in outs],
        compiler_params=params(60),
        cost_estimate=cost(16 * 10**9, 10**7, 6 * 10**6),
    )(meta, queries, keys, values, grads, lse, delta, logit, *far)


def cut_pieces(own, got, packet):
    return pl.pallas_call(
        piece_kernel,
        out_shape=jax.ShapeDtypeStruct((16, 208, 128), BF16),
        compiler_params=pltpu.CompilerParams(vmem_limit_bytes=16 * 2**20),
        cost_estimate=cost(10**6, 3 * 10**6),
    )(own, got, packet)


def sum_pieces(meta, upper, lower, heads):
    return pl.pallas_call(
        sum_kernel,
        grid_spec=pltpu.PrefetchScalarGridSpec(
            num_scalar_prefetch=1,
            grid=(1,),
            in_specs=[whole(a.shape) for a in (upper, lower, heads)],
            out_specs=whole((8, 176, 128)),
        ),
        out_shape=jax.ShapeDtypeStruct((8, 176, 128), BF16),
        compiler_params=params(16),
        cost_estimate=cost(10**7, 2 * 10**6),
    )(meta, upper, lower, heads)


def total_rows(meta, got):
    outs = ((12, 128),) * 4 + ((128, 128),)
    return pl.pallas_call(
        final_kernel,
        grid_spec=pltpu.PrefetchScalarGridSpec(
            num_scalar_prefetch=1,
            grid=(1,),
            in_specs=[whole(got.shape)],
            out_specs=[whole(s) for s in outs],
        ),
        out_shape=[jax.ShapeDtypeStruct(s, F32) for s in outs],
        compiler_params=params(16),
        cost_estimate=cost(10**6, 10**6),
    )(meta, got)


def join(meta, rows, share, swapped):
    outs = ((12, D), (4, D), (4, DI), (1, D), (1, DI), (2, DI))
    args = (*rows, share, swapped)
    return pl.pallas_call(
        join_kernel,
        grid_spec=pltpu.PrefetchScalarGridSpec(
            num_scalar_prefetch=1,
            grid=(1,),
            in_specs=[whole(a.shape) for a in args],
            out_specs=[whole(s) for s in outs],
        ),
        out_shape=[jax.ShapeDtypeStruct(s, F32) for s in outs],
        compiler_params=params(16),
        cost_estimate=cost(10**5, 10**5),
    )(meta, *args)


def to_samples(event_ids, event_side, me):
    codes = jnp.concatenate([event_ids // 256, event_ids % 256], axis=1).astype(BF16)
    codes = jnp.concatenate([codes[:, None], jnp.zeros((SAMPLES, 15, D), BF16)], axis=1)

    def part(sample):
        sample = jnp.minimum(sample, SAMPLES - 1)
        side = lax.dynamic_index_in_dim(event_side, sample, 0, keepdims=False)
        code = lax.dynamic_index_in_dim(codes, sample, 0, keepdims=False)
        return jnp.concatenate([side, code])

    got = [part(me)]
    for k in (1, 2, 3):
        pairs = [(i, (i + k) % 4) for i in range(4) if (i + k) % 4 < SAMPLES]
        got.append(lax.ppermute(part((me + k) % 4), CTX, pairs))
    return got


def swap_cores(value):
    return lax.ppermute(value, "core", [(0, 1), (1, 0)])


def per_device(
    event_ids, lengths, event_side, dense_input, labels, event_table, seq_gain, w_mix, w_query,
    w_key, w_value, w_out, w_pool, w_cross, b_cross, w_heads,
):
    me = lax.axis_index(CTX)
    core = lax.axis_index("core")
    chip = lax.axis_index(("z", "ylo", "x", "yhi"))
    own = jnp.minimum(me, SAMPLES - 1)
    parts = to_samples(event_ids, event_side, me)
    length = jnp.where(me < SAMPLES, lengths[own], 0)
    plane = lax.axis_index(PLANE)
    meta = [me, length, labels[own, 0], labels[own, 1], chip, lax.axis_index("z"), core, plane]
    meta = jnp.stack(meta).astype(jnp.int32)
    dense = lax.dynamic_slice_in_dim(dense_input, own, 1, 0)
    mix_row = dot(dense, w_mix)
    base = dot(dense, w_cross) + b_cross[None]

    heads = w_heads.T
    (queries, keys, values, grads, mixed, normed, lse, delta, own, other, packet, logit) = forward(
        meta,
        (*parts, mix_row, seq_gain[None], base, dense.astype(F32), heads),
        (event_table, w_query, w_key, w_value, w_out, w_pool),
    )
    upper_got = swap_cores(other)
    attention = (queries, keys, values, grads, lse, delta)
    one = first_pair_back(meta, *attention)
    upper_got, one = lax.optimization_barrier((upper_got, one))
    pieces = cut_pieces(own, upper_got, packet)
    pieces, attention = lax.optimization_barrier((pieces, attention))
    upper_plane = lax.all_to_all(pieces, PLANE, 0, 0)
    own, other, packet = rest_back(
        meta, *attention, logit, one, mixed, normed, w_query, w_key, w_value
    )
    upper_plane, other = lax.optimization_barrier((upper_plane, other))
    lower_got = swap_cores(other)
    pieces = cut_pieces(own, lower_got, packet)
    lower_plane = lax.all_to_all(pieces, PLANE, 0, 0)
    got = lax.all_to_all(sum_pieces(meta, upper_plane, lower_plane, heads), "z", 0, 0)
    *rows, share = total_rows(meta, got)
    entries = rows[:1]
    for k in (1, 2, 3):
        entries.append(lax.ppermute(rows[k], CTX, [(i, (i + k) % 4) for i in range(4)]))
    swapped = swap_cores(share)
    sequence, mix, cross, gain, bias, grad_heads = join(meta, entries, share, swapped)
    return (sequence, mix, cross, gain.reshape(D), bias.reshape(DI), grad_heads.T)


def solution(mesh):
    fine = Mesh(mesh.devices.reshape(8, 2, 4, 2, 2), ("z", "ylo", "x", "yhi", "core"))
    dp = ("z", "ylo", "x")
    every = dp + CTX
    in_specs = (P(dp, CTX), P(dp), P(dp, CTX, None), P(dp, None), P(dp, None)) + (P(),) * 11
    out_specs = (P(every, None), P(every, None), P(every, None), P(), P(), P())
    return jax.shard_map(
        per_device, mesh=fine, in_specs=in_specs, out_specs=out_specs, check_vma=False
    )
```

```python
import functools

import jax
import jax.numpy as jnp
from jax import lax
from jax.experimental import pallas as pl
from jax.experimental.pallas import tpu as pltpu
from jax.sharding import Mesh, PartitionSpec as P

HEADS = 8
BATCH = 192
SAMPLES = 3
BLOCK = 256
BLOCKS = 4
LEN = 1024
D = 512
DI = 1024
VOCAB = 2048
MASKED = -1e30
EPSILON = 1e-06
LOSS_SCALE = 32768.0
F32 = jnp.float32
BF16 = jnp.bfloat16
CTX = ("yhi", "core")
PLANE = ("ylo", "x", "yhi")


def dot(a, b):
    return lax.dot_general(a, b, (((1,), (0,)), ((), ())), preferred_element_type=F32)


def dot_nt(a, b):
    return lax.dot_general(a, b, (((1,), (1,)), ((), ())), preferred_element_type=F32)


def dot_tn(a, b):
    return lax.dot_general(a, b, (((0,), (0,)), ((), ())), preferred_element_type=F32)


def both_heads(rows):
    low = lax.broadcasted_iota(jnp.int32, rows.shape, 1) < 64
    zero = jnp.zeros_like(rows)
    return jnp.concatenate([jnp.where(low, rows, zero), jnp.where(low, zero, rows)], axis=0)


def causal(tile):
    key = lax.broadcasted_iota(jnp.int32, tile.shape, 0)
    query = lax.broadcasted_iota(jnp.int32, tile.shape, 1) & (BLOCK - 1)
    return key <= query


def spread(core, acc_ref, own_ref, other_ref):
    for mine in (0, 1):

        @pl.when(core == mine)
        def _():
            for block in range(acc_ref.shape[1] // 128):
                target = own_ref if block % 2 == mine else other_ref
                lanes = slice(block * 128, (block + 1) * 128)
                place = slice(block // 2 * 96, (block // 2 + 1) * 96)
                for g in range(16):
                    rows = [acc_ref[n * 384 + g * 24 : n * 384 + (g + 1) * 24, lanes] for n in range(4)]
                    target[g, place, :] = jnp.concatenate(rows, axis=0).astype(BF16)


def forward_kernel(
    meta, part0, part1, part2, part3, mix_ref, gain_ref, base_ref, dense_ref, heads_ref,
    table_far, wq_far, wk_far, wv_far, wo_far, wp_far,
    q_ref, k_ref, v_ref, do_ref, mixed_ref, normed_ref, lse_ref, delta_ref, own_ref, other_ref,
    packet_ref, logit_ref,
    part_ref, q_all, k_all, vt_ref, att_ref, o_ref, res_ref, pre_ref, sum_ref, scaled_ref,
    term_acc, table_ref, wq_ref, wk_ref, wv_ref, wo_ref, wp_ref, sems,
):
    far = (table_far, wq_far, wk_far, wv_far, wo_far, wp_far)
    near = (table_ref, wq_ref, wk_ref, wv_ref, wo_ref, wp_ref)
    copies = [pltpu.make_async_copy(f, n, sems.at[i]) for i, (f, n) in enumerate(zip(far, near))]
    step = pl.program_id(0)
    length = meta[1]

    @pl.when(step == 0)
    def _():
        for copy in copies:
            copy.start()
        sum_ref[...] = jnp.zeros_like(sum_ref)
        term_acc[...] = jnp.zeros_like(term_acc)

    source = lax.rem(meta[0] - jnp.minimum(step, BLOCKS - 1) + BLOCKS, BLOCKS)
    for n, ref in enumerate((part0, part1, part2, part3)):

        @pl.when((step < BLOCKS) & (source == n))
        def _():
            part_ref[...] = ref[...]

    def ahead(c):
        here = slice(c * BLOCK, (c + 1) * BLOCK)
        if c == 0:
            for copy in copies[:4]:
                copy.wait()
        codes = part_ref[BLOCK:, :].astype(F32)
        ids = (codes[:, :BLOCK] * 256.0 + codes[:, BLOCK:]).T[:, 0:1].astype(jnp.int32)
        slots = lax.broadcasted_iota(jnp.int32, (BLOCK, VOCAB), 1)
        picked = jnp.where(slots == ids, 1.0, 0.0).astype(BF16)
        tokens = dot(picked, table_ref[...]) + part_ref[:BLOCK, :].astype(F32)
        mean = jnp.mean(tokens * tokens, axis=1, keepdims=True)
        normed = tokens * lax.rsqrt(mean + EPSILON)
        normed_ref[...] = normed.astype(BF16)
        mixed = (normed * gain_ref[...] + mix_ref[...]).astype(BF16)
        mixed_ref[...] = mixed
        queries = (dot(mixed, wq_ref[...]).astype(BF16).astype(F32) * 0.125).astype(BF16)
        q_ref[...] = queries
        q_all[...] = queries
        keys_now = dot(mixed, wk_ref[...]).astype(BF16)
        k_ref[...] = keys_now
        k_all[here, :] = keys_now
        values = dot(mixed, wv_ref[...]).astype(BF16)
        v_ref[...] = values
        vt_ref[:, here] = values.T
        for p in range(4):
            lanes = slice(p * 128, (p + 1) * 128)
            chosen = both_heads(q_all[:, lanes])
            tiles = []
            for j in range(c + 1):
                tile = dot_nt(k_all[j * BLOCK : (j + 1) * BLOCK, lanes], chosen)
                if j == c:
                    tile = jnp.where(causal(tile), tile, MASKED)
                tiles.append(tile)
            top = functools.reduce(jnp.maximum, [jnp.max(t, axis=0, keepdims=True) for t in tiles])
            raised = [jnp.exp(t - top) for t in tiles]
            total = functools.reduce(jnp.add, [jnp.sum(t, axis=0, keepdims=True) for t in raised])
            inverse = 1.0 / total
            shares = [(t * inverse).astype(BF16) for t in raised]
            lse = top + jnp.log(total)
            lse_ref[p, 0:1, here] = lse[:, :BLOCK]
            lse_ref[p, 1:2, here] = lse[:, BLOCK:]
            first = jnp.zeros((64, BLOCK), F32)
            second = jnp.zeros((64, BLOCK), F32)
            for j in range(c + 1):
                keys = slice(j * BLOCK, (j + 1) * BLOCK)
                first += dot(vt_ref[p * 128 : p * 128 + 64, keys], shares[j][:, :BLOCK])
                second += dot(vt_ref[p * 128 + 64 : p * 128 + 128, keys], shares[j][:, BLOCK:])
            joined = jnp.concatenate([first, second], axis=0).T
            o_ref[here, lanes] = joined
            att_ref[here, lanes] = joined.astype(BF16)
        if c == 0:
            for copy in copies[4:]:
                copy.wait()
        residual = tokens + dot(att_ref[here, :], wo_ref[...])
        half = residual.astype(BF16)
        res_ref[here, :] = half
        pre = dot(half, wp_ref[...])
        pre_ref[here, :] = pre
        valid = (c * BLOCK + lax.broadcasted_iota(jnp.int32, pre.shape, 0)) < length
        silu = jnp.where(valid, pre * jax.nn.sigmoid(pre), 0.0)
        sum_ref[...] += jnp.sum(silu, axis=0, keepdims=True)

    def blank(c):
        if c == 0:
            for copy in copies:
                copy.wait()
        here = slice(c * BLOCK, (c + 1) * BLOCK)
        for ref in (q_ref, k_ref, v_ref, mixed_ref, normed_ref):
            ref[...] = jnp.zeros((BLOCK, D), ref.dtype)
        lse_ref[:, :, here] = jnp.zeros((4, 2, BLOCK), F32)
        delta_ref[:, :, here] = jnp.zeros((4, 2, BLOCK), F32)

    for c in range(BLOCKS):
        pl.when((step == c) & (length > c * BLOCK))(functools.partial(ahead, c))
        pl.when((step == c) & (length <= c * BLOCK))(functools.partial(blank, c))

    @pl.when(step == BLOCKS)
    def _():
        span = jnp.maximum(length, 1).astype(F32)
        dense = dense_ref[...]
        gate = base_ref[...] + sum_ref[...] / span
        crossed = dense + dense * gate
        rows = [dense[:, n * 128 : (n + 1) * 128] for n in range(8)]
        rows += [crossed[:, n * 128 : (n + 1) * 128] for n in range(8)]
        packet_ref[...] = jnp.concatenate(rows, axis=0).astype(BF16)
        a = jnp.sum(crossed * heads_ref[0:1, :], axis=1, keepdims=True)
        c = jnp.sum(crossed * heads_ref[1:2, :], axis=1, keepdims=True)
        clicked = meta[2].astype(F32)
        converted = (meta[2] * meta[3]).astype(F32)
        top = jnp.maximum(jnp.maximum(a, c), 0.0)
        ea, ec = jnp.exp(a - top), jnp.exp(c - top)
        below = jnp.exp(-top) + ea + ec
        grad_a = jax.nn.sigmoid(a) - clicked - converted * jax.nn.sigmoid(-a)
        grad_a = grad_a - (1.0 - converted) * (ea / below - jax.nn.sigmoid(a))
        grad_c = -converted * jax.nn.sigmoid(-c)
        grad_c = grad_c - (1.0 - converted) * (ec / below - jax.nn.sigmoid(c))
        factor = jnp.where(length > 0, LOSS_SCALE / BATCH, 0.0)
        grad_a = grad_a * factor
        grad_c = grad_c * factor
        lane = lax.broadcasted_iota(jnp.int32, (1, 128), 1)
        logit_ref[...] = jnp.where(lane == 0, grad_a, jnp.where(lane == 1, grad_c, 0.0))
        grad_gate = (grad_a * heads_ref[0:1, :] + grad_c * heads_ref[1:2, :]) * dense
        scaled_ref[...] = grad_gate / span

    def back(c):
        here = slice(c * BLOCK, (c + 1) * BLOCK)
        pre = pre_ref[here, :]
        sig = jax.nn.sigmoid(pre)
        valid = (c * BLOCK + lax.broadcasted_iota(jnp.int32, pre.shape, 0)) < length
        slope = sig * (1.0 + pre * (1.0 - sig)) * scaled_ref[...]
        grad_pre = jnp.where(valid, slope, 0.0).astype(BF16)
        term_acc[D:, :] += dot_tn(grad_pre, res_ref[here, :])
        grad_res = dot_nt(grad_pre, wp_ref[...]).astype(BF16)
        term_acc[:D, :] += dot_tn(att_ref[here, :], grad_res)
        grad_att = dot_nt(grad_res, wo_ref[...]).astype(BF16)
        do_ref[...] = grad_att
        product = grad_att.astype(F32) * o_ref[here, :]
        head = lax.broadcasted_iota(jnp.int32, (HEADS, D), 0)
        column = lax.broadcasted_iota(jnp.int32, (HEADS, D), 1) // 64
        picks = jnp.where(head == column, 1.0, 0.0).astype(BF16)
        high = product.astype(BF16)
        low = (product - high.astype(F32)).astype(BF16)
        delta = dot_nt(picks, high) + dot_nt(picks, low)
        for p in range(4):
            delta_ref[p, :, here] = delta[2 * p : 2 * p + 2, :]

    def quiet():
        do_ref[...] = jnp.zeros((BLOCK, D), BF16)

    for c in range(BLOCKS):
        pl.when((step == BLOCKS + c) & (length > c * BLOCK))(functools.partial(back, c))
        pl.when((step == BLOCKS + c) & (length <= c * BLOCK))(quiet)

    @pl.when(step == 2 * BLOCKS - 1)
    def _():
        spread(meta[6], term_acc, own_ref, other_ref)


def pair_body(
    length, q_ref, k_ref, v_ref, do_ref, lse_ref, delta_ref, dq_ref, dk_ref, dv_ref, dk_acc, dv_acc, kt_ref
):
    dk_acc[...] = jnp.zeros_like(dk_acc)
    dv_acc[...] = jnp.zeros_like(dv_acc)
    kt_ref[...] = k_ref[...].T

    def block(c):
        here = slice(c * BLOCK, (c + 1) * BLOCK)
        chosen = both_heads(q_ref[here, :])
        grads = both_heads(do_ref[here, :])
        lse = jnp.concatenate([lse_ref[0, 0:1, here], lse_ref[0, 1:2, here]], axis=1)
        delta = jnp.concatenate([delta_ref[0, 0:1, here], delta_ref[0, 1:2, here]], axis=1)
        first = jnp.zeros((64, BLOCK), F32)
        second = jnp.zeros((64, BLOCK), F32)
        for j in range(c + 1):
            keys = slice(j * BLOCK, (j + 1) * BLOCK)
            shares = jnp.exp(dot_nt(k_ref[keys, :], chosen) - lse)
            if j == c:
                shares = jnp.where(causal(shares), shares, 0.0)
            grad_shares = dot_nt(v_ref[keys, :], grads)
            grad_scores = (shares * (grad_shares - delta)).astype(BF16)
            dv_acc[keys, :] += dot(shares.astype(BF16), grads)
            dk_acc[keys, :] += dot(grad_scores, chosen)
            first += dot(kt_ref[0:64, keys], grad_scores[:, :BLOCK])
            second += dot(kt_ref[64:128, keys], grad_scores[:, BLOCK:])
        joined = jnp.concatenate([first, second], axis=0) * 0.125
        dq_ref[here, :] = joined.T.astype(BF16)

    def blank(c):
        here = slice(c * BLOCK, (c + 1) * BLOCK)
        dq_ref[here, :] = jnp.zeros((BLOCK, 128), BF16)

    for c in range(BLOCKS):
        pl.when(length > c * BLOCK)(functools.partial(block, c))
        pl.when(length <= c * BLOCK)(functools.partial(blank, c))
    dk_ref[...] = dk_acc[...].astype(BF16)
    dv_ref[...] = dv_acc[...].astype(BF16)


def pairs_kernel(
    first,
    meta, q_ref, k_ref, v_ref, do_ref, lse_ref, delta_ref, logit_ref, prior_ref,
    mixed_far, normed_far, wq_far, wk_far, wv_far,
    own_ref, other_ref, sums_ref, packet_ref,
    dk_acc, dv_acc, kt_ref, term_ref, grad_ref, mixed_ref, normed_ref, wq_ref, wk_ref, wv_ref, sems,
):
    step = pl.program_id(0)
    columns = pl.ds(first * 128, 256)
    far = (mixed_far, normed_far) + tuple(w.at[:, columns] for w in (wq_far, wk_far, wv_far))
    near = (mixed_ref, normed_ref, wq_ref, wk_ref, wv_ref)
    copies = [pltpu.make_async_copy(f, n, sems.at[i]) for i, (f, n) in enumerate(zip(far, near))]

    @pl.when(step == 0)
    def _():
        for copy in copies:
            copy.start()

    pair_body(
        meta[1], q_ref, k_ref, v_ref, do_ref, lse_ref, delta_ref,
        grad_ref.at[0, step], grad_ref.at[1, step], grad_ref.at[2, step], dk_acc, dv_acc, kt_ref,
    )

    @pl.when(step == 1)
    def _():
        for copy in copies:
            copy.wait()
        turned = mixed_ref[...].T
        total = None
        for n, weight in enumerate((wq_ref, wk_ref, wv_ref)):
            rows = jnp.concatenate([grad_ref[n, 0], grad_ref[n, 1]], axis=1)
            term_ref[n * D : (n + 1) * D, :] = dot(turned, rows)
            part = dot_nt(rows, weight[...])
            total = part if total is None else total + part
        spread(meta[6], term_ref, own_ref, other_ref)
        mix = jnp.sum(total, axis=0, keepdims=True) + prior_ref[0:1, :]
        gain = jnp.sum(total * normed_ref[...].astype(F32), axis=0, keepdims=True) + prior_ref[1:2, :]
        sums_ref[...] = jnp.concatenate([mix, gain], axis=0)
        logit = logit_ref[...]
        high = logit.astype(BF16).astype(F32)
        lines = [mix[:, n * 128 : (n + 1) * 128] for n in range(4)]
        lines += [gain[:, n * 128 : (n + 1) * 128] for n in range(4)]
        lines += [high, logit - high, jnp.zeros((6, 128), F32)]
        packet_ref[...] = jnp.concatenate(lines, axis=0).astype(BF16)


def piece_kernel(packet_ref, *refs):
    *halves, piece_ref = refs
    for g in range(16):
        start = 0
        for own_ref, got_ref in zip(halves[::2], halves[1::2]):
            count = own_ref.shape[1]
            total = own_ref[g].astype(F32) + got_ref[g].astype(F32)
            piece_ref[g, start : start + count, :] = total.astype(BF16)
            start += count
        piece_ref[g, start:, :] = packet_ref[...]


def exact_dot(a, b):
    return lax.dot_general(
        a, b, (((1,), (0,)), ((), ())),
        precision=lax.Precision.HIGHEST, preferred_element_type=F32,
    )


def sum_kernel(meta, upper_ref, lower_ref, heads_ref, piece_ref):
    upper_packets = [upper_ref[g, 288:, :].astype(F32) for g in range(16)]
    lower_packets = [lower_ref[g, 96:, :].astype(F32) for g in range(16)]

    def pick(packets, row):
        return jnp.concatenate([p[row : row + 1, :] for p in packets], axis=0)

    first = functools.reduce(jnp.add, [upper_ref[g, :288, :].astype(F32) for g in range(16)])
    second = functools.reduce(jnp.add, [lower_ref[g, :96, :].astype(F32) for g in range(16)])
    for n in range(4):
        here = slice(n * 24, (n + 1) * 24)
        rows = jnp.concatenate([first[192:][here], second[here]], axis=0)
        piece_ref[n, :48, :] = rows.astype(BF16)
        rows = jnp.concatenate([first[:96][here], first[96:192][here]], axis=0)
        piece_ref[4 + n, :48, :] = rows.astype(BF16)
    logits = pick(lower_packets, 8) + pick(lower_packets, 9)
    grad_a, grad_c = logits[:, 0:1], logits[:, 1:2]
    lane = lax.broadcasted_iota(jnp.int32, (8, 128), 1)
    line = lax.broadcasted_iota(jnp.int32, (8, 128), 0)
    picks = jnp.where(lane == meta[7] * 8 + line, 1.0, 0.0).astype(BF16)
    dense = [pick(upper_packets, r) for r in range(8)]
    columns = jnp.concatenate([dot_nt(picks, d.astype(BF16)) for d in dense], axis=0)
    flat = [jnp.sum(pick(lower_packets, 4 + r), axis=0, keepdims=True) for r in range(4)]
    gates = []
    for r in range(8):
        lanes = slice(r * 128, (r + 1) * 128)
        gate = (grad_a * heads_ref[0:1, lanes] + grad_c * heads_ref[1:2, lanes]) * dense[r]
        gates.append(gate)
        flat.append(jnp.sum(gate, axis=0, keepdims=True))
    crossed = [pick(upper_packets, 8 + r) for r in range(8)]
    flat += [jnp.sum(d * grad_a, axis=0, keepdims=True) for d in crossed]
    flat += [jnp.sum(d * grad_c, axis=0, keepdims=True) for d in crossed]
    flat = jnp.concatenate(flat + [jnp.zeros((4, 128), F32)], axis=0).astype(BF16)
    products = [exact_dot(columns, gate) for gate in gates]
    products += [exact_dot(columns, pick(lower_packets, r)) for r in range(4)]
    for z in range(8):
        rows = jnp.concatenate([p[z * 8 : (z + 1) * 8, :] for p in products], axis=0)
        piece_ref[z, 48:144, :] = rows.astype(BF16)
        piece_ref[z, 144:176, :] = flat


def final_kernel(meta, got_ref, kept_ref, sent_ref):
    total = functools.reduce(jnp.add, [got_ref[z].astype(F32) for z in range(8)])

    def of_core(core):
        rows = [total[n * 24 + core * 12 : n * 24 + (core + 1) * 12, :] for n in range(2)]
        rows += [total[48 + r * 8 + core * 4 : 52 + r * 8 + core * 4, :] for r in range(12)]
        return jnp.concatenate(rows + [total[144:176, :]], axis=0)

    for core in (0, 1):

        @pl.when(meta[6] == core)
        def _():
            kept_ref[...] = of_core(core)
            sent_ref[...] = of_core(1 - core)


def join_kernel(meta, kept_ref, got_ref, sequence_ref, mix_ref, cross_ref, gain_ref, bias_ref, heads_ref):
    for core in (0, 1):

        @pl.when(meta[6] == core)
        def _():
            for n in range(2):
                for ref, owner in ((kept_ref, core), (got_ref, 1 - core)):
                    start = n * 256 + owner * 128
                    sequence_ref[:, start : start + 128] = ref[n * 12 : (n + 1) * 12, :]

    total = kept_ref[...] + got_ref[...]
    for r in range(8):
        cross_ref[:, r * 128 : (r + 1) * 128] = total[24 + r * 4 : 28 + r * 4, :]
    for r in range(4):
        lanes = slice(r * 128, (r + 1) * 128)
        mix_ref[:, lanes] = total[56 + r * 4 : 60 + r * 4, :]
        gain_ref[:, lanes] = total[72 + r : 73 + r, :]
    for r in range(8):
        lanes = slice(r * 128, (r + 1) * 128)
        bias_ref[:, lanes] = total[76 + r : 77 + r, :]
        heads_ref[0:1, lanes] = total[84 + r : 85 + r, :]
        heads_ref[1:2, lanes] = total[92 + r : 93 + r, :]


def whole(shape):
    return pl.BlockSpec(shape, lambda i, m: (0,) * len(shape))


def params(megabytes):
    return pltpu.CompilerParams(
        dimension_semantics=("arbitrary",), vmem_limit_bytes=megabytes * 2**20
    )


def cost(flops, moved, exps=0):
    return pl.CostEstimate(flops=flops, bytes_accessed=moved, transcendentals=exps)


def forward(meta, small, large):
    early = pl.BlockSpec((BLOCK, D), lambda i, m: (jnp.minimum(i, BLOCKS - 1), 0))
    late = pl.BlockSpec((BLOCK, D), lambda i, m: (jnp.maximum(i - BLOCKS, 0), 0))
    outs = [((LEN, D), BF16)] * 6 + [
        ((4, 2, LEN), F32), ((4, 2, LEN), F32), ((16, 192, 128), BF16), ((16, 192, 128), BF16),
        ((16, 128), BF16),
        ((1, 128), F32),
    ]
    return pl.pallas_call(
        forward_kernel,
        grid_spec=pltpu.PrefetchScalarGridSpec(
            num_scalar_prefetch=1,
            grid=(2 * BLOCKS,),
            in_specs=[whole(a.shape) for a in small] + [pl.BlockSpec(memory_space=pl.ANY)] * 6,
            out_specs=[early] * 3 + [late] + [early] * 2 + [whole(s) for s, _ in outs[6:]],
            scratch_shapes=[
                pltpu.VMEM((BLOCK + 16, D), BF16),
                pltpu.VMEM((BLOCK, D), BF16),
                pltpu.VMEM((LEN, D), BF16),
                pltpu.VMEM((D, LEN), BF16),
                pltpu.VMEM((LEN, D), BF16),
                pltpu.VMEM((LEN, D), F32),
                pltpu.VMEM((LEN, D), BF16),
                pltpu.VMEM((LEN, DI), F32),
                pltpu.VMEM((1, DI), F32),
                pltpu.VMEM((1, DI), F32),
                pltpu.VMEM((3 * D, D), F32),
            ] + [pltpu.VMEM(a.shape, BF16) for a in large] + [pltpu.SemaphoreType.DMA((6,))],
        ),
        out_shape=[jax.ShapeDtypeStruct(s, t) for s, t in outs],
        compiler_params=params(58),
        cost_estimate=cost(10**10, 2 * 10**7, 10**7),
    )(meta, *small, *large)


def pairs_back(meta, first, queries, keys, values, grads, lse, delta, logit, prior, *far):
    lanes = pl.BlockSpec((LEN, 128), lambda i, m: (0, first + i))
    pair = pl.BlockSpec((1, 2, LEN), lambda i, m: (first + i, 0, 0))
    outs = [((16, 96, 128), BF16), ((16, 96, 128), BF16), ((2, D), F32), ((16, 128), BF16)]
    return pl.pallas_call(
        functools.partial(pairs_kernel, first),
        grid_spec=pltpu.PrefetchScalarGridSpec(
            num_scalar_prefetch=1,
            grid=(2,),
            in_specs=[lanes] * 4 + [pair] * 2 + [whole(logit.shape), whole(prior.shape)]
            + [pl.BlockSpec(memory_space=pl.ANY)] * 5,
            out_specs=[whole(s) for s, _ in outs],
            scratch_shapes=[
                pltpu.VMEM((LEN, 128), F32),
                pltpu.VMEM((LEN, 128), F32),
                pltpu.VMEM((128, LEN), BF16),
                pltpu.VMEM((3 * D, 256), F32),
                pltpu.VMEM((3, 2, LEN, 128), BF16),
                pltpu.VMEM((LEN, D), BF16),
                pltpu.VMEM((LEN, D), BF16),
            ] + [pltpu.VMEM((D, 256), BF16)] * 3 + [pltpu.SemaphoreType.DMA((5,))],
        ),
        out_shape=[jax.ShapeDtypeStruct(s, t) for s, t in outs],
        compiler_params=params(60),
        cost_estimate=cost(10**10, 10**7, 4 * 10**6),
    )(meta, queries, keys, values, grads, lse, delta, logit, prior, *far)


def cut_pieces(packet, *halves):
    count = sum(h.shape[1] for h in halves[::2]) + packet.shape[0]
    return pl.pallas_call(
        piece_kernel,
        out_shape=jax.ShapeDtypeStruct((16, count, 128), BF16),
        compiler_params=pltpu.CompilerParams(vmem_limit_bytes=16 * 2**20),
        cost_estimate=cost(10**6, 3 * 10**6),
    )(packet, *halves)


def sum_pieces(meta, upper, lower, heads):
    return pl.pallas_call(
        sum_kernel,
        grid_spec=pltpu.PrefetchScalarGridSpec(
            num_scalar_prefetch=1,
            grid=(1,),
            in_specs=[whole(a.shape) for a in (upper, lower, heads)],
            out_specs=whole((8, 176, 128)),
        ),
        out_shape=jax.ShapeDtypeStruct((8, 176, 128), BF16),
        compiler_params=params(16),
        cost_estimate=cost(10**7, 2 * 10**6),
    )(meta, upper, lower, heads)


def total_rows(meta, got):
    outs = ((104, 128),) * 2
    return pl.pallas_call(
        final_kernel,
        grid_spec=pltpu.PrefetchScalarGridSpec(
            num_scalar_prefetch=1,
            grid=(1,),
            in_specs=[whole(got.shape)],
            out_specs=[whole(s) for s in outs],
        ),
        out_shape=[jax.ShapeDtypeStruct(s, F32) for s in outs],
        compiler_params=params(16),
        cost_estimate=cost(10**6, 10**6),
    )(meta, got)


def join(meta, *args):
    outs = ((12, D), (4, D), (4, DI), (1, D), (1, DI), (2, DI))
    return pl.pallas_call(
        join_kernel,
        grid_spec=pltpu.PrefetchScalarGridSpec(
            num_scalar_prefetch=1,
            grid=(1,),
            in_specs=[whole(a.shape) for a in args],
            out_specs=[whole(s) for s in outs],
        ),
        out_shape=[jax.ShapeDtypeStruct(s, F32) for s in outs],
        compiler_params=params(16),
        cost_estimate=cost(10**5, 10**5),
    )(meta, *args)


def to_samples(event_ids, event_side, me):
    codes = jnp.concatenate([event_ids // 256, event_ids % 256], axis=1).astype(BF16)
    codes = jnp.concatenate([codes[:, None], jnp.zeros((SAMPLES, 15, D), BF16)], axis=1)

    def part(sample):
        sample = jnp.minimum(sample, SAMPLES - 1)
        side = lax.dynamic_index_in_dim(event_side, sample, 0, keepdims=False)
        code = lax.dynamic_index_in_dim(codes, sample, 0, keepdims=False)
        return jnp.concatenate([side, code])

    got = [part(me)]
    for k in (1, 2, 3):
        pairs = [(i, (i + k) % 4) for i in range(4) if (i + k) % 4 < SAMPLES]
        got.append(lax.ppermute(part((me + k) % 4), CTX, pairs))
    return got


def swap_cores(value):
    return lax.ppermute(value, "core", [(0, 1), (1, 0)])


def per_device(
    event_ids, lengths, event_side, dense_input, labels, event_table, seq_gain, w_mix, w_query,
    w_key, w_value, w_out, w_pool, w_cross, b_cross, w_heads,
):
    me = lax.axis_index(CTX)
    core = lax.axis_index("core")
    chip = lax.axis_index(("z", "ylo", "x", "yhi"))
    own = jnp.minimum(me, SAMPLES - 1)
    parts = to_samples(event_ids, event_side, me)
    length = jnp.where(me < SAMPLES, lengths[own], 0)
    plane = lax.axis_index(PLANE)
    meta = [me, length, labels[own, 0], labels[own, 1], chip, lax.axis_index("z"), core, plane]
    meta = jnp.stack(meta).astype(jnp.int32)
    dense = lax.dynamic_slice_in_dim(dense_input, own, 1, 0)
    mix_row = dot(dense, w_mix)
    base = dot(dense, w_cross) + b_cross[None]

    heads = w_heads.T
    (queries, keys, values, grads, mixed, normed, lse, delta, own, other, packet, logit) = forward(
        meta,
        (*parts, mix_row, seq_gain[None], base, dense.astype(F32), heads),
        (event_table, w_query, w_key, w_value, w_out, w_pool),
    )
    got = swap_cores(other)
    attention = (queries, keys, values, grads, lse, delta, logit)
    rest = (mixed, normed, w_query, w_key, w_value)
    own_first, other_first, sums, _ = pairs_back(
        meta, 0, *attention, jnp.zeros((2, D), F32), *rest
    )
    got, other_first = lax.optimization_barrier((got, other_first))
    pieces = cut_pieces(packet, own, got, own_first, swap_cores(other_first))
    pieces, attention = lax.optimization_barrier((pieces, attention))
    upper_plane = lax.all_to_all(pieces, PLANE, 0, 0)
    own, other, _, packet = pairs_back(meta, 2, *attention, sums, *rest)
    pieces = cut_pieces(packet, own, swap_cores(other))
    lower_plane = lax.all_to_all(pieces, PLANE, 0, 0)
    got = lax.all_to_all(sum_pieces(meta, upper_plane, lower_plane, heads), "z", 0, 0)
    kept, sent = total_rows(meta, got)
    sequence, mix, cross, gain, bias, grad_heads = join(meta, kept, swap_cores(sent))
    return (sequence, mix, cross, gain.reshape(D), bias.reshape(DI), grad_heads.T)


def solution(mesh):
    fine = Mesh(mesh.devices.reshape(8, 2, 4, 2, 2), ("z", "ylo", "x", "yhi", "core"))
    dp = ("z", "ylo", "x")
    every = dp + CTX
    in_specs = (P(dp, CTX), P(dp), P(dp, CTX, None), P(dp, None), P(dp, None)) + (P(),) * 11
    out_specs = (P(every, None), P(every, None), P(every, None), P(), P(), P())
    return jax.shard_map(
        per_device, mesh=fine, in_specs=in_specs, out_specs=out_specs, check_vma=False
    )
```

```python
import functools

import jax
import jax.numpy as jnp
import numpy as np
from jax import lax
from jax.experimental import pallas as pl
from jax.experimental.pallas import tpu as pltpu
from jax.sharding import Mesh, PartitionSpec as P

HEADS = 8
BATCH = 192
SAMPLES = 3
BLOCK = 256
BLOCKS = 4
LEN = 1024
D = 512
DI = 1024
VOCAB = 2048
MASKED = -1e30
EPSILON = 1e-06
LOSS_SCALE = 32768.0
F32 = jnp.float32
BF16 = jnp.bfloat16
CTX = ("yhi", "core")
PLANE = ("ylo", "x", "yhi")


def dot(a, b):
    return lax.dot_general(a, b, (((1,), (0,)), ((), ())), preferred_element_type=F32)


def dot_nt(a, b):
    return lax.dot_general(a, b, (((1,), (1,)), ((), ())), preferred_element_type=F32)


def dot_tn(a, b):
    return lax.dot_general(a, b, (((0,), (0,)), ((), ())), preferred_element_type=F32)


def both_heads(rows):
    low = lax.broadcasted_iota(jnp.int32, rows.shape, 1) < 64
    zero = jnp.zeros_like(rows)
    return jnp.concatenate([jnp.where(low, rows, zero), jnp.where(low, zero, rows)], axis=0)


def causal(tile):
    key = lax.broadcasted_iota(jnp.int32, tile.shape, 0)
    query = lax.broadcasted_iota(jnp.int32, tile.shape, 1) & (BLOCK - 1)
    return key <= query


def spread(core, acc_ref, own_ref, other_ref):
    for mine in (0, 1):

        @pl.when(core == mine)
        def _():
            for block in range(acc_ref.shape[1] // 128):
                target = own_ref if block % 2 == mine else other_ref
                lanes = slice(block * 128, (block + 1) * 128)
                place = slice(block // 2 * 96, (block // 2 + 1) * 96)
                for g in range(16):
                    rows = [acc_ref[n * 384 + g * 24 : n * 384 + (g + 1) * 24, lanes] for n in range(4)]
                    target[g, place, :] = jnp.concatenate(rows, axis=0).astype(BF16)


def own_sample(meta, lengths):
    own = jnp.minimum(meta[0], SAMPLES - 1)
    return own, jnp.where(meta[0] < SAMPLES, lengths[own], 0)


def forward_kernel(
    meta, lengths, labels, part0, part1, part2, part3, mix_ref, gain_ref, base_ref, bias_ref, dense_ref, heads_ref,
    table_far, wq_far, wk_far, wv_far, wo_far, wp_far,
    q_ref, k_ref, v_ref, do_ref, mixed_ref, normed_ref, lse_ref, delta_ref, own_ref, other_ref,
    packet_ref, logit_ref,
    part_ref, q_all, k_all, vt_ref, att_ref, o_ref, res_ref, pre_ref, sum_ref, scaled_ref,
    term_acc, table_ref, wq_ref, wk_ref, wv_ref, wo_ref, wp_ref, sems,
):
    far = (table_far, wq_far, wk_far, wv_far, wo_far, wp_far)
    near = (table_ref, wq_ref, wk_ref, wv_ref, wo_ref, wp_ref)
    copies = [pltpu.make_async_copy(f, n, sems.at[i]) for i, (f, n) in enumerate(zip(far, near))]
    step = pl.program_id(0)
    own, length = own_sample(meta, lengths)

    @pl.when(step == 0)
    def _():
        for copy in copies:
            copy.start()
        sum_ref[...] = jnp.zeros_like(sum_ref)
        term_acc[...] = jnp.zeros_like(term_acc)

    source = lax.rem(meta[0] - jnp.minimum(step, BLOCKS - 1) + BLOCKS, BLOCKS)
    for n, ref in enumerate((part0, part1, part2, part3)):

        @pl.when((step < BLOCKS) & (source == n))
        def _():
            part_ref[...] = ref[...]

    def ahead(c):
        here = slice(c * BLOCK, (c + 1) * BLOCK)
        if c == 0:
            for copy in copies[:4]:
                copy.wait()
        codes = part_ref[BLOCK:, :].astype(F32)
        ids = (codes[:, :BLOCK] * 256.0 + codes[:, BLOCK:]).T[:, 0:1].astype(jnp.int32)
        slots = lax.broadcasted_iota(jnp.int32, (BLOCK, VOCAB), 1)
        picked = jnp.where(slots == ids, 1.0, 0.0).astype(BF16)
        tokens = dot(picked, table_ref[...]) + part_ref[:BLOCK, :].astype(F32)
        mean = jnp.mean(tokens * tokens, axis=1, keepdims=True)
        normed = tokens * lax.rsqrt(mean + EPSILON)
        normed_ref[...] = normed.astype(BF16)
        mixed = (normed * gain_ref[...] + mix_ref[...]).astype(BF16)
        mixed_ref[...] = mixed
        queries = (dot(mixed, wq_ref[...]).astype(BF16).astype(F32) * 0.125).astype(BF16)
        q_ref[...] = queries
        q_all[...] = queries
        keys_now = dot(mixed, wk_ref[...]).astype(BF16)
        k_ref[...] = keys_now
        k_all[here, :] = keys_now
        values = dot(mixed, wv_ref[...]).astype(BF16)
        v_ref[...] = values
        vt_ref[:, here] = values.T
        for p in range(4):
            lanes = slice(p * 128, (p + 1) * 128)
            chosen = both_heads(q_all[:, lanes])
            tiles = []
            for j in range(c + 1):
                tile = dot_nt(k_all[j * BLOCK : (j + 1) * BLOCK, lanes], chosen)
                if j == c:
                    tile = jnp.where(causal(tile), tile, MASKED)
                tiles.append(tile)
            top = functools.reduce(jnp.maximum, [jnp.max(t, axis=0, keepdims=True) for t in tiles])
            raised = [jnp.exp(t - top) for t in tiles]
            total = functools.reduce(jnp.add, [jnp.sum(t, axis=0, keepdims=True) for t in raised])
            inverse = 1.0 / total
            shares = [(t * inverse).astype(BF16) for t in raised]
            lse = top + jnp.log(total)
            lse_ref[p, 0:1, here] = lse[:, :BLOCK]
            lse_ref[p, 1:2, here] = lse[:, BLOCK:]
            first = jnp.zeros((64, BLOCK), F32)
            second = jnp.zeros((64, BLOCK), F32)
            for j in range(c + 1):
                keys = slice(j * BLOCK, (j + 1) * BLOCK)
                first += dot(vt_ref[p * 128 : p * 128 + 64, keys], shares[j][:, :BLOCK])
                second += dot(vt_ref[p * 128 + 64 : p * 128 + 128, keys], shares[j][:, BLOCK:])
            joined = jnp.concatenate([first, second], axis=0).T
            o_ref[here, lanes] = joined
            att_ref[here, lanes] = joined.astype(BF16)
        if c == 0:
            for copy in copies[4:]:
                copy.wait()
        residual = tokens + dot(att_ref[here, :], wo_ref[...])
        half = residual.astype(BF16)
        res_ref[here, :] = half
        pre = dot(half, wp_ref[...])
        pre_ref[here, :] = pre
        valid = (c * BLOCK + lax.broadcasted_iota(jnp.int32, pre.shape, 0)) < length
        silu = jnp.where(valid, pre * jax.nn.sigmoid(pre), 0.0)
        sum_ref[...] += jnp.sum(silu, axis=0, keepdims=True)

    def blank(c):
        if c == 0:
            for copy in copies:
                copy.wait()
        here = slice(c * BLOCK, (c + 1) * BLOCK)
        for ref in (q_ref, k_ref, v_ref, mixed_ref, normed_ref):
            ref[...] = jnp.zeros((BLOCK, D), ref.dtype)
        lse_ref[:, :, here] = jnp.zeros((4, 2, BLOCK), F32)
        delta_ref[:, :, here] = jnp.zeros((4, 2, BLOCK), F32)

    for c in range(BLOCKS):
        pl.when((step == c) & (length > c * BLOCK))(functools.partial(ahead, c))
        pl.when((step == c) & (length <= c * BLOCK))(functools.partial(blank, c))

    @pl.when(step == BLOCKS)
    def _():
        span = jnp.maximum(length, 1).astype(F32)
        dense = dense_ref[...].astype(F32)
        gate = base_ref[...] + bias_ref[...] + sum_ref[...] / span
        crossed = dense + dense * gate
        rows = [dense[:, n * 128 : (n + 1) * 128] for n in range(8)]
        rows += [crossed[:, n * 128 : (n + 1) * 128] for n in range(8)]
        packet_ref[...] = jnp.concatenate(rows, axis=0).astype(BF16)
        a = jnp.sum(crossed * heads_ref[0:1, :], axis=1, keepdims=True)
        c = jnp.sum(crossed * heads_ref[1:2, :], axis=1, keepdims=True)
        clicked = labels[own, 0].astype(F32)
        converted = (labels[own, 0] * labels[own, 1]).astype(F32)
        top = jnp.maximum(jnp.maximum(a, c), 0.0)
        ea, ec = jnp.exp(a - top), jnp.exp(c - top)
        below = jnp.exp(-top) + ea + ec
        grad_a = jax.nn.sigmoid(a) - clicked - converted * jax.nn.sigmoid(-a)
        grad_a = grad_a - (1.0 - converted) * (ea / below - jax.nn.sigmoid(a))
        grad_c = -converted * jax.nn.sigmoid(-c)
        grad_c = grad_c - (1.0 - converted) * (ec / below - jax.nn.sigmoid(c))
        factor = jnp.where(length > 0, LOSS_SCALE / BATCH, 0.0)
        grad_a = grad_a * factor
        grad_c = grad_c * factor
        lane = lax.broadcasted_iota(jnp.int32, (1, 128), 1)
        logit_ref[...] = jnp.where(lane == 0, grad_a, jnp.where(lane == 1, grad_c, 0.0))
        grad_gate = (grad_a * heads_ref[0:1, :] + grad_c * heads_ref[1:2, :]) * dense
        scaled_ref[...] = grad_gate / span

    def back(c):
        here = slice(c * BLOCK, (c + 1) * BLOCK)
        pre = pre_ref[here, :]
        sig = jax.nn.sigmoid(pre)
        valid = (c * BLOCK + lax.broadcasted_iota(jnp.int32, pre.shape, 0)) < length
        slope = sig * (1.0 + pre * (1.0 - sig)) * scaled_ref[...]
        grad_pre = jnp.where(valid, slope, 0.0).astype(BF16)
        term_acc[D:, :] += dot_tn(grad_pre, res_ref[here, :])
        grad_res = dot_nt(grad_pre, wp_ref[...]).astype(BF16)
        term_acc[:D, :] += dot_tn(att_ref[here, :], grad_res)
        grad_att = dot_nt(grad_res, wo_ref[...]).astype(BF16)
        do_ref[...] = grad_att
        product = grad_att.astype(F32) * o_ref[here, :]
        head = lax.broadcasted_iota(jnp.int32, (HEADS, D), 0)
        column = lax.broadcasted_iota(jnp.int32, (HEADS, D), 1) // 64
        picks = jnp.where(head == column, 1.0, 0.0).astype(BF16)
        high = product.astype(BF16)
        low = (product - high.astype(F32)).astype(BF16)
        delta = dot_nt(picks, high) + dot_nt(picks, low)
        for p in range(4):
            delta_ref[p, :, here] = delta[2 * p : 2 * p + 2, :]

    def quiet():
        do_ref[...] = jnp.zeros((BLOCK, D), BF16)

    for c in range(BLOCKS):
        pl.when((step == BLOCKS + c) & (length > c * BLOCK))(functools.partial(back, c))
        pl.when((step == BLOCKS + c) & (length <= c * BLOCK))(quiet)

    @pl.when(step == 2 * BLOCKS - 1)
    def _():
        spread(meta[1], term_acc, own_ref, other_ref)


def pair_body(
    length, q_ref, k_ref, v_ref, do_ref, lse_ref, delta_ref, dq_ref, dk_ref, dv_ref, dk_acc, dv_acc, kt_ref
):
    dk_acc[...] = jnp.zeros_like(dk_acc)
    dv_acc[...] = jnp.zeros_like(dv_acc)
    kt_ref[...] = k_ref[...].T

    def block(c):
        here = slice(c * BLOCK, (c + 1) * BLOCK)
        chosen = both_heads(q_ref[here, :])
        grads = both_heads(do_ref[here, :])
        lse = jnp.concatenate([lse_ref[0, 0:1, here], lse_ref[0, 1:2, here]], axis=1)
        delta = jnp.concatenate([delta_ref[0, 0:1, here], delta_ref[0, 1:2, here]], axis=1)
        first = jnp.zeros((64, BLOCK), F32)
        second = jnp.zeros((64, BLOCK), F32)
        for j in range(c + 1):
            keys = slice(j * BLOCK, (j + 1) * BLOCK)
            shares = jnp.exp(dot_nt(k_ref[keys, :], chosen) - lse)
            if j == c:
                shares = jnp.where(causal(shares), shares, 0.0)
            grad_shares = dot_nt(v_ref[keys, :], grads)
            grad_scores = (shares * (grad_shares - delta)).astype(BF16)
            dv_acc[keys, :] += dot(shares.astype(BF16), grads)
            dk_acc[keys, :] += dot(grad_scores, chosen)
            first += dot(kt_ref[0:64, keys], grad_scores[:, :BLOCK])
            second += dot(kt_ref[64:128, keys], grad_scores[:, BLOCK:])
        joined = jnp.concatenate([first, second], axis=0) * 0.125
        dq_ref[here, :] = joined.T.astype(BF16)

    def blank(c):
        here = slice(c * BLOCK, (c + 1) * BLOCK)
        dq_ref[here, :] = jnp.zeros((BLOCK, 128), BF16)

    for c in range(BLOCKS):
        pl.when(length > c * BLOCK)(functools.partial(block, c))
        pl.when(length <= c * BLOCK)(functools.partial(blank, c))
    dk_ref[...] = dk_acc[...].astype(BF16)
    dv_ref[...] = dv_acc[...].astype(BF16)


def pairs_kernel(
    first,
    meta, lengths, q_ref, k_ref, v_ref, do_ref, lse_ref, delta_ref, logit_ref, *refs
):
    prior_ref = refs[0] if first else None
    (
        mixed_far, normed_far, wq_far, wk_far, wv_far, own_ref, other_ref, sums_ref, packet_ref,
        dk_acc, dv_acc, kt_ref, term_ref, grad_ref, mixed_ref, normed_ref, wq_ref, wk_ref, wv_ref, sems,
    ) = refs[1:] if first else refs
    step = pl.program_id(0)
    columns = pl.ds(first * 128, 256)
    far = (mixed_far, normed_far) + tuple(w.at[:, columns] for w in (wq_far, wk_far, wv_far))
    near = (mixed_ref, normed_ref, wq_ref, wk_ref, wv_ref)
    copies = [pltpu.make_async_copy(f, n, sems.at[i]) for i, (f, n) in enumerate(zip(far, near))]

    @pl.when(step == 0)
    def _():
        for copy in copies:
            copy.start()

    _, length = own_sample(meta, lengths)
    pair_body(
        length, q_ref, k_ref, v_ref, do_ref, lse_ref, delta_ref,
        grad_ref.at[0, step], grad_ref.at[1, step], grad_ref.at[2, step], dk_acc, dv_acc, kt_ref,
    )

    @pl.when(step == 1)
    def _():
        for copy in copies:
            copy.wait()
        turned = mixed_ref[...].T
        total = None
        for n, weight in enumerate((wq_ref, wk_ref, wv_ref)):
            rows = jnp.concatenate([grad_ref[n, 0], grad_ref[n, 1]], axis=1)
            term_ref[n * D : (n + 1) * D, :] = dot(turned, rows)
            part = dot_nt(rows, weight[...])
            total = part if total is None else total + part
        spread(meta[1], term_ref, own_ref, other_ref)
        mix = jnp.sum(total, axis=0, keepdims=True)
        gain = jnp.sum(total * normed_ref[...].astype(F32), axis=0, keepdims=True)
        if first:
            mix, gain = mix + prior_ref[0:1, :], gain + prior_ref[1:2, :]
        sums_ref[...] = jnp.concatenate([mix, gain], axis=0)
        logit = logit_ref[...]
        high = logit.astype(BF16).astype(F32)
        lines = [mix[:, n * 128 : (n + 1) * 128] for n in range(4)]
        lines += [gain[:, n * 128 : (n + 1) * 128] for n in range(4)]
        lines += [high, logit - high, jnp.zeros((6, 128), F32)]
        packet_ref[...] = jnp.concatenate(lines, axis=0).astype(BF16)


def piece_kernel(packet_ref, *refs):
    *halves, piece_ref = refs
    for g in range(16):
        start = 0
        for own_ref, got_ref in zip(halves[::2], halves[1::2]):
            count = own_ref.shape[1]
            total = own_ref[g].astype(F32) + got_ref[g].astype(F32)
            piece_ref[g, start : start + count, :] = total.astype(BF16)
            start += count
        piece_ref[g, start:, :] = packet_ref[...]


def exact_dot(a, b):
    return lax.dot_general(
        a, b, (((1,), (0,)), ((), ())),
        precision=lax.Precision.HIGHEST, preferred_element_type=F32,
    )


def sum_kernel(meta, upper_ref, lower_ref, heads_ref, piece_ref):
    upper_packets = [upper_ref[g, 288:, :].astype(F32) for g in range(16)]
    lower_packets = [lower_ref[g, 96:, :].astype(F32) for g in range(16)]

    def pick(packets, row):
        return jnp.concatenate([p[row : row + 1, :] for p in packets], axis=0)

    first = functools.reduce(jnp.add, [upper_ref[g, :288, :].astype(F32) for g in range(16)])
    second = functools.reduce(jnp.add, [lower_ref[g, :96, :].astype(F32) for g in range(16)])
    for n in range(4):
        here = slice(n * 24, (n + 1) * 24)
        rows = jnp.concatenate([first[192:][here], second[here]], axis=0)
        piece_ref[n, :48, :] = rows.astype(BF16)
        rows = jnp.concatenate([first[:96][here], first[96:192][here]], axis=0)
        piece_ref[4 + n, :48, :] = rows.astype(BF16)
    logits = pick(lower_packets, 8) + pick(lower_packets, 9)
    grad_a, grad_c = logits[:, 0:1], logits[:, 1:2]
    lane = lax.broadcasted_iota(jnp.int32, (8, 128), 1)
    line = lax.broadcasted_iota(jnp.int32, (8, 128), 0)
    picks = jnp.where(lane == meta[2] * 8 + line, 1.0, 0.0).astype(BF16)
    dense = [pick(upper_packets, r) for r in range(8)]
    columns = jnp.concatenate([dot_nt(picks, d.astype(BF16)) for d in dense], axis=0)
    flat = [jnp.sum(pick(lower_packets, 4 + r), axis=0, keepdims=True) for r in range(4)]
    gates = []
    for r in range(8):
        lanes = slice(r * 128, (r + 1) * 128)
        gate = (grad_a * heads_ref[0:1, lanes] + grad_c * heads_ref[1:2, lanes]) * dense[r]
        gates.append(gate)
        flat.append(jnp.sum(gate, axis=0, keepdims=True))
    crossed = [pick(upper_packets, 8 + r) for r in range(8)]
    flat += [jnp.sum(d * grad_a, axis=0, keepdims=True) for d in crossed]
    flat += [jnp.sum(d * grad_c, axis=0, keepdims=True) for d in crossed]
    flat = jnp.concatenate(flat + [jnp.zeros((4, 128), F32)], axis=0).astype(BF16)
    products = [exact_dot(columns, gate) for gate in gates]
    products += [exact_dot(columns, pick(lower_packets, r)) for r in range(4)]
    for z in range(8):
        rows = jnp.concatenate([p[z * 8 : (z + 1) * 8, :] for p in products], axis=0)
        piece_ref[z, 48:144, :] = rows.astype(BF16)
        piece_ref[z, 144:176, :] = flat


def final_kernel(meta, got_ref, kept_ref, sent_ref):
    total = functools.reduce(jnp.add, [got_ref[z].astype(F32) for z in range(8)])

    def of_core(core):
        rows = [total[n * 24 + core * 12 : n * 24 + (core + 1) * 12, :] for n in range(2)]
        rows += [total[48 + r * 8 + core * 4 : 52 + r * 8 + core * 4, :] for r in range(12)]
        return jnp.concatenate(rows + [total[144:176, :]], axis=0)

    for core in (0, 1):

        @pl.when(meta[1] == core)
        def _():
            kept_ref[...] = of_core(core)
            sent_ref[...] = of_core(1 - core)


def join_kernel(meta, kept_ref, got_ref, sequence_ref, mix_ref, cross_ref, gain_ref, bias_ref, heads_ref):
    for core in (0, 1):

        @pl.when(meta[1] == core)
        def _():
            for n in range(2):
                for ref, owner in ((kept_ref, core), (got_ref, 1 - core)):
                    start = n * 256 + owner * 128
                    sequence_ref[:, start : start + 128] = ref[n * 12 : (n + 1) * 12, :]

    total = kept_ref[...] + got_ref[...]
    for r in range(8):
        cross_ref[:, r * 128 : (r + 1) * 128] = total[24 + r * 4 : 28 + r * 4, :]
    for r in range(4):
        lanes = slice(r * 128, (r + 1) * 128)
        mix_ref[:, lanes] = total[56 + r * 4 : 60 + r * 4, :]
        gain_ref[:, lanes] = total[72 + r : 73 + r, :]
    for r in range(8):
        lanes = slice(r * 128, (r + 1) * 128)
        bias_ref[:, lanes] = total[76 + r : 77 + r, :]
        heads_ref[0:1, lanes] = total[84 + r : 85 + r, :]
        heads_ref[1:2, lanes] = total[92 + r : 93 + r, :]


def whole(shape):
    return pl.BlockSpec(shape, lambda i, *m: (0,) * len(shape))


def params(megabytes):
    return pltpu.CompilerParams(
        dimension_semantics=("arbitrary",), vmem_limit_bytes=megabytes * 2**20
    )


def cost(flops, moved, exps=0):
    return pl.CostEstimate(flops=flops, bytes_accessed=moved, transcendentals=exps)


def forward(scalars, small, large):
    early = pl.BlockSpec((BLOCK, D), lambda i, *m: (jnp.minimum(i, BLOCKS - 1), 0))
    late = pl.BlockSpec((BLOCK, D), lambda i, *m: (jnp.maximum(i - BLOCKS, 0), 0))
    outs = [((LEN, D), BF16)] * 6 + [
        ((4, 2, LEN), F32), ((4, 2, LEN), F32), ((16, 192, 128), BF16), ((16, 192, 128), BF16),
        ((16, 128), BF16),
        ((1, 128), F32),
    ]
    return pl.pallas_call(
        forward_kernel,
        grid_spec=pltpu.PrefetchScalarGridSpec(
            num_scalar_prefetch=3,
            grid=(2 * BLOCKS,),
            in_specs=[whole(a.shape) for a in small] + [pl.BlockSpec(memory_space=pl.ANY)] * 6,
            out_specs=[early] * 3 + [late] + [early] * 2 + [whole(s) for s, _ in outs[6:]],
            scratch_shapes=[
                pltpu.VMEM((BLOCK + 16, D), BF16),
                pltpu.VMEM((BLOCK, D), BF16),
                pltpu.VMEM((LEN, D), BF16),
                pltpu.VMEM((D, LEN), BF16),
                pltpu.VMEM((LEN, D), BF16),
                pltpu.VMEM((LEN, D), F32),
                pltpu.VMEM((LEN, D), BF16),
                pltpu.VMEM((LEN, DI), F32),
                pltpu.VMEM((1, DI), F32),
                pltpu.VMEM((1, DI), F32),
                pltpu.VMEM((3 * D, D), F32),
            ] + [pltpu.VMEM(a.shape, BF16) for a in large] + [pltpu.SemaphoreType.DMA((6,))],
        ),
        out_shape=[jax.ShapeDtypeStruct(s, t) for s, t in outs],
        compiler_params=params(58),
        cost_estimate=cost(10**10, 2 * 10**7, 10**7),
    )(*scalars, *small, *large)


def pairs_back(scalars, first, queries, keys, values, grads, lse, delta, logit, *far):
    prior = [whole((2, D))] if first else []
    lanes = pl.BlockSpec((LEN, 128), lambda i, *m: (0, first + i))
    pair = pl.BlockSpec((1, 2, LEN), lambda i, *m: (first + i, 0, 0))
    outs = [((16, 96, 128), BF16), ((16, 96, 128), BF16), ((2, D), F32), ((16, 128), BF16)]
    return pl.pallas_call(
        functools.partial(pairs_kernel, first),
        grid_spec=pltpu.PrefetchScalarGridSpec(
            num_scalar_prefetch=2,
            grid=(2,),
            in_specs=[lanes] * 4 + [pair] * 2 + [whole(logit.shape)]
            + prior + [pl.BlockSpec(memory_space=pl.ANY)] * 5,
            out_specs=[whole(s) for s, _ in outs],
            scratch_shapes=[
                pltpu.VMEM((LEN, 128), F32),
                pltpu.VMEM((LEN, 128), F32),
                pltpu.VMEM((128, LEN), BF16),
                pltpu.VMEM((3 * D, 256), F32),
                pltpu.VMEM((3, 2, LEN, 128), BF16),
                pltpu.VMEM((LEN, D), BF16),
                pltpu.VMEM((LEN, D), BF16),
            ] + [pltpu.VMEM((D, 256), BF16)] * 3 + [pltpu.SemaphoreType.DMA((5,))],
        ),
        out_shape=[jax.ShapeDtypeStruct(s, t) for s, t in outs],
        compiler_params=params(60),
        cost_estimate=cost(10**10, 10**7, 4 * 10**6),
    )(*scalars, queries, keys, values, grads, lse, delta, logit, *far)


def cut_pieces(packet, *halves):
    count = sum(h.shape[1] for h in halves[::2]) + packet.shape[0]
    return pl.pallas_call(
        piece_kernel,
        out_shape=jax.ShapeDtypeStruct((16, count, 128), BF16),
        compiler_params=pltpu.CompilerParams(vmem_limit_bytes=16 * 2**20),
        cost_estimate=cost(10**6, 3 * 10**6),
    )(packet, *halves)


def sum_pieces(meta, upper, lower, heads):
    return pl.pallas_call(
        sum_kernel,
        grid_spec=pltpu.PrefetchScalarGridSpec(
            num_scalar_prefetch=1,
            grid=(1,),
            in_specs=[whole(a.shape) for a in (upper, lower, heads)],
            out_specs=whole((8, 176, 128)),
        ),
        out_shape=jax.ShapeDtypeStruct((8, 176, 128), BF16),
        compiler_params=params(16),
        cost_estimate=cost(10**7, 2 * 10**6),
    )(meta, upper, lower, heads)


def total_rows(meta, got):
    outs = ((104, 128),) * 2
    return pl.pallas_call(
        final_kernel,
        grid_spec=pltpu.PrefetchScalarGridSpec(
            num_scalar_prefetch=1,
            grid=(1,),
            in_specs=[whole(got.shape)],
            out_specs=[whole(s) for s in outs],
        ),
        out_shape=[jax.ShapeDtypeStruct(s, F32) for s in outs],
        compiler_params=params(16),
        cost_estimate=cost(10**6, 10**6),
    )(meta, got)


def join(meta, *args):
    outs = ((12, D), (4, D), (4, DI), (1, D), (1, DI), (2, DI))
    return pl.pallas_call(
        join_kernel,
        grid_spec=pltpu.PrefetchScalarGridSpec(
            num_scalar_prefetch=1,
            grid=(1,),
            in_specs=[whole(a.shape) for a in args],
            out_specs=[whole(s) for s in outs],
        ),
        out_shape=[jax.ShapeDtypeStruct(s, F32) for s in outs],
        compiler_params=params(16),
        cost_estimate=cost(10**5, 10**5),
    )(meta, *args)


def to_samples(event_ids, event_side, me):
    codes = jnp.concatenate([event_ids // 256, event_ids % 256], axis=1).astype(BF16)
    codes = jnp.concatenate([codes[:, None], jnp.zeros((SAMPLES, 15, D), BF16)], axis=1)

    def part(sample):
        sample = jnp.minimum(sample, SAMPLES - 1)
        side = lax.dynamic_index_in_dim(event_side, sample, 0, keepdims=False)
        code = lax.dynamic_index_in_dim(codes, sample, 0, keepdims=False)
        return jnp.concatenate([side, code])

    got = [part(me)]
    for k in (1, 2, 3):
        pairs = [(i, (i + k) % 4) for i in range(4) if (i + k) % 4 < SAMPLES]
        got.append(lax.ppermute(part((me + k) % 4), CTX, pairs))
    return got


def swap_cores(value):
    return lax.ppermute(value, "core", [(0, 1), (1, 0)])


def per_device(
    event_ids, lengths, event_side, dense_input, labels, event_table, seq_gain, w_mix, w_query,
    w_key, w_value, w_out, w_pool, w_cross, b_cross, w_heads,
):
    me = lax.axis_index(CTX)
    own = jnp.minimum(me, SAMPLES - 1)
    parts = to_samples(event_ids, event_side, me)
    device = np.arange(256)
    places = np.stack([device % 4, device % 2, device // 2 % 16] + [0 * device] * 5, axis=1)
    meta = jnp.asarray(places, jnp.int32)[lax.axis_index(("z", "ylo", "x") + CTX)]
    dense = lax.dynamic_slice_in_dim(dense_input, own, 1, 0)
    mix_row = dot(dense, w_mix)
    base = dot(dense, w_cross)
    heads = w_heads.T
    (queries, keys, values, grads, mixed, normed, lse, delta, own, other, packet, logit) = forward(
        (meta, lengths, labels),
        (*parts, mix_row, seq_gain[None], base, b_cross[None], dense, heads),
        (event_table, w_query, w_key, w_value, w_out, w_pool),
    )
    got = swap_cores(other)
    attention = (queries, keys, values, grads, lse, delta, logit)
    rest = (mixed, normed, w_query, w_key, w_value)
    own_first, other_first, sums, _ = pairs_back((meta, lengths), 0, *attention, *rest)
    got, other_first = lax.optimization_barrier((got, other_first))
    pieces = cut_pieces(packet, own, got, own_first, swap_cores(other_first))
    pieces, attention = lax.optimization_barrier((pieces, attention))
    upper_plane = lax.all_to_all(pieces, PLANE, 0, 0)
    own, other, _, packet = pairs_back((meta, lengths), 2, *attention, sums, *rest)
    upper_plane, other = lax.optimization_barrier((upper_plane, other))
    pieces = cut_pieces(packet, own, swap_cores(other))
    lower_plane = lax.all_to_all(pieces, PLANE, 0, 0)
    got = lax.all_to_all(sum_pieces(meta, upper_plane, lower_plane, heads), "z", 0, 0)
    kept, sent = total_rows(meta, got)
    sequence, mix, cross, gain, bias, grad_heads = join(meta, kept, swap_cores(sent))
    return (sequence, mix, cross, gain.reshape(D), bias.reshape(DI), grad_heads.T)


def solution(mesh):
    fine = Mesh(mesh.devices.reshape(8, 2, 4, 2, 2), ("z", "ylo", "x", "yhi", "core"))
    dp = ("z", "ylo", "x")
    every = dp + CTX
    in_specs = (P(dp, CTX), P(dp), P(dp, CTX, None), P(dp, None), P(dp, None)) + (P(),) * 11
    out_specs = (P(every, None), P(every, None), P(every, None), P(), P(), P())
    return jax.shard_map(
        per_device, mesh=fine, in_specs=in_specs, out_specs=out_specs, check_vma=False
    )
```

```python
import functools

import jax
import jax.numpy as jnp
import numpy as np
from jax import lax
from jax.experimental import pallas as pl
from jax.experimental.pallas import tpu as pltpu
from jax.sharding import Mesh, PartitionSpec as P

HEADS = 8
BATCH = 192
SAMPLES = 3
BLOCK = 256
BLOCKS = 4
LEN = 1024
D = 512
DI = 1024
VOCAB = 2048
MASKED = -1e30
EPSILON = 1e-06
LOSS_SCALE = 32768.0
F32 = jnp.float32
BF16 = jnp.bfloat16
CTX = ("yhi", "core")
PLANE = ("ylo", "x", "yhi")


def dot(a, b):
    return lax.dot_general(a, b, (((1,), (0,)), ((), ())), preferred_element_type=F32)


def dot_nt(a, b):
    return lax.dot_general(a, b, (((1,), (1,)), ((), ())), preferred_element_type=F32)


def dot_tn(a, b):
    return lax.dot_general(a, b, (((0,), (0,)), ((), ())), preferred_element_type=F32)


def both_heads(rows):
    low = lax.broadcasted_iota(jnp.int32, rows.shape, 1) < 64
    zero = jnp.zeros_like(rows)
    return jnp.concatenate([jnp.where(low, rows, zero), jnp.where(low, zero, rows)], axis=0)


def causal(tile):
    key = lax.broadcasted_iota(jnp.int32, tile.shape, 0)
    query = lax.broadcasted_iota(jnp.int32, tile.shape, 1) & (BLOCK - 1)
    return key <= query


def spread(core, acc_ref, own_ref, other_ref):
    for mine in (0, 1):

        @pl.when(core == mine)
        def _():
            for block in range(acc_ref.shape[1] // 128):
                target = own_ref if block % 2 == mine else other_ref
                lanes = slice(block * 128, (block + 1) * 128)
                place = slice(block // 2 * 96, (block // 2 + 1) * 96)
                for g in range(16):
                    rows = [acc_ref[n * 384 + g * 24 : n * 384 + (g + 1) * 24, lanes] for n in range(4)]
                    target[g, place, :] = jnp.concatenate(rows, axis=0).astype(BF16)


def own_sample(meta, lengths):
    own = jnp.minimum(meta[0], SAMPLES - 1)
    return own, jnp.where(meta[0] < SAMPLES, lengths[own], 0)


def forward_kernel(
    meta, lengths, labels, part0, part1, part2, part3, mix_ref, gain_ref, base_ref, bias_ref, dense_ref, heads_ref,
    table_far, wq_far, wk_far, wv_far, wo_far, wp_far,
    q_ref, k_ref, v_ref, do_ref, mixed_ref, normed_ref, lse_ref, delta_ref, own_ref, other_ref,
    packet_ref, logit_ref,
    part_ref, q_all, k_all, vt_ref, att_ref, o_ref, res_ref, pre_ref, sum_ref, scaled_ref,
    term_acc, table_ref, wq_ref, wk_ref, wv_ref, wo_ref, wp_ref, sems,
):
    far = (table_far, wq_far, wk_far, wv_far, wo_far, wp_far)
    near = (table_ref, wq_ref, wk_ref, wv_ref, wo_ref, wp_ref)
    copies = [pltpu.make_async_copy(f, n, sems.at[i]) for i, (f, n) in enumerate(zip(far, near))]
    step = pl.program_id(0)
    own, length = own_sample(meta, lengths)

    @pl.when(step == 0)
    def _():
        for copy in copies:
            copy.start()
        sum_ref[...] = jnp.zeros_like(sum_ref)
        term_acc[...] = jnp.zeros_like(term_acc)

    source = lax.rem(meta[0] - jnp.minimum(step, BLOCKS - 1) + BLOCKS, BLOCKS)
    for n, ref in enumerate((part0, part1, part2, part3)):

        @pl.when((step < BLOCKS) & (source == n))
        def _():
            part_ref[...] = ref[...]

    def ahead(c):
        here = slice(c * BLOCK, (c + 1) * BLOCK)
        if c == 0:
            for copy in copies[:4]:
                copy.wait()
        codes = part_ref[BLOCK:, :].astype(F32)
        ids = (codes[:, :BLOCK] * 256.0 + codes[:, BLOCK:]).T[:, 0:1].astype(jnp.int32)
        slots = lax.broadcasted_iota(jnp.int32, (BLOCK, VOCAB), 1)
        picked = jnp.where(slots == ids, 1.0, 0.0).astype(BF16)
        tokens = dot(picked, table_ref[...]) + part_ref[:BLOCK, :].astype(F32)
        mean = jnp.mean(tokens * tokens, axis=1, keepdims=True)
        normed = tokens * lax.rsqrt(mean + EPSILON)
        normed_ref[...] = normed.astype(BF16)
        mixed = (normed * gain_ref[...] + mix_ref[...]).astype(BF16)
        mixed_ref[...] = mixed
        queries = (dot(mixed, wq_ref[...]).astype(BF16).astype(F32) * 0.125).astype(BF16)
        q_ref[...] = queries
        q_all[...] = queries
        keys_now = dot(mixed, wk_ref[...]).astype(BF16)
        k_ref[...] = keys_now
        k_all[here, :] = keys_now
        values = dot(mixed, wv_ref[...]).astype(BF16)
        v_ref[...] = values
        vt_ref[:, here] = values.T
        for p in range(4):
            lanes = slice(p * 128, (p + 1) * 128)
            chosen = both_heads(q_all[:, lanes])
            tiles = []
            for j in range(c + 1):
                tile = dot_nt(k_all[j * BLOCK : (j + 1) * BLOCK, lanes], chosen)
                if j == c:
                    tile = jnp.where(causal(tile), tile, MASKED)
                tiles.append(tile)
            top = functools.reduce(jnp.maximum, [jnp.max(t, axis=0, keepdims=True) for t in tiles])
            raised = [jnp.exp(t - top) for t in tiles]
            total = functools.reduce(jnp.add, [jnp.sum(t, axis=0, keepdims=True) for t in raised])
            inverse = 1.0 / total
            shares = [(t * inverse).astype(BF16) for t in raised]
            lse = top + jnp.log(total)
            lse_ref[p, 0:1, here] = lse[:, :BLOCK]
            lse_ref[p, 1:2, here] = lse[:, BLOCK:]
            first = jnp.zeros((64, BLOCK), F32)
            second = jnp.zeros((64, BLOCK), F32)
            for j in range(c + 1):
                keys = slice(j * BLOCK, (j + 1) * BLOCK)
                first += dot(vt_ref[p * 128 : p * 128 + 64, keys], shares[j][:, :BLOCK])
                second += dot(vt_ref[p * 128 + 64 : p * 128 + 128, keys], shares[j][:, BLOCK:])
            joined = jnp.concatenate([first, second], axis=0).T
            o_ref[here, lanes] = joined
            att_ref[here, lanes] = joined.astype(BF16)
        if c == 0:
            for copy in copies[4:]:
                copy.wait()
        residual = tokens + dot(att_ref[here, :], wo_ref[...])
        half = residual.astype(BF16)
        res_ref[here, :] = half
        pre = dot(half, wp_ref[...])
        pre_ref[here, :] = pre
        valid = (c * BLOCK + lax.broadcasted_iota(jnp.int32, pre.shape, 0)) < length
        silu = jnp.where(valid, pre * jax.nn.sigmoid(pre), 0.0)
        sum_ref[...] += jnp.sum(silu, axis=0, keepdims=True)

    def blank(c):
        if c == 0:
            for copy in copies:
                copy.wait()
        here = slice(c * BLOCK, (c + 1) * BLOCK)
        for ref in (q_ref, k_ref, v_ref, mixed_ref, normed_ref):
            ref[...] = jnp.zeros((BLOCK, D), ref.dtype)
        lse_ref[:, :, here] = jnp.zeros((4, 2, BLOCK), F32)
        delta_ref[:, :, here] = jnp.zeros((4, 2, BLOCK), F32)

    for c in range(BLOCKS):
        pl.when((step == c) & (length > c * BLOCK))(functools.partial(ahead, c))
        pl.when((step == c) & (length <= c * BLOCK))(functools.partial(blank, c))

    @pl.when(step == BLOCKS)
    def _():
        span = jnp.maximum(length, 1).astype(F32)
        dense = dense_ref[...].astype(F32)
        gate = base_ref[...] + bias_ref[...] + sum_ref[...] / span
        crossed = dense + dense * gate
        rows = [dense[:, n * 128 : (n + 1) * 128] for n in range(8)]
        rows += [crossed[:, n * 128 : (n + 1) * 128] for n in range(8)]
        packet_ref[...] = jnp.concatenate(rows, axis=0).astype(BF16)
        a = jnp.sum(crossed * heads_ref[0:1, :], axis=1, keepdims=True)
        c = jnp.sum(crossed * heads_ref[1:2, :], axis=1, keepdims=True)
        clicked = labels[own, 0].astype(F32)
        converted = (labels[own, 0] * labels[own, 1]).astype(F32)
        top = jnp.maximum(jnp.maximum(a, c), 0.0)
        ea, ec = jnp.exp(a - top), jnp.exp(c - top)
        below = jnp.exp(-top) + ea + ec
        grad_a = jax.nn.sigmoid(a) - clicked - converted * jax.nn.sigmoid(-a)
        grad_a = grad_a - (1.0 - converted) * (ea / below - jax.nn.sigmoid(a))
        grad_c = -converted * jax.nn.sigmoid(-c)
        grad_c = grad_c - (1.0 - converted) * (ec / below - jax.nn.sigmoid(c))
        factor = jnp.where(length > 0, LOSS_SCALE / BATCH, 0.0)
        grad_a = grad_a * factor
        grad_c = grad_c * factor
        lane = lax.broadcasted_iota(jnp.int32, (1, 128), 1)
        logit_ref[...] = jnp.where(lane == 0, grad_a, jnp.where(lane == 1, grad_c, 0.0))
        grad_gate = (grad_a * heads_ref[0:1, :] + grad_c * heads_ref[1:2, :]) * dense
        scaled_ref[...] = grad_gate / span

    def back(c):
        here = slice(c * BLOCK, (c + 1) * BLOCK)
        pre = pre_ref[here, :]
        sig = jax.nn.sigmoid(pre)
        valid = (c * BLOCK + lax.broadcasted_iota(jnp.int32, pre.shape, 0)) < length
        slope = sig * (1.0 + pre * (1.0 - sig)) * scaled_ref[...]
        grad_pre = jnp.where(valid, slope, 0.0).astype(BF16)
        term_acc[D:, :] += dot_tn(grad_pre, res_ref[here, :])
        grad_res = dot_nt(grad_pre, wp_ref[...]).astype(BF16)
        term_acc[:D, :] += dot_tn(att_ref[here, :], grad_res)
        grad_att = dot_nt(grad_res, wo_ref[...]).astype(BF16)
        do_ref[...] = grad_att
        product = grad_att.astype(F32) * o_ref[here, :]
        head = lax.broadcasted_iota(jnp.int32, (HEADS, D), 0)
        column = lax.broadcasted_iota(jnp.int32, (HEADS, D), 1) // 64
        picks = jnp.where(head == column, 1.0, 0.0).astype(BF16)
        high = product.astype(BF16)
        low = (product - high.astype(F32)).astype(BF16)
        delta = dot_nt(picks, high) + dot_nt(picks, low)
        for p in range(4):
            delta_ref[p, :, here] = delta[2 * p : 2 * p + 2, :]

    def quiet():
        do_ref[...] = jnp.zeros((BLOCK, D), BF16)

    for c in range(BLOCKS):
        pl.when((step == BLOCKS + c) & (length > c * BLOCK))(functools.partial(back, c))
        pl.when((step == BLOCKS + c) & (length <= c * BLOCK))(quiet)

    @pl.when(step == 2 * BLOCKS - 1)
    def _():
        spread(meta[1], term_acc, own_ref, other_ref)


def pair_body(
    length, q_ref, k_ref, v_ref, do_ref, lse_ref, delta_ref, dq_ref, dk_ref, dv_ref, dk_acc, dv_acc, kt_ref
):
    dk_acc[...] = jnp.zeros_like(dk_acc)
    dv_acc[...] = jnp.zeros_like(dv_acc)
    kt_ref[...] = k_ref[...].T

    def block(c):
        here = slice(c * BLOCK, (c + 1) * BLOCK)
        chosen = both_heads(q_ref[here, :])
        grads = both_heads(do_ref[here, :])
        lse = jnp.concatenate([lse_ref[0, 0:1, here], lse_ref[0, 1:2, here]], axis=1)
        delta = jnp.concatenate([delta_ref[0, 0:1, here], delta_ref[0, 1:2, here]], axis=1)
        first = jnp.zeros((64, BLOCK), F32)
        second = jnp.zeros((64, BLOCK), F32)
        for j in range(c + 1):
            keys = slice(j * BLOCK, (j + 1) * BLOCK)
            shares = jnp.exp(dot_nt(k_ref[keys, :], chosen) - lse)
            if j == c:
                shares = jnp.where(causal(shares), shares, 0.0)
            grad_shares = dot_nt(v_ref[keys, :], grads)
            grad_scores = (shares * (grad_shares - delta)).astype(BF16)
            dv_acc[keys, :] += dot(shares.astype(BF16), grads)
            dk_acc[keys, :] += dot(grad_scores, chosen)
            first += dot(kt_ref[0:64, keys], grad_scores[:, :BLOCK])
            second += dot(kt_ref[64:128, keys], grad_scores[:, BLOCK:])
        joined = jnp.concatenate([first, second], axis=0) * 0.125
        dq_ref[here, :] = joined.T.astype(BF16)

    def blank(c):
        here = slice(c * BLOCK, (c + 1) * BLOCK)
        dq_ref[here, :] = jnp.zeros((BLOCK, 128), BF16)

    for c in range(BLOCKS):
        pl.when(length > c * BLOCK)(functools.partial(block, c))
        pl.when(length <= c * BLOCK)(functools.partial(blank, c))
    dk_ref[...] = dk_acc[...].astype(BF16)
    dv_ref[...] = dv_acc[...].astype(BF16)


def pairs_kernel(
    first,
    meta, lengths, q_ref, k_ref, v_ref, do_ref, lse_ref, delta_ref, logit_ref, *refs
):
    prior_ref = refs[0] if first else None
    (
        mixed_far, normed_far, wq_far, wk_far, wv_far, own_ref, other_ref, sums_ref, packet_ref,
        dk_acc, dv_acc, kt_ref, term_ref, grad_ref, mixed_ref, normed_ref, wq_ref, wk_ref, wv_ref, sems,
    ) = refs[1:] if first else refs
    step = pl.program_id(0)
    columns = pl.ds(first * 128, 256)
    far = (mixed_far, normed_far) + tuple(w.at[:, columns] for w in (wq_far, wk_far, wv_far))
    near = (mixed_ref, normed_ref, wq_ref, wk_ref, wv_ref)
    copies = [pltpu.make_async_copy(f, n, sems.at[i]) for i, (f, n) in enumerate(zip(far, near))]

    @pl.when(step == 0)
    def _():
        for copy in copies:
            copy.start()

    _, length = own_sample(meta, lengths)
    pair_body(
        length, q_ref, k_ref, v_ref, do_ref, lse_ref, delta_ref,
        grad_ref.at[0, step], grad_ref.at[1, step], grad_ref.at[2, step], dk_acc, dv_acc, kt_ref,
    )

    @pl.when(step == 1)
    def _():
        for copy in copies:
            copy.wait()
        turned = mixed_ref[...].T
        total = None
        for n, weight in enumerate((wq_ref, wk_ref, wv_ref)):
            rows = jnp.concatenate([grad_ref[n, 0], grad_ref[n, 1]], axis=1)
            term_ref[n * D : (n + 1) * D, :] = dot(turned, rows)
            part = dot_nt(rows, weight[...])
            total = part if total is None else total + part
        spread(meta[1], term_ref, own_ref, other_ref)
        mix = jnp.sum(total, axis=0, keepdims=True)
        gain = jnp.sum(total * normed_ref[...].astype(F32), axis=0, keepdims=True)
        if first:
            mix, gain = mix + prior_ref[0:1, :], gain + prior_ref[1:2, :]
        sums_ref[...] = jnp.concatenate([mix, gain], axis=0)
        logit = logit_ref[...]
        high = logit.astype(BF16).astype(F32)
        lines = [mix[:, n * 128 : (n + 1) * 128] for n in range(4)]
        lines += [gain[:, n * 128 : (n + 1) * 128] for n in range(4)]
        lines += [high, logit - high, jnp.zeros((6, 128), F32)]
        packet_ref[...] = jnp.concatenate(lines, axis=0).astype(BF16)


def piece_kernel(packet_ref, *refs):
    *halves, piece_ref = refs
    for g in range(16):
        start = 0
        for own_ref, got_ref in zip(halves[::2], halves[1::2]):
            count = own_ref.shape[1]
            total = own_ref[g].astype(F32) + got_ref[g].astype(F32)
            piece_ref[g, start : start + count, :] = total.astype(BF16)
            start += count
        piece_ref[g, start:, :] = packet_ref[...]


def exact_dot(a, b):
    return lax.dot_general(
        a, b, (((1,), (0,)), ((), ())),
        precision=lax.Precision.HIGHEST, preferred_element_type=F32,
    )


def sum_kernel(meta, upper_ref, lower_ref, heads_ref, piece_ref):
    upper_packets = [upper_ref[g, 288:, :].astype(F32) for g in range(16)]
    lower_packets = [lower_ref[g, 96:, :].astype(F32) for g in range(16)]

    def pick(packets, row):
        return jnp.concatenate([p[row : row + 1, :] for p in packets], axis=0)

    first = functools.reduce(jnp.add, [upper_ref[g, :288, :].astype(F32) for g in range(16)])
    second = functools.reduce(jnp.add, [lower_ref[g, :96, :].astype(F32) for g in range(16)])
    for n in range(4):
        here = slice(n * 24, (n + 1) * 24)
        rows = jnp.concatenate([first[192:][here], second[here]], axis=0)
        piece_ref[n, :48, :] = rows.astype(BF16)
        rows = jnp.concatenate([first[:96][here], first[96:192][here]], axis=0)
        piece_ref[4 + n, :48, :] = rows.astype(BF16)
    logits = pick(lower_packets, 8) + pick(lower_packets, 9)
    grad_a, grad_c = logits[:, 0:1], logits[:, 1:2]
    lane = lax.broadcasted_iota(jnp.int32, (8, 128), 1)
    line = lax.broadcasted_iota(jnp.int32, (8, 128), 0)
    picks = jnp.where(lane == meta[2] * 8 + line, 1.0, 0.0).astype(BF16)
    dense = [pick(upper_packets, r) for r in range(8)]
    columns = jnp.concatenate([dot_nt(picks, d.astype(BF16)) for d in dense], axis=0)
    flat = [jnp.sum(pick(lower_packets, 4 + r), axis=0, keepdims=True) for r in range(4)]
    gates = []
    for r in range(8):
        lanes = slice(r * 128, (r + 1) * 128)
        gate = (grad_a * heads_ref[0:1, lanes] + grad_c * heads_ref[1:2, lanes]) * dense[r]
        gates.append(gate)
        flat.append(jnp.sum(gate, axis=0, keepdims=True))
    crossed = [pick(upper_packets, 8 + r) for r in range(8)]
    flat += [jnp.sum(d * grad_a, axis=0, keepdims=True) for d in crossed]
    flat += [jnp.sum(d * grad_c, axis=0, keepdims=True) for d in crossed]
    flat = jnp.concatenate(flat + [jnp.zeros((4, 128), F32)], axis=0).astype(BF16)
    products = [exact_dot(columns, gate) for gate in gates]
    products += [exact_dot(columns, pick(lower_packets, r)) for r in range(4)]
    for z in range(8):
        rows = jnp.concatenate([p[z * 8 : (z + 1) * 8, :] for p in products], axis=0)
        piece_ref[z, 48:144, :] = rows.astype(BF16)
        piece_ref[z, 144:176, :] = flat


def final_kernel(meta, got_ref, kept_ref, sent_ref):
    total = functools.reduce(jnp.add, [got_ref[z].astype(F32) for z in range(8)])

    def of_core(core):
        rows = [total[n * 24 + core * 12 : n * 24 + (core + 1) * 12, :] for n in range(2)]
        rows += [total[48 + r * 8 + core * 4 : 52 + r * 8 + core * 4, :] for r in range(12)]
        return jnp.concatenate(rows + [total[144:176, :]], axis=0)

    for core in (0, 1):

        @pl.when(meta[1] == core)
        def _():
            kept_ref[...] = of_core(core)
            sent_ref[...] = of_core(1 - core)


def join_kernel(meta, kept_ref, got_ref, sequence_ref, mix_ref, cross_ref, gain_ref, bias_ref, heads_ref):
    for core in (0, 1):

        @pl.when(meta[1] == core)
        def _():
            for n in range(2):
                for ref, owner in ((kept_ref, core), (got_ref, 1 - core)):
                    start = n * 256 + owner * 128
                    sequence_ref[:, start : start + 128] = ref[n * 12 : (n + 1) * 12, :]

    total = kept_ref[...] + got_ref[...]
    for r in range(8):
        cross_ref[:, r * 128 : (r + 1) * 128] = total[24 + r * 4 : 28 + r * 4, :]
    for r in range(4):
        lanes = slice(r * 128, (r + 1) * 128)
        mix_ref[:, lanes] = total[56 + r * 4 : 60 + r * 4, :]
        gain_ref[:, lanes] = total[72 + r : 73 + r, :]
    for r in range(8):
        lanes = slice(r * 128, (r + 1) * 128)
        bias_ref[:, lanes] = total[76 + r : 77 + r, :]
        heads_ref[0:1, lanes] = total[84 + r : 85 + r, :]
        heads_ref[1:2, lanes] = total[92 + r : 93 + r, :]


def whole(shape):
    return pl.BlockSpec(shape, lambda i, *m: (0,) * len(shape))


def params(megabytes):
    return pltpu.CompilerParams(
        dimension_semantics=("arbitrary",), vmem_limit_bytes=megabytes * 2**20
    )


def cost(flops, moved, exps=0):
    return pl.CostEstimate(flops=flops, bytes_accessed=moved, transcendentals=exps)


def forward(scalars, small, large):
    early = pl.BlockSpec((BLOCK, D), lambda i, *m: (jnp.minimum(i, BLOCKS - 1), 0))
    late = pl.BlockSpec((BLOCK, D), lambda i, *m: (jnp.maximum(i - BLOCKS, 0), 0))
    outs = [((LEN, D), BF16)] * 6 + [
        ((4, 2, LEN), F32), ((4, 2, LEN), F32), ((16, 192, 128), BF16), ((16, 192, 128), BF16),
        ((16, 128), BF16),
        ((1, 128), F32),
    ]
    return pl.pallas_call(
        forward_kernel,
        grid_spec=pltpu.PrefetchScalarGridSpec(
            num_scalar_prefetch=3,
            grid=(2 * BLOCKS,),
            in_specs=[whole(a.shape) for a in small] + [pl.BlockSpec(memory_space=pl.ANY)] * 6,
            out_specs=[early] * 3 + [late] + [early] * 2 + [whole(s) for s, _ in outs[6:]],
            scratch_shapes=[
                pltpu.VMEM((BLOCK + 16, D), BF16),
                pltpu.VMEM((BLOCK, D), BF16),
                pltpu.VMEM((LEN, D), BF16),
                pltpu.VMEM((D, LEN), BF16),
                pltpu.VMEM((LEN, D), BF16),
                pltpu.VMEM((LEN, D), F32),
                pltpu.VMEM((LEN, D), BF16),
                pltpu.VMEM((LEN, DI), F32),
                pltpu.VMEM((1, DI), F32),
                pltpu.VMEM((1, DI), F32),
                pltpu.VMEM((3 * D, D), F32),
            ] + [pltpu.VMEM(a.shape, BF16) for a in large] + [pltpu.SemaphoreType.DMA((6,))],
        ),
        out_shape=[jax.ShapeDtypeStruct(s, t) for s, t in outs],
        compiler_params=params(58),
        cost_estimate=cost(10**10, 2 * 10**7, 10**7),
    )(*scalars, *small, *large)


def pairs_back(scalars, first, queries, keys, values, grads, lse, delta, logit, *far):
    prior = [whole((2, D))] if first else []
    lanes = pl.BlockSpec((LEN, 128), lambda i, *m: (0, first + i))
    pair = pl.BlockSpec((1, 2, LEN), lambda i, *m: (first + i, 0, 0))
    outs = [((16, 96, 128), BF16), ((16, 96, 128), BF16), ((2, D), F32), ((16, 128), BF16)]
    return pl.pallas_call(
        functools.partial(pairs_kernel, first),
        grid_spec=pltpu.PrefetchScalarGridSpec(
            num_scalar_prefetch=2,
            grid=(2,),
            in_specs=[lanes] * 4 + [pair] * 2 + [whole(logit.shape)]
            + prior + [pl.BlockSpec(memory_space=pl.ANY)] * 5,
            out_specs=[whole(s) for s, _ in outs],
            scratch_shapes=[
                pltpu.VMEM((LEN, 128), F32),
                pltpu.VMEM((LEN, 128), F32),
                pltpu.VMEM((128, LEN), BF16),
                pltpu.VMEM((3 * D, 256), F32),
                pltpu.VMEM((3, 2, LEN, 128), BF16),
                pltpu.VMEM((LEN, D), BF16),
                pltpu.VMEM((LEN, D), BF16),
            ] + [pltpu.VMEM((D, 256), BF16)] * 3 + [pltpu.SemaphoreType.DMA((5,))],
        ),
        out_shape=[jax.ShapeDtypeStruct(s, t) for s, t in outs],
        compiler_params=params(60),
        cost_estimate=cost(10**10, 10**7, 4 * 10**6),
    )(*scalars, queries, keys, values, grads, lse, delta, logit, *far)


def cut_pieces(packet, *halves):
    count = sum(h.shape[1] for h in halves[::2]) + packet.shape[0]
    return pl.pallas_call(
        piece_kernel,
        out_shape=jax.ShapeDtypeStruct((16, count, 128), BF16),
        compiler_params=pltpu.CompilerParams(vmem_limit_bytes=16 * 2**20),
        cost_estimate=cost(10**6, 3 * 10**6),
    )(packet, *halves)


def sum_pieces(meta, upper, lower, heads):
    return pl.pallas_call(
        sum_kernel,
        grid_spec=pltpu.PrefetchScalarGridSpec(
            num_scalar_prefetch=1,
            grid=(1,),
            in_specs=[whole(a.shape) for a in (upper, lower, heads)],
            out_specs=whole((8, 176, 128)),
        ),
        out_shape=jax.ShapeDtypeStruct((8, 176, 128), BF16),
        compiler_params=params(16),
        cost_estimate=cost(10**7, 2 * 10**6),
    )(meta, upper, lower, heads)


def total_rows(meta, got):
    outs = ((104, 128),) * 2
    return pl.pallas_call(
        final_kernel,
        grid_spec=pltpu.PrefetchScalarGridSpec(
            num_scalar_prefetch=1,
            grid=(1,),
            in_specs=[whole(got.shape)],
            out_specs=[whole(s) for s in outs],
        ),
        out_shape=[jax.ShapeDtypeStruct(s, F32) for s in outs],
        compiler_params=params(16),
        cost_estimate=cost(10**6, 10**6),
    )(meta, got)


def join(meta, *args):
    outs = ((12, D), (4, D), (4, DI), (1, D), (1, DI), (2, DI))
    return pl.pallas_call(
        join_kernel,
        grid_spec=pltpu.PrefetchScalarGridSpec(
            num_scalar_prefetch=1,
            grid=(1,),
            in_specs=[whole(a.shape) for a in args],
            out_specs=[whole(s) for s in outs],
        ),
        out_shape=[jax.ShapeDtypeStruct(s, F32) for s in outs],
        compiler_params=params(16),
        cost_estimate=cost(10**5, 10**5),
    )(meta, *args)


def to_samples(event_ids, event_side, me):
    codes = jnp.concatenate([event_ids // 256, event_ids % 256], axis=1).astype(BF16)
    codes = jnp.concatenate([codes[:, None], jnp.zeros((SAMPLES, 15, D), BF16)], axis=1)

    def part(sample):
        sample = jnp.minimum(sample, SAMPLES - 1)
        side = lax.dynamic_index_in_dim(event_side, sample, 0, keepdims=False)
        code = lax.dynamic_index_in_dim(codes, sample, 0, keepdims=False)
        return jnp.concatenate([side, code])

    got = [part(me)]
    for k in (1, 2, 3):
        pairs = [(i, (i + k) % 4) for i in range(4) if (i + k) % 4 < SAMPLES]
        got.append(lax.ppermute(part((me + k) % 4), CTX, pairs))
    return got


def swap_cores(value):
    return lax.ppermute(value, "core", [(0, 1), (1, 0)])


def per_device(
    event_ids, lengths, event_side, dense_input, labels, event_table, seq_gain, w_mix, w_query,
    w_key, w_value, w_out, w_pool, w_cross, b_cross, w_heads,
):
    me = lax.axis_index(CTX)
    own = jnp.minimum(me, SAMPLES - 1)
    parts = to_samples(event_ids, event_side, me)
    device = np.arange(256)
    places = np.stack([device % 4, device % 2, device // 2 % 16] + [0 * device] * 5, axis=1)
    meta = jnp.asarray(places, jnp.int32)[lax.axis_index(("z", "ylo", "x") + CTX)]
    dense = lax.dynamic_slice_in_dim(dense_input, own, 1, 0)
    mix_row = dot(dense, w_mix)
    base = dot(dense, w_cross)
    heads = w_heads.T
    (queries, keys, values, grads, mixed, normed, lse, delta, own, other, packet, logit) = forward(
        (meta, lengths, labels),
        (*parts, mix_row, seq_gain[None], base, b_cross[None], dense, heads),
        (event_table, w_query, w_key, w_value, w_out, w_pool),
    )
    got = swap_cores(other)
    attention = (queries, keys, values, grads, lse, delta, logit)
    rest = (mixed, normed, w_query, w_key, w_value)
    own_first, other_first, sums, _ = pairs_back((meta, lengths), 0, *attention, *rest)
    got, other_first = lax.optimization_barrier((got, other_first))
    pieces = cut_pieces(packet, own, got, own_first, swap_cores(other_first))
    pieces, attention = lax.optimization_barrier((pieces, attention))
    upper_plane = lax.all_to_all(pieces, PLANE, 0, 0)
    own, other, _, packet = pairs_back((meta, lengths), 2, *attention, sums, *rest)
    pieces = cut_pieces(packet, own, swap_cores(other))
    upper_plane, pieces = lax.optimization_barrier((upper_plane, pieces))
    lower_plane = lax.all_to_all(pieces, PLANE, 0, 0)
    got = lax.all_to_all(sum_pieces(meta, upper_plane, lower_plane, heads), "z", 0, 0)
    kept, sent = total_rows(meta, got)
    sequence, mix, cross, gain, bias, grad_heads = join(meta, kept, swap_cores(sent))
    return (sequence, mix, cross, gain.reshape(D), bias.reshape(DI), grad_heads.T)


def solution(mesh):
    fine = Mesh(mesh.devices.reshape(8, 2, 4, 2, 2), ("z", "ylo", "x", "yhi", "core"))
    dp = ("z", "ylo", "x")
    every = dp + CTX
    in_specs = (P(dp, CTX), P(dp), P(dp, CTX, None), P(dp, None), P(dp, None)) + (P(),) * 11
    out_specs = (P(every, None), P(every, None), P(every, None), P(), P(), P())
    return jax.shard_map(
        per_device, mesh=fine, in_specs=in_specs, out_specs=out_specs, check_vma=False
    )
```

```python
import functools

import jax
import jax.numpy as jnp
import numpy as np
from jax import lax
from jax.experimental import pallas as pl
from jax.experimental.pallas import tpu as pltpu
from jax.sharding import Mesh, PartitionSpec as P

HEADS = 8
BATCH = 192
SAMPLES = 3
BLOCK = 256
BLOCKS = 4
LEN = 1024
D = 512
DI = 1024
VOCAB = 2048
MASKED = -1e30
EPSILON = 1e-06
LOSS_SCALE = 32768.0
F32 = jnp.float32
BF16 = jnp.bfloat16
CTX = ("yhi", "core")
PLANE = ("ylo", "x", "yhi")


def dot(a, b):
    return lax.dot_general(a, b, (((1,), (0,)), ((), ())), preferred_element_type=F32)


def dot_nt(a, b):
    return lax.dot_general(a, b, (((1,), (1,)), ((), ())), preferred_element_type=F32)


def dot_tn(a, b):
    return lax.dot_general(a, b, (((0,), (0,)), ((), ())), preferred_element_type=F32)


def both_heads(rows):
    low = lax.broadcasted_iota(jnp.int32, rows.shape, 1) < 64
    zero = jnp.zeros_like(rows)
    return jnp.concatenate([jnp.where(low, rows, zero), jnp.where(low, zero, rows)], axis=0)


def causal(tile):
    key = lax.broadcasted_iota(jnp.int32, tile.shape, 0)
    query = lax.broadcasted_iota(jnp.int32, tile.shape, 1) & (BLOCK - 1)
    return key <= query


def spread(core, acc_ref, own_ref, other_ref):
    for mine in (0, 1):

        @pl.when(core == mine)
        def _():
            for block in range(acc_ref.shape[1] // 128):
                target = own_ref if block % 2 == mine else other_ref
                lanes = slice(block * 128, (block + 1) * 128)
                place = slice(block // 2 * 96, (block // 2 + 1) * 96)
                for g in range(16):
                    rows = [acc_ref[n * 384 + g * 24 : n * 384 + (g + 1) * 24, lanes] for n in range(4)]
                    target[g, place, :] = jnp.concatenate(rows, axis=0).astype(BF16)


def own_sample(meta, lengths):
    own = jnp.minimum(meta[0], SAMPLES - 1)
    return own, jnp.where(meta[0] < SAMPLES, lengths[own], 0)


def forward_kernel(
    meta, lengths, labels, part0, part1, part2, part3, mix_ref, gain_ref, base_ref, bias_ref, dense_ref, heads_ref,
    table_far, wq_far, wk_far, wv_far, wo_far, wp_far,
    q_ref, k_ref, v_ref, do_ref, mixed_ref, normed_ref, lse_ref, delta_ref, own_ref, other_ref,
    packet_ref, logit_ref,
    part_ref, q_all, k_all, vt_ref, att_ref, o_ref, res_ref, pre_ref, sum_ref, scaled_ref,
    term_acc, table_ref, wq_ref, wk_ref, wv_ref, wo_ref, wp_ref, sems,
):
    far = (table_far, wq_far, wk_far, wv_far, wo_far, wp_far)
    near = (table_ref, wq_ref, wk_ref, wv_ref, wo_ref, wp_ref)
    copies = [pltpu.make_async_copy(f, n, sems.at[i]) for i, (f, n) in enumerate(zip(far, near))]
    step = pl.program_id(0)
    own, length = own_sample(meta, lengths)

    @pl.when(step == 0)
    def _():
        for copy in copies[:4]:
            copy.start()
        sum_ref[...] = jnp.zeros_like(sum_ref)
        term_acc[...] = jnp.zeros_like(term_acc)

    source = lax.rem(meta[0] - jnp.minimum(step, BLOCKS - 1) + BLOCKS, BLOCKS)
    for n, ref in enumerate((part0, part1, part2, part3)):

        @pl.when((step < BLOCKS) & (source == n))
        def _():
            part_ref[...] = ref[...]

    def ahead(c):
        here = slice(c * BLOCK, (c + 1) * BLOCK)
        codes = part_ref[BLOCK:, :].astype(F32)
        ids = (codes[:, :BLOCK] * 256.0 + codes[:, BLOCK:]).T[:, 0:1].astype(jnp.int32)
        slots = lax.broadcasted_iota(jnp.int32, (BLOCK, VOCAB), 1)
        picked = jnp.where(slots == ids, 1.0, 0.0).astype(BF16)
        if c == 0:
            copies[0].wait()
            for copy in copies[4:]:
                copy.start()
        tokens = dot(picked, table_ref[...]) + part_ref[:BLOCK, :].astype(F32)
        mean = jnp.mean(tokens * tokens, axis=1, keepdims=True)
        normed = tokens * lax.rsqrt(mean + EPSILON)
        normed_ref[...] = normed.astype(BF16)
        mixed = (normed * gain_ref[...] + mix_ref[...]).astype(BF16)
        mixed_ref[...] = mixed
        if c == 0:
            for copy in copies[1:4]:
                copy.wait()
        queries = (dot(mixed, wq_ref[...]).astype(BF16).astype(F32) * 0.125).astype(BF16)
        q_ref[...] = queries
        q_all[...] = queries
        keys_now = dot(mixed, wk_ref[...]).astype(BF16)
        k_ref[...] = keys_now
        k_all[here, :] = keys_now
        values = dot(mixed, wv_ref[...]).astype(BF16)
        v_ref[...] = values
        vt_ref[:, here] = values.T
        for p in range(4):
            lanes = slice(p * 128, (p + 1) * 128)
            chosen = both_heads(q_all[:, lanes])
            tiles = []
            for j in range(c + 1):
                tile = dot_nt(k_all[j * BLOCK : (j + 1) * BLOCK, lanes], chosen)
                if j == c:
                    tile = jnp.where(causal(tile), tile, MASKED)
                tiles.append(tile)
            top = functools.reduce(jnp.maximum, [jnp.max(t, axis=0, keepdims=True) for t in tiles])
            raised = [jnp.exp(t - top) for t in tiles]
            total = functools.reduce(jnp.add, [jnp.sum(t, axis=0, keepdims=True) for t in raised])
            inverse = 1.0 / total
            shares = [(t * inverse).astype(BF16) for t in raised]
            lse = top + jnp.log(total)
            lse_ref[p, 0:1, here] = lse[:, :BLOCK]
            lse_ref[p, 1:2, here] = lse[:, BLOCK:]
            first = jnp.zeros((64, BLOCK), F32)
            second = jnp.zeros((64, BLOCK), F32)
            for j in range(c + 1):
                keys = slice(j * BLOCK, (j + 1) * BLOCK)
                first += dot(vt_ref[p * 128 : p * 128 + 64, keys], shares[j][:, :BLOCK])
                second += dot(vt_ref[p * 128 + 64 : p * 128 + 128, keys], shares[j][:, BLOCK:])
            joined = jnp.concatenate([first, second], axis=0).T
            o_ref[here, lanes] = joined
            att_ref[here, lanes] = joined.astype(BF16)
        if c == 0:
            for copy in copies[4:]:
                copy.wait()
        residual = tokens + dot(att_ref[here, :], wo_ref[...])
        half = residual.astype(BF16)
        res_ref[here, :] = half
        pre = dot(half, wp_ref[...])
        pre_ref[here, :] = pre
        valid = (c * BLOCK + lax.broadcasted_iota(jnp.int32, pre.shape, 0)) < length
        silu = jnp.where(valid, pre * jax.nn.sigmoid(pre), 0.0)
        sum_ref[...] += jnp.sum(silu, axis=0, keepdims=True)

    def blank(c):
        if c == 0:
            for copy in copies[4:]:
                copy.start()
            for copy in copies:
                copy.wait()
        here = slice(c * BLOCK, (c + 1) * BLOCK)
        for ref in (q_ref, k_ref, v_ref, mixed_ref, normed_ref):
            ref[...] = jnp.zeros((BLOCK, D), ref.dtype)
        lse_ref[:, :, here] = jnp.zeros((4, 2, BLOCK), F32)
        delta_ref[:, :, here] = jnp.zeros((4, 2, BLOCK), F32)

    for c in range(BLOCKS):
        pl.when((step == c) & (length > c * BLOCK))(functools.partial(ahead, c))
        pl.when((step == c) & (length <= c * BLOCK))(functools.partial(blank, c))

    @pl.when(step == BLOCKS)
    def _():
        span = jnp.maximum(length, 1).astype(F32)
        dense = dense_ref[...].astype(F32)
        gate = base_ref[...] + bias_ref[...] + sum_ref[...] / span
        crossed = dense + dense * gate
        rows = [dense[:, n * 128 : (n + 1) * 128] for n in range(8)]
        rows += [crossed[:, n * 128 : (n + 1) * 128] for n in range(8)]
        packet_ref[...] = jnp.concatenate(rows, axis=0).astype(BF16)
        a = jnp.sum(crossed * heads_ref[0:1, :], axis=1, keepdims=True)
        c = jnp.sum(crossed * heads_ref[1:2, :], axis=1, keepdims=True)
        clicked = labels[own, 0].astype(F32)
        converted = (labels[own, 0] * labels[own, 1]).astype(F32)
        top = jnp.maximum(jnp.maximum(a, c), 0.0)
        ea, ec = jnp.exp(a - top), jnp.exp(c - top)
        below = jnp.exp(-top) + ea + ec
        grad_a = jax.nn.sigmoid(a) - clicked - converted * jax.nn.sigmoid(-a)
        grad_a = grad_a - (1.0 - converted) * (ea / below - jax.nn.sigmoid(a))
        grad_c = -converted * jax.nn.sigmoid(-c)
        grad_c = grad_c - (1.0 - converted) * (ec / below - jax.nn.sigmoid(c))
        factor = jnp.where(length > 0, LOSS_SCALE / BATCH, 0.0)
        grad_a = grad_a * factor
        grad_c = grad_c * factor
        lane = lax.broadcasted_iota(jnp.int32, (1, 128), 1)
        logit_ref[...] = jnp.where(lane == 0, grad_a, jnp.where(lane == 1, grad_c, 0.0))
        grad_gate = (grad_a * heads_ref[0:1, :] + grad_c * heads_ref[1:2, :]) * dense
        scaled_ref[...] = grad_gate / span

    def back(c):
        here = slice(c * BLOCK, (c + 1) * BLOCK)
        pre = pre_ref[here, :]
        sig = jax.nn.sigmoid(pre)
        valid = (c * BLOCK + lax.broadcasted_iota(jnp.int32, pre.shape, 0)) < length
        slope = sig * (1.0 + pre * (1.0 - sig)) * scaled_ref[...]
        grad_pre = jnp.where(valid, slope, 0.0).astype(BF16)
        term_acc[D:, :] += dot_tn(grad_pre, res_ref[here, :])
        grad_res = dot_nt(grad_pre, wp_ref[...]).astype(BF16)
        term_acc[:D, :] += dot_tn(att_ref[here, :], grad_res)
        grad_att = dot_nt(grad_res, wo_ref[...]).astype(BF16)
        do_ref[...] = grad_att
        product = grad_att.astype(F32) * o_ref[here, :]
        head = lax.broadcasted_iota(jnp.int32, (HEADS, D), 0)
        column = lax.broadcasted_iota(jnp.int32, (HEADS, D), 1) // 64
        picks = jnp.where(head == column, 1.0, 0.0).astype(BF16)
        high = product.astype(BF16)
        low = (product - high.astype(F32)).astype(BF16)
        delta = dot_nt(picks, high) + dot_nt(picks, low)
        for p in range(4):
            delta_ref[p, :, here] = delta[2 * p : 2 * p + 2, :]

    def quiet():
        do_ref[...] = jnp.zeros((BLOCK, D), BF16)

    for c in range(BLOCKS):
        pl.when((step == BLOCKS + c) & (length > c * BLOCK))(functools.partial(back, c))
        pl.when((step == BLOCKS + c) & (length <= c * BLOCK))(quiet)

    @pl.when(step == 2 * BLOCKS - 1)
    def _():
        spread(meta[1], term_acc, own_ref, other_ref)


def pair_body(
    length, q_ref, k_ref, v_ref, do_ref, lse_ref, delta_ref, dq_ref, dk_ref, dv_ref, dk_acc, dv_acc, kt_ref
):
    dk_acc[...] = jnp.zeros_like(dk_acc)
    dv_acc[...] = jnp.zeros_like(dv_acc)
    kt_ref[...] = k_ref[...].T

    def block(c):
        here = slice(c * BLOCK, (c + 1) * BLOCK)
        chosen = both_heads(q_ref[here, :])
        grads = both_heads(do_ref[here, :])
        lse = jnp.concatenate([lse_ref[0, 0:1, here], lse_ref[0, 1:2, here]], axis=1)
        delta = jnp.concatenate([delta_ref[0, 0:1, here], delta_ref[0, 1:2, here]], axis=1)
        first = jnp.zeros((64, BLOCK), F32)
        second = jnp.zeros((64, BLOCK), F32)
        for j in range(c + 1):
            keys = slice(j * BLOCK, (j + 1) * BLOCK)
            shares = jnp.exp(dot_nt(k_ref[keys, :], chosen) - lse)
            if j == c:
                shares = jnp.where(causal(shares), shares, 0.0)
            grad_shares = dot_nt(v_ref[keys, :], grads)
            grad_scores = (shares * (grad_shares - delta)).astype(BF16)
            dv_acc[keys, :] += dot(shares.astype(BF16), grads)
            dk_acc[keys, :] += dot(grad_scores, chosen)
            first += dot(kt_ref[0:64, keys], grad_scores[:, :BLOCK])
            second += dot(kt_ref[64:128, keys], grad_scores[:, BLOCK:])
        joined = jnp.concatenate([first, second], axis=0) * 0.125
        dq_ref[here, :] = joined.T.astype(BF16)

    def blank(c):
        here = slice(c * BLOCK, (c + 1) * BLOCK)
        dq_ref[here, :] = jnp.zeros((BLOCK, 128), BF16)

    for c in range(BLOCKS):
        pl.when(length > c * BLOCK)(functools.partial(block, c))
        pl.when(length <= c * BLOCK)(functools.partial(blank, c))
    dk_ref[...] = dk_acc[...].astype(BF16)
    dv_ref[...] = dv_acc[...].astype(BF16)


def pairs_kernel(
    first,
    meta, lengths, q_ref, k_ref, v_ref, do_ref, lse_ref, delta_ref, logit_ref, *refs
):
    prior_ref = refs[0] if first else None
    (
        mixed_far, normed_far, wq_far, wk_far, wv_far, own_ref, other_ref, sums_ref, packet_ref,
        dk_acc, dv_acc, kt_ref, term_ref, grad_ref, mixed_ref, normed_ref, wq_ref, wk_ref, wv_ref, sems,
    ) = refs[1:] if first else refs
    step = pl.program_id(0)
    columns = pl.ds(first * 128, 256)
    far = (mixed_far, normed_far) + tuple(w.at[:, columns] for w in (wq_far, wk_far, wv_far))
    near = (mixed_ref, normed_ref, wq_ref, wk_ref, wv_ref)
    copies = [pltpu.make_async_copy(f, n, sems.at[i]) for i, (f, n) in enumerate(zip(far, near))]

    @pl.when(step == 0)
    def _():
        for copy in copies:
            copy.start()

    _, length = own_sample(meta, lengths)
    pair_body(
        length, q_ref, k_ref, v_ref, do_ref, lse_ref, delta_ref,
        grad_ref.at[0, step], grad_ref.at[1, step], grad_ref.at[2, step], dk_acc, dv_acc, kt_ref,
    )

    @pl.when(step == 1)
    def _():
        for copy in copies:
            copy.wait()
        turned = mixed_ref[...].T
        total = None
        for n, weight in enumerate((wq_ref, wk_ref, wv_ref)):
            rows = jnp.concatenate([grad_ref[n, 0], grad_ref[n, 1]], axis=1)
            term_ref[n * D : (n + 1) * D, :] = dot(turned, rows)
            part = dot_nt(rows, weight[...])
            total = part if total is None else total + part
        spread(meta[1], term_ref, own_ref, other_ref)
        mix = jnp.sum(total, axis=0, keepdims=True)
        gain = jnp.sum(total * normed_ref[...].astype(F32), axis=0, keepdims=True)
        if first:
            mix, gain = mix + prior_ref[0:1, :], gain + prior_ref[1:2, :]
        sums_ref[...] = jnp.concatenate([mix, gain], axis=0)
        logit = logit_ref[...]
        high = logit.astype(BF16).astype(F32)
        lines = [mix[:, n * 128 : (n + 1) * 128] for n in range(4)]
        lines += [gain[:, n * 128 : (n + 1) * 128] for n in range(4)]
        lines += [high, logit - high, jnp.zeros((6, 128), F32)]
        packet_ref[...] = jnp.concatenate(lines, axis=0).astype(BF16)


def piece_kernel(packet_ref, *refs):
    *halves, piece_ref = refs
    for g in range(16):
        start = 0
        for own_ref, got_ref in zip(halves[::2], halves[1::2]):
            count = own_ref.shape[1]
            total = own_ref[g].astype(F32) + got_ref[g].astype(F32)
            piece_ref[g, start : start + count, :] = total.astype(BF16)
            start += count
        piece_ref[g, start:, :] = packet_ref[...]


def exact_dot(a, b):
    return lax.dot_general(
        a, b, (((1,), (0,)), ((), ())),
        precision=lax.Precision.HIGHEST, preferred_element_type=F32,
    )


def sum_kernel(meta, upper_ref, lower_ref, heads_ref, piece_ref):
    upper_packets = [upper_ref[g, 288:, :].astype(F32) for g in range(16)]
    lower_packets = [lower_ref[g, 96:, :].astype(F32) for g in range(16)]

    def pick(packets, row):
        return jnp.concatenate([p[row : row + 1, :] for p in packets], axis=0)

    first = functools.reduce(jnp.add, [upper_ref[g, :288, :].astype(F32) for g in range(16)])
    second = functools.reduce(jnp.add, [lower_ref[g, :96, :].astype(F32) for g in range(16)])
    for n in range(4):
        here = slice(n * 24, (n + 1) * 24)
        rows = jnp.concatenate([first[192:][here], second[here]], axis=0)
        piece_ref[n, :48, :] = rows.astype(BF16)
        rows = jnp.concatenate([first[:96][here], first[96:192][here]], axis=0)
        piece_ref[4 + n, :48, :] = rows.astype(BF16)
    logits = pick(lower_packets, 8) + pick(lower_packets, 9)
    grad_a, grad_c = logits[:, 0:1], logits[:, 1:2]
    lane = lax.broadcasted_iota(jnp.int32, (8, 128), 1)
    line = lax.broadcasted_iota(jnp.int32, (8, 128), 0)
    picks = jnp.where(lane == meta[2] * 8 + line, 1.0, 0.0).astype(BF16)
    dense = [pick(upper_packets, r) for r in range(8)]
    columns = jnp.concatenate([dot_nt(picks, d.astype(BF16)) for d in dense], axis=0)
    flat = [jnp.sum(pick(lower_packets, 4 + r), axis=0, keepdims=True) for r in range(4)]
    gates = []
    for r in range(8):
        lanes = slice(r * 128, (r + 1) * 128)
        gate = (grad_a * heads_ref[0:1, lanes] + grad_c * heads_ref[1:2, lanes]) * dense[r]
        gates.append(gate)
        flat.append(jnp.sum(gate, axis=0, keepdims=True))
    crossed = [pick(upper_packets, 8 + r) for r in range(8)]
    flat += [jnp.sum(d * grad_a, axis=0, keepdims=True) for d in crossed]
    flat += [jnp.sum(d * grad_c, axis=0, keepdims=True) for d in crossed]
    flat = jnp.concatenate(flat + [jnp.zeros((4, 128), F32)], axis=0).astype(BF16)
    products = [exact_dot(columns, gate) for gate in gates]
    products += [exact_dot(columns, pick(lower_packets, r)) for r in range(4)]
    for z in range(8):
        rows = jnp.concatenate([p[z * 8 : (z + 1) * 8, :] for p in products], axis=0)
        piece_ref[z, 48:144, :] = rows.astype(BF16)
        piece_ref[z, 144:176, :] = flat


def final_kernel(meta, got_ref, kept_ref, sent_ref):
    total = functools.reduce(jnp.add, [got_ref[z].astype(F32) for z in range(8)])

    def of_core(core):
        rows = [total[n * 24 + core * 12 : n * 24 + (core + 1) * 12, :] for n in range(2)]
        rows += [total[48 + r * 8 + core * 4 : 52 + r * 8 + core * 4, :] for r in range(12)]
        return jnp.concatenate(rows + [total[144:176, :]], axis=0)

    for core in (0, 1):

        @pl.when(meta[1] == core)
        def _():
            kept_ref[...] = of_core(core)
            sent_ref[...] = of_core(1 - core)


def join_kernel(meta, kept_ref, got_ref, sequence_ref, mix_ref, cross_ref, gain_ref, bias_ref, heads_ref):
    for core in (0, 1):

        @pl.when(meta[1] == core)
        def _():
            for n in range(2):
                for ref, owner in ((kept_ref, core), (got_ref, 1 - core)):
                    start = n * 256 + owner * 128
                    sequence_ref[:, start : start + 128] = ref[n * 12 : (n + 1) * 12, :]

    total = kept_ref[...] + got_ref[...]
    for r in range(8):
        cross_ref[:, r * 128 : (r + 1) * 128] = total[24 + r * 4 : 28 + r * 4, :]
    for r in range(4):
        lanes = slice(r * 128, (r + 1) * 128)
        mix_ref[:, lanes] = total[56 + r * 4 : 60 + r * 4, :]
        gain_ref[:, lanes] = total[72 + r : 73 + r, :]
    for r in range(8):
        lanes = slice(r * 128, (r + 1) * 128)
        bias_ref[:, lanes] = total[76 + r : 77 + r, :]
        heads_ref[0:1, lanes] = total[84 + r : 85 + r, :]
        heads_ref[1:2, lanes] = total[92 + r : 93 + r, :]


def whole(shape):
    return pl.BlockSpec(shape, lambda i, *m: (0,) * len(shape))


def params(megabytes):
    return pltpu.CompilerParams(
        dimension_semantics=("arbitrary",), vmem_limit_bytes=megabytes * 2**20
    )


def cost(flops, moved, exps=0):
    return pl.CostEstimate(flops=flops, bytes_accessed=moved, transcendentals=exps)


def forward(scalars, small, large):
    early = pl.BlockSpec((BLOCK, D), lambda i, *m: (jnp.minimum(i, BLOCKS - 1), 0))
    late = pl.BlockSpec((BLOCK, D), lambda i, *m: (jnp.maximum(i - BLOCKS, 0), 0))
    outs = [((LEN, D), BF16)] * 6 + [
        ((4, 2, LEN), F32), ((4, 2, LEN), F32), ((16, 192, 128), BF16), ((16, 192, 128), BF16),
        ((16, 128), BF16),
        ((1, 128), F32),
    ]
    return pl.pallas_call(
        forward_kernel,
        grid_spec=pltpu.PrefetchScalarGridSpec(
            num_scalar_prefetch=3,
            grid=(2 * BLOCKS,),
            in_specs=[whole(a.shape) for a in small] + [pl.BlockSpec(memory_space=pl.ANY)] * 6,
            out_specs=[early] * 3 + [late] + [early] * 2 + [whole(s) for s, _ in outs[6:]],
            scratch_shapes=[
                pltpu.VMEM((BLOCK + 16, D), BF16),
                pltpu.VMEM((BLOCK, D), BF16),
                pltpu.VMEM((LEN, D), BF16),
                pltpu.VMEM((D, LEN), BF16),
                pltpu.VMEM((LEN, D), BF16),
                pltpu.VMEM((LEN, D), F32),
                pltpu.VMEM((LEN, D), BF16),
                pltpu.VMEM((LEN, DI), F32),
                pltpu.VMEM((1, DI), F32),
                pltpu.VMEM((1, DI), F32),
                pltpu.VMEM((3 * D, D), F32),
            ] + [pltpu.VMEM(a.shape, BF16) for a in large] + [pltpu.SemaphoreType.DMA((6,))],
        ),
        out_shape=[jax.ShapeDtypeStruct(s, t) for s, t in outs],
        compiler_params=params(58),
        cost_estimate=cost(10**10, 2 * 10**7, 10**7),
    )(*scalars, *small, *large)


def pairs_back(scalars, first, queries, keys, values, grads, lse, delta, logit, *far):
    prior = [whole((2, D))] if first else []
    lanes = pl.BlockSpec((LEN, 128), lambda i, *m: (0, first + i))
    pair = pl.BlockSpec((1, 2, LEN), lambda i, *m: (first + i, 0, 0))
    outs = [((16, 96, 128), BF16), ((16, 96, 128), BF16), ((2, D), F32), ((16, 128), BF16)]
    return pl.pallas_call(
        functools.partial(pairs_kernel, first),
        grid_spec=pltpu.PrefetchScalarGridSpec(
            num_scalar_prefetch=2,
            grid=(2,),
            in_specs=[lanes] * 4 + [pair] * 2 + [whole(logit.shape)]
            + prior + [pl.BlockSpec(memory_space=pl.ANY)] * 5,
            out_specs=[whole(s) for s, _ in outs],
            scratch_shapes=[
                pltpu.VMEM((LEN, 128), F32),
                pltpu.VMEM((LEN, 128), F32),
                pltpu.VMEM((128, LEN), BF16),
                pltpu.VMEM((3 * D, 256), F32),
                pltpu.VMEM((3, 2, LEN, 128), BF16),
                pltpu.VMEM((LEN, D), BF16),
                pltpu.VMEM((LEN, D), BF16),
            ] + [pltpu.VMEM((D, 256), BF16)] * 3 + [pltpu.SemaphoreType.DMA((5,))],
        ),
        out_shape=[jax.ShapeDtypeStruct(s, t) for s, t in outs],
        compiler_params=params(60),
        cost_estimate=cost(10**10, 10**7, 4 * 10**6),
    )(*scalars, queries, keys, values, grads, lse, delta, logit, *far)


def cut_pieces(packet, *halves):
    count = sum(h.shape[1] for h in halves[::2]) + packet.shape[0]
    return pl.pallas_call(
        piece_kernel,
        out_shape=jax.ShapeDtypeStruct((16, count, 128), BF16),
        compiler_params=pltpu.CompilerParams(vmem_limit_bytes=16 * 2**20),
        cost_estimate=cost(10**6, 3 * 10**6),
    )(packet, *halves)


def sum_pieces(meta, upper, lower, heads):
    return pl.pallas_call(
        sum_kernel,
        grid_spec=pltpu.PrefetchScalarGridSpec(
            num_scalar_prefetch=1,
            grid=(1,),
            in_specs=[whole(a.shape) for a in (upper, lower, heads)],
            out_specs=whole((8, 176, 128)),
        ),
        out_shape=jax.ShapeDtypeStruct((8, 176, 128), BF16),
        compiler_params=params(16),
        cost_estimate=cost(10**7, 2 * 10**6),
    )(meta, upper, lower, heads)


def total_rows(meta, got):
    outs = ((104, 128),) * 2
    return pl.pallas_call(
        final_kernel,
        grid_spec=pltpu.PrefetchScalarGridSpec(
            num_scalar_prefetch=1,
            grid=(1,),
            in_specs=[whole(got.shape)],
            out_specs=[whole(s) for s in outs],
        ),
        out_shape=[jax.ShapeDtypeStruct(s, F32) for s in outs],
        compiler_params=params(16),
        cost_estimate=cost(10**6, 10**6),
    )(meta, got)


def join(meta, *args):
    outs = ((12, D), (4, D), (4, DI), (1, D), (1, DI), (2, DI))
    return pl.pallas_call(
        join_kernel,
        grid_spec=pltpu.PrefetchScalarGridSpec(
            num_scalar_prefetch=1,
            grid=(1,),
            in_specs=[whole(a.shape) for a in args],
            out_specs=[whole(s) for s in outs],
        ),
        out_shape=[jax.ShapeDtypeStruct(s, F32) for s in outs],
        compiler_params=params(16),
        cost_estimate=cost(10**5, 10**5),
    )(meta, *args)


def to_samples(event_ids, event_side, me):
    codes = jnp.concatenate([event_ids // 256, event_ids % 256], axis=1).astype(BF16)
    codes = jnp.concatenate([codes[:, None], jnp.zeros((SAMPLES, 15, D), BF16)], axis=1)

    def part(sample):
        sample = jnp.minimum(sample, SAMPLES - 1)
        side = lax.dynamic_index_in_dim(event_side, sample, 0, keepdims=False)
        code = lax.dynamic_index_in_dim(codes, sample, 0, keepdims=False)
        return jnp.concatenate([side, code])

    got = [part(me)]
    for k in (1, 2, 3):
        pairs = [(i, (i + k) % 4) for i in range(4) if (i + k) % 4 < SAMPLES]
        got.append(lax.ppermute(part((me + k) % 4), CTX, pairs))
    return got


def swap_cores(value):
    return lax.ppermute(value, "core", [(0, 1), (1, 0)])


def per_device(
    event_ids, lengths, event_side, dense_input, labels, event_table, seq_gain, w_mix, w_query,
    w_key, w_value, w_out, w_pool, w_cross, b_cross, w_heads,
):
    me = lax.axis_index(CTX)
    own = jnp.minimum(me, SAMPLES - 1)
    parts = to_samples(event_ids, event_side, me)
    device = np.arange(256)
    places = np.stack([device % 4, device % 2, device // 2 % 16] + [0 * device] * 5, axis=1)
    meta = jnp.asarray(places, jnp.int32)[lax.axis_index(("z", "ylo", "x") + CTX)]
    dense = lax.dynamic_slice_in_dim(dense_input, own, 1, 0)
    mix_row = dot(dense, w_mix)
    base = dot(dense, w_cross)
    heads = w_heads.T
    (queries, keys, values, grads, mixed, normed, lse, delta, own, other, packet, logit) = forward(
        (meta, lengths, labels),
        (*parts, mix_row, seq_gain[None], base, b_cross[None], dense, heads),
        (event_table, w_query, w_key, w_value, w_out, w_pool),
    )
    got = swap_cores(other)
    attention = (queries, keys, values, grads, lse, delta, logit)
    rest = (mixed, normed, w_query, w_key, w_value)
    own_first, other_first, sums, _ = pairs_back((meta, lengths), 0, *attention, *rest)
    got, other_first = lax.optimization_barrier((got, other_first))
    pieces = cut_pieces(packet, own, got, own_first, swap_cores(other_first))
    pieces, attention = lax.optimization_barrier((pieces, attention))
    upper_plane = lax.all_to_all(pieces, PLANE, 0, 0)
    own, other, _, packet = pairs_back((meta, lengths), 2, *attention, sums, *rest)
    pieces = cut_pieces(packet, own, swap_cores(other))
    upper_plane, pieces = lax.optimization_barrier((upper_plane, pieces))
    lower_plane = lax.all_to_all(pieces, PLANE, 0, 0)
    got = lax.all_to_all(sum_pieces(meta, upper_plane, lower_plane, heads), "z", 0, 0)
    kept, sent = total_rows(meta, got)
    sequence, mix, cross, gain, bias, grad_heads = join(meta, kept, swap_cores(sent))
    return (sequence, mix, cross, gain.reshape(D), bias.reshape(DI), grad_heads.T)


def solution(mesh):
    fine = Mesh(mesh.devices.reshape(8, 2, 4, 2, 2), ("z", "ylo", "x", "yhi", "core"))
    dp = ("z", "ylo", "x")
    every = dp + CTX
    in_specs = (P(dp, CTX), P(dp), P(dp, CTX, None), P(dp, None), P(dp, None)) + (P(),) * 11
    out_specs = (P(every, None), P(every, None), P(every, None), P(), P(), P())
    return jax.shard_map(
        per_device, mesh=fine, in_specs=in_specs, out_specs=out_specs, check_vma=False
    )
```
